128 devices in a mesh: row: 16 (over y, x), col: 8 (over z, core).
Axes of the slice: x: 4, y: 4, z: 4, core: 2. Of those that a mesh axis runs over, the one named last changes fastest.
Arguments:
- inputs: bfloat16 [1, 256, 256, 512], P(None, 'row', 'col'), may hold values from -30 to 30, as said below
- out_grad: bfloat16 [1, 256, 256, 512], P(None, 'row', 'col'), may hold values from -6 to 6
- w_expand: bfloat16 [512, 2048], replicated, may hold values from -0.25 to 0.25
- dw_kernel: float32 [3, 3, 2048], replicated, may hold values from -2 to 2
- se_reduce: float32 [2048, 128], replicated, may hold values from -0.125 to 0.125
- se_expand: float32 [128, 2048], replicated, may hold values from -0.5 to 0.5
- w_project: bfloat16 [2048, 512], replicated, may hold values from -0.125 to 0.125
- w_qkv: bfloat16 [512, 1536], replicated, may hold values from -0.25 to 0.25
- w_out: bfloat16 [512, 512], replicated, may hold values from -0.25 to 0.25
- pos_table: float32 [16, 225], replicated, may hold values from -4 to 320
Outputs:
- block_out: bfloat16 [1, 256, 256, 512], P(None, 'row', 'col')
- input_gradient: bfloat16 [1, 256, 256, 512], P(None, 'row', 'col')
- expand_grad: float32 [512, 2048], P(('row', 'col'))
- project_grad: float32 [2048, 512], P(('row', 'col'))
- qkv_grad: float32 [512, 1536], P(('row', 'col'))
- out_proj_grad: float32 [512, 512], P(('row', 'col'))
- kernel_grad: float32 [3, 3, 2048], replicated
- se_reduce_grad: float32 [2048, 128], replicated
- se_expand_grad: float32 [128, 2048], replicated
- table_grad: float32 [16, 225], replicated
The draws below stay inside these ranges and needn't reach their ends.
Inputs may be any that keep to these rules, and one draw needn't show every extreme that they name: `inputs`: activations of the block's input.
All inputs are finite; a program needn't handle non-finite values.
Results may differ from the reference program's by a relative error of at most 0.015.
Values may be sent and summed in bfloat16 or wider, within the bound.
A program may use at most 192 MiB of HBM per device.

```python
import math
import jax
import jax.numpy as jnp
from jax import lax

CHANNEL_COUNT = 512
E = 2048
SQUEEZE = 128
HEADS = 16
GRID = 8
IMAGES = 1
TOKEN_ROWS = 256
TOKEN_COLUMNS = 256


def draw_inputs(key, part):
    streams = jax.random.split(key, 4)
    full_shape = (IMAGES, TOKEN_ROWS, TOKEN_COLUMNS, CHANNEL_COUNT)
    base_values = jax.random.truncated_normal(streams[0], -4.0, 4.0, full_shape, jnp.float32)
    reach = 0.5
    row_scale = jnp.exp(jax.random.uniform(streams[1], (IMAGES, TOKEN_ROWS, TOKEN_COLUMNS, 1), jnp.float32, math.log(0.3), math.log(3.0)))
    rough = jax.random.uniform(streams[2], (IMAGES, TOKEN_ROWS, TOKEN_COLUMNS, 1), jnp.float32, 0.5, 1.5)
    downward = jnp.arange(TOKEN_ROWS, dtype=jnp.float32).reshape(1, TOKEN_ROWS, 1, 1) / TOKEN_ROWS
    sideways = jnp.arange(TOKEN_COLUMNS, dtype=jnp.float32).reshape(1, 1, TOKEN_COLUMNS, 1) / TOKEN_COLUMNS
    pattern = jax.random.truncated_normal(streams[3], -3.0, 3.0, (CHANNEL_COUNT,), jnp.float32)
    ramp = reach * (downward + sideways) * rough
    return (row_scale * (base_values + ramp * pattern)).astype(jnp.bfloat16)


def draw_pos_table(key, part):
    span = (2 * GRID - 1) ** 2
    table = jax.random.truncated_normal(key, -4.0, 4.0, (HEADS, span), jnp.float32)
    return table


def levels(key, extent, cuts, least, high):
    factor_of, own = 1.0, jax.random.fold_in(key, 6)
    for position, blocks in cuts:
        steps = jnp.exp(jax.random.uniform(jax.random.fold_in(own, position), (blocks,), jnp.float32, least / len(cuts), high / len(cuts)))
        factor_of = factor_of * jnp.repeat(steps, extent[position] // blocks).reshape([-1 if axis == position else 1 for axis in range(len(extent))])
    return factor_of


def gaussian(key, extent, width, most, cuts=(), kind=jnp.bfloat16):
    entries = jax.random.normal(key, extent, jnp.float32) * width
    if len(cuts) > 0:
        entries = levels(key, extent, cuts, -0.22, 0.18) * entries
    return jnp.clip(entries, min=-most, max=most).astype(kind)


def setup_inputs(seed: int = 0) -> dict:
    key_of = jax.random.split(jax.random.key(seed), 11)
    inputs = draw_inputs(jax.random.fold_in(key_of[10], 71), 0)
    out_grad = gaussian(key_of[1], (IMAGES, TOKEN_ROWS, TOKEN_COLUMNS, CHANNEL_COUNT), 1.0, 6.0, ((1, 16), (2, 8)))
    w_expand = gaussian(key_of[2], (CHANNEL_COUNT, E), CHANNEL_COUNT ** -0.5, 0.25)
    dw_kernel = gaussian(key_of[3], (3, 3, E), 9 ** -0.5, 2.0, (), jnp.float32)
    se_reduce = gaussian(key_of[4], (E, SQUEEZE), E ** -0.5, 0.125, (), jnp.float32)
    se_expand = gaussian(key_of[5], (SQUEEZE, E), SQUEEZE ** -0.5, 0.5, (), jnp.float32)
    w_project = gaussian(key_of[6], (E, CHANNEL_COUNT), E ** -0.5, 0.125)
    w_qkv = gaussian(key_of[7], (CHANNEL_COUNT, 3 * CHANNEL_COUNT), CHANNEL_COUNT ** -0.5, 0.25)
    w_out = gaussian(key_of[8], (CHANNEL_COUNT, CHANNEL_COUNT), CHANNEL_COUNT ** -0.5, 0.25)
    pos_table = draw_pos_table(jax.random.fold_in(key_of[10], 71), 0)
    return dict(inputs=inputs, out_grad=out_grad, w_expand=w_expand, dw_kernel=dw_kernel, se_reduce=se_reduce, se_expand=se_expand, w_project=w_project, w_qkv=w_qkv, w_out=w_out, pos_table=pos_table)


EPSILON = 1e-05
GELU_SCALE = math.sqrt(2.0 / math.pi)
HIGHEST = lax.Precision.HIGHEST

def gelu_slope(values):
    cubic = values * values * values
    bent = jnp.tanh(GELU_SCALE * (values + 0.044715 * cubic))
    result = 0.5 * values * (1.0 + bent)
    slope = 0.5 * (1.0 + bent) + 0.5 * values * (1.0 - bent * bent) * GELU_SCALE * (1.0 + 3.0 * 0.044715 * values * values)
    return (result, slope)

def layer_normalize(values):
    values = values.astype(jnp.float32)
    centred = values - lax.optimization_barrier(jnp.mean(values, axis=-1, keepdims=True))
    inverse = lax.rsqrt(lax.optimization_barrier(jnp.mean(centred * centred, axis=-1, keepdims=True)) + EPSILON)
    return (centred * inverse, inverse)

def norm_backward_pass(normal_values, inverse, grads):
    grads = grads.astype(jnp.float32)
    return inverse * (grads - lax.optimization_barrier(jnp.mean(grads, axis=-1, keepdims=True)) - normal_values * lax.optimization_barrier(jnp.mean(grads * normal_values, axis=-1, keepdims=True)))

def offset_table(side):
    places = jnp.arange(side * side, dtype=jnp.int32)
    place_row = places // side
    place_col = places % side
    offset_index = (place_row[:, None] - place_row[None, :] + side - 1) * (2 * side - 1) + place_col[:, None] - place_col[None, :] + side - 1
    table_slots = jnp.arange((2 * side - 1) ** 2, dtype=jnp.int32)
    return (table_slots[:, None] == offset_index.reshape(1, -1)).astype(jnp.float32)

def depthwise(padded, kernel):
    out_rows = padded.shape[1] - 2
    out_cols = padded.shape[2] - 2
    summed = jnp.zeros((padded.shape[0], out_rows, out_cols, padded.shape[3]), jnp.float32)
    for shift_row in range(3):
        for shift_col in range(3):
            window = padded[:, shift_row:shift_row + out_rows, shift_col:shift_col + out_cols, :].astype(jnp.float32)
            summed = summed + window * kernel[shift_row, shift_col]
    return summed

def kernel_terms(padded, grads):
    out_rows = grads.shape[1]
    out_cols = grads.shape[2]
    grads_wide = grads.astype(jnp.float32)
    collected = []
    for shift_row in range(3):
        for shift_col in range(3):
            window = padded[:, shift_row:shift_row + out_rows, shift_col:shift_col + out_cols, :].astype(jnp.float32)
            collected.append(lax.optimization_barrier(jnp.sum(window * grads_wide, axis=(0, 1, 2))))
    return jnp.stack(collected).reshape(3, 3, -1)

def grid_groups(tiles):
    image_count, height, breadth, feature_count = tiles.shape
    shaped = tiles.reshape(image_count, GRID, height // GRID, GRID, breadth // GRID, feature_count)
    shaped = shaped.transpose(0, 2, 4, 1, 3, 5)
    return shaped.reshape(-1, GRID * GRID, feature_count)

def grid_tiles(groups, image_count, height, breadth):
    feature_count = groups.shape[-1]
    shaped = groups.reshape(image_count, height // GRID, breadth // GRID, GRID, GRID, feature_count)
    shaped = shaped.transpose(0, 3, 1, 4, 2, 5)
    return shaped.reshape(image_count, height, breadth, feature_count)

def split_heads(grouped):
    group_count, places, feature_count = grouped.shape
    return grouped.reshape(group_count, places, HEADS, feature_count // HEADS)

def attend_forward(queries, keys_in, values_in, bias):
    factor = queries.shape[-1] ** (-0.5)
    scores = jnp.einsum('gphd,gqhd->ghpq', queries.astype(jnp.float32), keys_in.astype(jnp.float32)) * factor + bias
    scores = scores - lax.optimization_barrier(jnp.max(scores, axis=-1, keepdims=True))
    weights = jnp.exp(scores)
    weights = weights / lax.optimization_barrier(jnp.sum(weights, axis=-1, keepdims=True))
    weights_b = weights.astype(jnp.bfloat16)
    context = jnp.einsum('ghpq,gqhd->gphd', weights_b.astype(jnp.float32), values_in.astype(jnp.float32)).astype(jnp.bfloat16)
    return (context, weights, weights_b)

def attend_backward(queries, keys_in, values_in, weights, weights_b, context_grad):
    factor = queries.shape[-1] ** (-0.5)
    grad_wide = context_grad.astype(jnp.float32)
    weights_grad = jnp.einsum('gphd,gqhd->ghpq', grad_wide, values_in.astype(jnp.float32))
    values_grad = jnp.einsum('ghpq,gphd->gqhd', weights_b.astype(jnp.float32), grad_wide).astype(jnp.bfloat16)
    scores_grad = weights * (weights_grad - lax.optimization_barrier(jnp.sum(weights * weights_grad, axis=-1, keepdims=True)))
    scores_b = (scores_grad * factor).astype(jnp.bfloat16).astype(jnp.float32)
    queries_grad = jnp.einsum('ghpq,gqhd->gphd', scores_b, keys_in.astype(jnp.float32)).astype(jnp.bfloat16)
    keys_grad = jnp.einsum('ghpq,gphd->gqhd', scores_b, queries.astype(jnp.float32)).astype(jnp.bfloat16)
    return (queries_grad, keys_grad, values_grad, lax.optimization_barrier(jnp.sum(scores_grad, axis=0)))

def reference(inputs, out_grad, w_expand, dw_kernel, se_reduce, se_expand, w_project, w_qkv, w_out, pos_table):
    onehot = offset_table(GRID)
    bias = jnp.dot(pos_table, onehot, precision=HIGHEST).reshape(HEADS, GRID * GRID, GRID * GRID)
    contract = (((0,), (0,)), ((), ()))
    backward = (((1,), (1,)), ((), ()))
    flattened_count = TOKEN_ROWS * TOKEN_COLUMNS
    places = GRID * GRID

    def one_image(carry, pieces):
        image_tokens, cotangent = pieces
        first_standardized, inverse_deviation_first = layer_normalize(image_tokens)
        first_normed_input = first_standardized.astype(jnp.bfloat16).reshape(flattened_count, CHANNEL_COUNT)
        pre_expand = jnp.dot(first_normed_input, w_expand, preferred_element_type=jnp.float32).reshape(1, TOKEN_ROWS, TOKEN_COLUMNS, E)
        expanded_f, slope_expand = gelu_slope(pre_expand)
        expanded = expanded_f.astype(jnp.bfloat16)
        padded = jnp.pad(expanded, ((0, 0), (1, 1), (1, 1), (0, 0)))
        pre_mix = depthwise(padded, dw_kernel)
        mixed, slope_mix = gelu_slope(pre_mix)
        pooled = lax.optimization_barrier(jnp.sum(mixed, axis=(1, 2))) / (TOKEN_ROWS * TOKEN_COLUMNS)
        squeeze_pre = jnp.dot(pooled, se_reduce, precision=HIGHEST)
        squeeze_sig = jax.nn.sigmoid(squeeze_pre)
        squeezed = squeeze_pre * squeeze_sig
        gate = jax.nn.sigmoid(jnp.dot(squeezed, se_expand, precision=HIGHEST))
        scaled = (mixed * gate[:, None, None, :]).astype(jnp.bfloat16).reshape(flattened_count, E)
        middle_activation = image_tokens.astype(jnp.float32).reshape(flattened_count, CHANNEL_COUNT) + jnp.dot(scaled, w_project, preferred_element_type=jnp.float32)
        second_standardized, inverse_deviation_second = layer_normalize(middle_activation)
        second_normed_input = second_standardized.astype(jnp.bfloat16)
        qkv = jnp.dot(second_normed_input, w_qkv, preferred_element_type=jnp.float32).astype(jnp.bfloat16)
        grid_qkv = grid_groups(qkv.reshape(1, TOKEN_ROWS, TOKEN_COLUMNS, 3 * CHANNEL_COUNT))
        queries = split_heads(grid_qkv[:, :, :CHANNEL_COUNT])
        keys_in = split_heads(grid_qkv[:, :, CHANNEL_COUNT:2 * CHANNEL_COUNT])
        values_in = split_heads(grid_qkv[:, :, 2 * CHANNEL_COUNT:])
        context, weights, weights_b = attend_forward(queries, keys_in, values_in, bias)
        context_flat = grid_tiles(context.reshape(-1, places, CHANNEL_COUNT), 1, TOKEN_ROWS, TOKEN_COLUMNS).reshape(flattened_count, CHANNEL_COUNT)
        block_out = (middle_activation + jnp.dot(context_flat, w_out, preferred_element_type=jnp.float32)).astype(jnp.bfloat16)
        flattened_cotangent = cotangent.reshape(flattened_count, CHANNEL_COUNT)
        context_grad = lax.dot_general(flattened_cotangent, w_out, backward, preferred_element_type=jnp.float32).astype(jnp.bfloat16)
        grid_cgrad = split_heads(grid_groups(context_grad.reshape(1, TOKEN_ROWS, TOKEN_COLUMNS, CHANNEL_COUNT)))
        queries_grad, keys_grad, values_grad, scores_sum = attend_backward(queries, keys_in, values_in, weights, weights_b, grid_cgrad)
        group_count = queries_grad.shape[0]
        grid_proj = jnp.concatenate([queries_grad.reshape(group_count, places, CHANNEL_COUNT), keys_grad.reshape(group_count, places, CHANNEL_COUNT), values_grad.reshape(group_count, places, CHANNEL_COUNT)], axis=-1)
        projections_grad = grid_tiles(grid_proj, 1, TOKEN_ROWS, TOKEN_COLUMNS).reshape(flattened_count, 3 * CHANNEL_COUNT)
        second_normed_gradient = lax.dot_general(projections_grad, w_qkv, backward, preferred_element_type=jnp.float32).astype(jnp.bfloat16)
        middle_gradient = flattened_cotangent.astype(jnp.float32) + norm_backward_pass(second_standardized, inverse_deviation_second, second_normed_gradient)
        middle_b = middle_gradient.astype(jnp.bfloat16)
        scaled_grad = lax.dot_general(middle_b, w_project, backward, preferred_element_type=jnp.float32).reshape(1, TOKEN_ROWS, TOKEN_COLUMNS, E)
        gate_grad = lax.optimization_barrier(jnp.sum(scaled_grad * mixed, axis=(1, 2)))
        excite_grad = gate_grad * gate * (1.0 - gate)
        squeezed_grad = lax.dot_general(excite_grad, se_expand, backward, precision=HIGHEST)
        squeeze_grad = squeezed_grad * squeeze_sig * (1.0 + squeeze_pre * (1.0 - squeeze_sig))
        pooled_grad = lax.dot_general(squeeze_grad, se_reduce, backward, precision=HIGHEST)
        premix_grad = ((scaled_grad * gate[:, None, None, :] + pooled_grad[:, None, None, :] / (TOKEN_ROWS * TOKEN_COLUMNS)) * slope_mix).astype(jnp.bfloat16)
        grad_padded = jnp.pad(premix_grad, ((0, 0), (1, 1), (1, 1), (0, 0)))
        expanded_grad = depthwise(grad_padded, dw_kernel[::-1, ::-1])
        preexp_grad = (expanded_grad * slope_expand).astype(jnp.bfloat16).reshape(flattened_count, E)
        first_normed_gradient = lax.dot_general(preexp_grad, w_expand, backward, preferred_element_type=jnp.float32).reshape(1, TOKEN_ROWS, TOKEN_COLUMNS, CHANNEL_COUNT)
        input_gradient = (middle_gradient.reshape(1, TOKEN_ROWS, TOKEN_COLUMNS, CHANNEL_COUNT) + norm_backward_pass(first_standardized, inverse_deviation_first, first_normed_gradient)).astype(jnp.bfloat16)
        updated = (carry[0] + lax.dot_general(first_normed_input, preexp_grad, contract, preferred_element_type=jnp.float32), carry[1] + lax.dot_general(scaled, middle_b, contract, preferred_element_type=jnp.float32), carry[2] + lax.dot_general(second_normed_input, projections_grad, contract, preferred_element_type=jnp.float32), carry[3] + lax.dot_general(context_flat, flattened_cotangent, contract, preferred_element_type=jnp.float32), carry[4] + kernel_terms(padded, premix_grad), carry[5] + lax.dot_general(pooled, squeeze_grad, contract, precision=HIGHEST), carry[6] + lax.dot_general(squeezed, excite_grad, contract, precision=HIGHEST), carry[7] + lax.dot_general(scores_sum.reshape(HEADS, places * places), onehot, backward, precision=HIGHEST))
        return (updated, (block_out.reshape(1, TOKEN_ROWS, TOKEN_COLUMNS, CHANNEL_COUNT), input_gradient))
    start = (jnp.zeros((CHANNEL_COUNT, E), jnp.float32), jnp.zeros((E, CHANNEL_COUNT), jnp.float32), jnp.zeros((CHANNEL_COUNT, 3 * CHANNEL_COUNT), jnp.float32), jnp.zeros((CHANNEL_COUNT, CHANNEL_COUNT), jnp.float32), jnp.zeros((3, 3, E), jnp.float32), jnp.zeros((E, SQUEEZE), jnp.float32), jnp.zeros((SQUEEZE, E), jnp.float32), jnp.zeros((HEADS, (2 * GRID - 1) ** 2), jnp.float32))
    totals, (outs_all, grads_all) = lax.scan(one_image, start, (inputs[:, None], out_grad[:, None]))
    factor = (IMAGES * TOKEN_ROWS * TOKEN_COLUMNS) ** (-0.5)
    return (outs_all.reshape(IMAGES, TOKEN_ROWS, TOKEN_COLUMNS, CHANNEL_COUNT), grads_all.reshape(IMAGES, TOKEN_ROWS, TOKEN_COLUMNS, CHANNEL_COUNT), totals[0] * factor, totals[1] * factor, totals[2] * factor, totals[3] * factor, totals[4] * factor, totals[5] * factor, totals[6] * factor, totals[7] * factor)
```

```python
import math

import jax
import jax.numpy as jnp
from jax import lax
from jax.sharding import PartitionSpec as P

GRID = 8


EPSILON = 1e-05
GELU_SCALE = math.sqrt(2.0 / math.pi)
HIGHEST = lax.Precision.HIGHEST
CONTRACT = (((0,), (0,)), ((), ()))
BACKWARD = (((1,), (1,)), ((), ()))


def padded_2(cells, sides, width):
    for axis, dim in sides:
        count = lax.axis_size(axis)
        ends = count - 1
        head = lax.slice_in_dim(cells, 0, width, axis=dim)
        tail = lax.slice_in_dim(cells, cells.shape[dim] - width, cells.shape[dim], axis=dim)
        cells = jnp.concatenate(
            [
                lax.ppermute(tail, axis, [(i, (i + 1) % count) for i in range(ends)]),
                cells,
                lax.ppermute(head, axis, [((i + 1) % count, i) for i in range(ends)]),
            ],
            axis=dim,
        )
    return cells


def gelu_slope(values):
    cubic = values * values * values
    bent = jnp.tanh(GELU_SCALE * (values + 0.044715 * cubic))
    result = 0.5 * values * (1.0 + bent)
    slope = 0.5 * (1.0 + bent) + 0.5 * values * (1.0 - bent * bent) * GELU_SCALE * (
        1.0 + 3.0 * 0.044715 * values * values
    )
    return (result, slope)


def layer_normalize(values):
    values = values.astype(jnp.float32)
    centred = values - jnp.mean(values, axis=-1, keepdims=True)
    inverse = lax.rsqrt(jnp.mean(centred * centred, axis=-1, keepdims=True) + EPSILON)
    return (centred * inverse, inverse)


def norm_backward_pass(normal_values, inverse, grads):
    grads = grads.astype(jnp.float32)
    return inverse * (
        grads
        - jnp.mean(grads, axis=-1, keepdims=True)
        - normal_values * jnp.mean(grads * normal_values, axis=-1, keepdims=True)
    )


def offset_table(side):
    places = jnp.arange(side * side, dtype=jnp.int32)
    place_row = places // side
    place_col = places % side
    offset_index = (
        (place_row[:, None] - place_row[None, :] + side - 1) * (2 * side - 1)
        + place_col[:, None]
        - place_col[None, :]
        + side
        - 1
    )
    table_slots = jnp.arange((2 * side - 1) ** 2, dtype=jnp.int32)
    return (table_slots[:, None] == offset_index.reshape(1, -1)).astype(jnp.float32)


def depthwise(padded, kernel):
    out_rows = padded.shape[1] - 2
    out_cols = padded.shape[2] - 2
    summed = jnp.zeros((padded.shape[0], out_rows, out_cols, padded.shape[3]), jnp.float32)
    for shift_row in range(3):
        for shift_col in range(3):
            window = padded[
                :, shift_row : shift_row + out_rows, shift_col : shift_col + out_cols, :
            ].astype(jnp.float32)
            summed = summed + window * kernel[shift_row, shift_col]
    return summed


def kernel_terms(padded, grads):
    out_rows = grads.shape[1]
    out_cols = grads.shape[2]
    grads_wide = grads.astype(jnp.float32)
    collected = []
    for shift_row in range(3):
        for shift_col in range(3):
            window = padded[
                :, shift_row : shift_row + out_rows, shift_col : shift_col + out_cols, :
            ].astype(jnp.float32)
            collected.append(jnp.sum(window * grads_wide, axis=(0, 1, 2)))
    return jnp.stack(collected).reshape(3, 3, -1)


def block_counts():
    return (max(1, GRID // lax.axis_size("row")), max(1, GRID // lax.axis_size("col")))


def to_grid(tiles):
    image_count, tile_rows, tile_cols, feature_count = tiles.shape
    row_blocks, col_blocks = block_counts()
    shaped = tiles.reshape(
        image_count,
        row_blocks,
        tile_rows // row_blocks,
        col_blocks,
        tile_cols // col_blocks,
        feature_count,
    )
    moved = lax.all_to_all(
        lax.all_to_all(shaped, "row", split_axis=2, concat_axis=1, tiled=True),
        "col",
        split_axis=4,
        concat_axis=3,
        tiled=True,
    )
    moved = moved.reshape(
        image_count, GRID, tile_rows // GRID, GRID, tile_cols // GRID, feature_count
    )
    moved = moved.transpose(0, 2, 4, 1, 3, 5)
    return moved.reshape(
        image_count * (tile_rows // GRID) * (tile_cols // GRID), GRID * GRID, feature_count
    )


def to_tiles(grouped, image_count, tile_rows, tile_cols):
    feature_count = grouped.shape[-1]
    row_blocks, col_blocks = block_counts()
    row_parts = row_blocks * lax.axis_size("row")
    col_parts = col_blocks * lax.axis_size("col")
    shaped = grouped.reshape(
        image_count, tile_rows // GRID, tile_cols // GRID, GRID, GRID, feature_count
    )
    shaped = shaped.transpose(0, 3, 1, 4, 2, 5)
    shaped = shaped.reshape(
        image_count,
        row_parts,
        tile_rows // row_parts,
        col_parts,
        tile_cols // col_parts,
        feature_count,
    )
    moved = lax.all_to_all(
        lax.all_to_all(shaped, "row", split_axis=1, concat_axis=2, tiled=True),
        "col",
        split_axis=3,
        concat_axis=4,
        tiled=True,
    )
    return moved.reshape(image_count, tile_rows, tile_cols, feature_count)


AXES = ("row", "col")


def exchange_all(parts):
    return lax.all_to_all(parts, AXES, 0, 0, tiled=True)


def gather_sum(values, axis):
    count = lax.axis_size(axis)
    spread = jnp.broadcast_to(values, (count,) + values.shape)
    return jnp.sum(lax.all_to_all(spread, axis, 0, 0, tiled=True), axis=0)


def small_sum(values):
    return gather_sum(gather_sum(values, "row"), "col")


def split_sum(values):
    rows = lax.axis_size("row")
    parts = values.reshape(rows, -1, 128)
    own = jnp.sum(lax.all_to_all(parts, "row", 0, 0, tiled=True), axis=0)
    own = gather_sum(own.reshape(-1, 128), "col")
    spread = jnp.broadcast_to(own, (rows,) + own.shape)
    return lax.all_to_all(spread, "row", 0, 0, tiled=True)


def weight_grad(left_side, right_side):
    count = lax.axis_size("row") * lax.axis_size("col")
    partial = lax.dot_general(left_side, right_side, CONTRACT, preferred_element_type=jnp.float32)
    height, width = partial.shape
    parts = partial.astype(jnp.bfloat16).reshape(count, height // count, width)
    return jnp.sum(exchange_all(parts).astype(jnp.float32), axis=0)


def split_heads(grouped, heads):
    group_count, places, feature_count = grouped.shape
    return grouped.reshape(group_count, places, heads, feature_count // heads)


def attend_forward(queries, keys_in, values_in, bias):
    factor = queries.shape[-1] ** (-0.5)
    scores = (
        jnp.einsum("gphd,gqhd->ghpq", queries, keys_in, preferred_element_type=jnp.float32) * factor
        + bias
    )
    scores = scores - jnp.max(scores, axis=-1, keepdims=True)
    weights = jnp.exp(scores)
    weights = weights / jnp.sum(weights, axis=-1, keepdims=True)
    weights_b = weights.astype(jnp.bfloat16)
    context = jnp.einsum(
        "ghpq,gqhd->gphd", weights_b, values_in, preferred_element_type=jnp.float32
    ).astype(jnp.bfloat16)
    return (context, weights, weights_b)


def attend_backward(queries, keys_in, values_in, weights, weights_b, context_grad):
    factor = queries.shape[-1] ** (-0.5)
    weights_grad = jnp.einsum(
        "gphd,gqhd->ghpq", context_grad, values_in, preferred_element_type=jnp.float32
    )
    values_grad = jnp.einsum(
        "ghpq,gphd->gqhd", weights_b, context_grad, preferred_element_type=jnp.float32
    ).astype(jnp.bfloat16)
    scores_grad = weights * (weights_grad - jnp.sum(weights * weights_grad, axis=-1, keepdims=True))
    scores_b = (scores_grad * factor).astype(jnp.bfloat16)
    queries_grad = jnp.einsum(
        "ghpq,gqhd->gphd", scores_b, keys_in, preferred_element_type=jnp.float32
    ).astype(jnp.bfloat16)
    keys_grad = jnp.einsum(
        "ghpq,gphd->gqhd", scores_b, queries, preferred_element_type=jnp.float32
    ).astype(jnp.bfloat16)
    return (queries_grad, keys_grad, values_grad, jnp.sum(scores_grad, axis=0))


def on_device(
    inputs, out_grad, w_expand, dw_kernel, se_reduce, se_expand, w_project, w_qkv, w_out, pos_table
):
    images, tile_rows, tile_cols, channels = inputs.shape
    hidden_units = w_expand.shape[1]
    heads = pos_table.shape[0]
    places = GRID * GRID
    full_rows = tile_rows * lax.axis_size("row")
    full_cols = tile_cols * lax.axis_size("col")
    cells = full_rows * full_cols
    factor = (images * cells) ** (-0.5)
    tokens = images * tile_rows * tile_cols
    onehot = offset_table(GRID)
    bias = jnp.dot(pos_table, onehot, precision=HIGHEST).reshape(heads, places, places)
    first_standardized, inverse_deviation_first = layer_normalize(inputs)
    first_normed_input = first_standardized.astype(jnp.bfloat16)
    pre_expand = jnp.dot(
        first_normed_input.reshape(tokens, channels), w_expand, preferred_element_type=jnp.float32
    )
    expanded_f, slope_expand = gelu_slope(
        pre_expand.reshape(images, tile_rows, tile_cols, hidden_units)
    )
    padded = padded_2(expanded_f.astype(jnp.bfloat16), (("row", 1), ("col", 2)), 1)
    pre_mix = depthwise(padded, dw_kernel)
    mixed, slope_mix = gelu_slope(pre_mix)
    pooled = small_sum(jnp.sum(mixed, axis=(1, 2)).reshape(-1, 128)).reshape(images, -1) / cells
    squeeze_pre = jnp.dot(pooled, se_reduce, precision=HIGHEST)
    squeeze_sig = jax.nn.sigmoid(squeeze_pre)
    squeezed = squeeze_pre * squeeze_sig
    gate = jax.nn.sigmoid(jnp.dot(squeezed, se_expand, precision=HIGHEST))
    scaled = (mixed * gate[:, None, None, :]).astype(jnp.bfloat16).reshape(tokens, hidden_units)
    middle_activation = inputs.astype(jnp.float32).reshape(tokens, channels) + jnp.dot(
        scaled, w_project, preferred_element_type=jnp.float32
    )
    second_standardized, inverse_deviation_second = layer_normalize(middle_activation)
    second_normed_input = second_standardized.astype(jnp.bfloat16)
    grid_normed = to_grid(second_normed_input.reshape(images, tile_rows, tile_cols, channels))
    grid_normed_flat = grid_normed.reshape(tokens, channels)
    grid_qkv = (
        jnp.dot(grid_normed_flat, w_qkv, preferred_element_type=jnp.float32)
        .astype(jnp.bfloat16)
        .reshape(-1, places, 3 * channels)
    )
    group_count = grid_qkv.shape[0]
    queries = split_heads(grid_qkv[:, :, :channels], heads)
    keys_in = split_heads(grid_qkv[:, :, channels : 2 * channels], heads)
    values_in = split_heads(grid_qkv[:, :, 2 * channels :], heads)
    context, weights, weights_b = attend_forward(queries, keys_in, values_in, bias)
    context_flat = to_tiles(
        context.reshape(group_count, places, channels), images, tile_rows, tile_cols
    ).reshape(tokens, channels)
    block_out = (
        middle_activation + jnp.dot(context_flat, w_out, preferred_element_type=jnp.float32)
    ).astype(jnp.bfloat16)
    flattened_cotangent = out_grad.reshape(tokens, channels)
    out_proj_grad = weight_grad(context_flat, flattened_cotangent) * factor
    context_grad = lax.dot_general(
        flattened_cotangent, w_out, BACKWARD, preferred_element_type=jnp.float32
    ).astype(jnp.bfloat16)
    grid_cgrad = split_heads(
        to_grid(context_grad.reshape(images, tile_rows, tile_cols, channels)), heads
    )
    queries_grad, keys_grad, values_grad, scores_sum = attend_backward(
        queries, keys_in, values_in, weights, weights_b, grid_cgrad
    )
    grid_proj = jnp.concatenate(
        [
            queries_grad.reshape(group_count, places, channels),
            keys_grad.reshape(group_count, places, channels),
            values_grad.reshape(group_count, places, channels),
        ],
        axis=-1,
    )
    table_part = lax.dot_general(
        scores_sum.reshape(heads, places * places), onehot, BACKWARD, precision=HIGHEST
    )
    projections_grad = grid_proj.reshape(tokens, 3 * channels)
    qkv_grad = weight_grad(grid_normed_flat, projections_grad) * factor
    grid_normed_gradient = lax.dot_general(
        projections_grad, w_qkv, BACKWARD, preferred_element_type=jnp.float32
    ).astype(jnp.bfloat16)
    second_normed_gradient = to_tiles(
        grid_normed_gradient.reshape(group_count, places, channels), images, tile_rows, tile_cols
    ).reshape(tokens, channels)
    middle_gradient = flattened_cotangent.astype(jnp.float32) + norm_backward_pass(
        second_standardized, inverse_deviation_second, second_normed_gradient
    )
    middle_b = middle_gradient.astype(jnp.bfloat16)
    project_grad = weight_grad(scaled, middle_b) * factor
    scaled_grad = lax.dot_general(
        middle_b, w_project, BACKWARD, preferred_element_type=jnp.float32
    ).reshape(images, tile_rows, tile_cols, hidden_units)
    gate_grad = small_sum(jnp.sum(scaled_grad * mixed, axis=(1, 2)).reshape(-1, 128)).reshape(
        images, -1
    )
    excite_grad = gate_grad * gate * (1.0 - gate)
    squeezed_grad = lax.dot_general(excite_grad, se_expand, BACKWARD, precision=HIGHEST)
    squeeze_grad = squeezed_grad * squeeze_sig * (1.0 + squeeze_pre * (1.0 - squeeze_sig))
    pooled_grad = lax.dot_general(squeeze_grad, se_reduce, BACKWARD, precision=HIGHEST)
    se_reduce_grad = lax.dot_general(pooled, squeeze_grad, CONTRACT, precision=HIGHEST) * factor
    se_expand_grad = lax.dot_general(squeezed, excite_grad, CONTRACT, precision=HIGHEST) * factor
    premix_grad = (
        (scaled_grad * gate[:, None, None, :] + pooled_grad[:, None, None, :] / cells) * slope_mix
    ).astype(jnp.bfloat16)
    grad_padded = padded_2(premix_grad, (("row", 1), ("col", 2)), 1)
    kernel_part = kernel_terms(padded, premix_grad)
    expanded_grad = depthwise(grad_padded, dw_kernel[::-1, ::-1])
    preexp_grad = (expanded_grad * slope_expand).astype(jnp.bfloat16).reshape(tokens, hidden_units)
    expand_grad = weight_grad(first_normed_input.reshape(tokens, channels), preexp_grad) * factor
    first_normed_gradient = lax.dot_general(
        preexp_grad, w_expand, BACKWARD, preferred_element_type=jnp.float32
    ).reshape(images, tile_rows, tile_cols, channels)
    input_gradient = (
        middle_gradient.reshape(images, tile_rows, tile_cols, channels)
        + norm_backward_pass(first_standardized, inverse_deviation_first, first_normed_gradient)
    ).astype(jnp.bfloat16)
    small = jnp.concatenate([kernel_part.reshape(-1), table_part.reshape(-1)])
    unit = lax.axis_size("row") * 1024
    room = -small.shape[0] % unit
    small = split_sum(jnp.pad(small, (0, room))).reshape(-1)
    kernel_size = kernel_part.size
    kernel_sum = small[:kernel_size].reshape(kernel_part.shape)
    table_sum = small[kernel_size : kernel_size + table_part.size].reshape(table_part.shape)
    return (
        block_out.reshape(images, tile_rows, tile_cols, channels),
        input_gradient,
        expand_grad,
        project_grad,
        qkv_grad,
        out_proj_grad,
        kernel_sum * factor,
        se_reduce_grad,
        se_expand_grad,
        table_sum * factor,
    )


def solution(mesh):
    placed = (
        P(None, "row", "col", None),
        P(None, "row", "col", None),
        P(),
        P(),
        P(),
        P(),
        P(),
        P(),
        P(),
        P(),
    )
    return jax.shard_map(
        on_device,
        mesh=mesh,
        in_specs=placed,
        out_specs=(
            P(None, "row", "col", None),
            P(None, "row", "col", None),
            P(("row", "col"), None),
            P(("row", "col"), None),
            P(("row", "col"), None),
            P(("row", "col"), None),
            P(),
            P(),
            P(),
            P(),
        ),
        check_vma=False,
    )
```

```python
import functools
import math

import jax
import jax.numpy as jnp
from jax import lax
from jax.experimental import pallas as pl
from jax.experimental.pallas import tpu as pltpu
from jax.sharding import PartitionSpec as P

GRID = 8


EPSILON = 1e-05
GELU_SCALE = math.sqrt(2.0 / math.pi)
HIGHEST = lax.Precision.HIGHEST
MESH = pl.DeviceIdType.MESH
CONTRACT = (((0,), (0,)), ((), ()))
BACKWARD = (((1,), (1,)), ((), ()))


def padded_2(cells, sides, width):
    for axis, dim in sides:
        count = lax.axis_size(axis)
        ends = count - 1
        head = lax.slice_in_dim(cells, 0, width, axis=dim)
        tail = lax.slice_in_dim(cells, cells.shape[dim] - width, cells.shape[dim], axis=dim)
        cells = jnp.concatenate(
            [
                lax.ppermute(tail, axis, [(i, (i + 1) % count) for i in range(ends)]),
                cells,
                lax.ppermute(head, axis, [((i + 1) % count, i) for i in range(ends)]),
            ],
            axis=dim,
        )
    return cells


def gelu_slope(values):
    cubic = values * values * values
    bent = jnp.tanh(GELU_SCALE * (values + 0.044715 * cubic))
    result = 0.5 * values * (1.0 + bent)
    slope = 0.5 * (1.0 + bent) + 0.5 * values * (1.0 - bent * bent) * GELU_SCALE * (
        1.0 + 3.0 * 0.044715 * values * values
    )
    return (result, slope)


def layer_normalize(values):
    values = values.astype(jnp.float32)
    centred = values - jnp.mean(values, axis=-1, keepdims=True)
    inverse = lax.rsqrt(jnp.mean(centred * centred, axis=-1, keepdims=True) + EPSILON)
    return (centred * inverse, inverse)


def norm_backward_pass(normal_values, inverse, grads):
    grads = grads.astype(jnp.float32)
    return inverse * (
        grads
        - jnp.mean(grads, axis=-1, keepdims=True)
        - normal_values * jnp.mean(grads * normal_values, axis=-1, keepdims=True)
    )


def offset_table(side):
    places = jnp.arange(side * side, dtype=jnp.int32)
    place_row = places // side
    place_col = places % side
    offset_index = (
        (place_row[None, :] - place_row[:, None] + side - 1) * (2 * side - 1)
        + place_col[None, :]
        - place_col[:, None]
        + side
        - 1
    )
    table_slots = jnp.arange((2 * side - 1) ** 2, dtype=jnp.int32)
    return (table_slots[:, None] == offset_index.reshape(1, -1)).astype(jnp.float32)


def depthwise(padded, kernel):
    out_rows = padded.shape[1] - 2
    out_cols = padded.shape[2] - 2
    summed = jnp.zeros((padded.shape[0], out_rows, out_cols, padded.shape[3]), jnp.float32)
    for shift_row in range(3):
        for shift_col in range(3):
            window = padded[
                :, shift_row : shift_row + out_rows, shift_col : shift_col + out_cols, :
            ].astype(jnp.float32)
            summed = summed + window * kernel[shift_row, shift_col]
    return summed


def kernel_terms(padded, grads):
    out_rows = grads.shape[1]
    out_cols = grads.shape[2]
    grads_wide = grads.astype(jnp.float32)
    collected = []
    for shift_row in range(3):
        for shift_col in range(3):
            window = padded[
                :, shift_row : shift_row + out_rows, shift_col : shift_col + out_cols, :
            ].astype(jnp.float32)
            collected.append(jnp.sum(window * grads_wide, axis=(0, 1, 2)))
    return jnp.stack(collected).reshape(3, 3, -1)


AXES = ("row", "col")


def exchange_all(parts):
    return lax.all_to_all(parts, AXES, 0, 0, tiled=True)


def gather_sum(values, axis):
    count = lax.axis_size(axis)
    spread = jnp.broadcast_to(values, (count,) + values.shape)
    return jnp.sum(lax.all_to_all(spread, axis, 0, 0, tiled=True), axis=0)


def small_sum_kernel(rows, cols, x_ref, o_ref, row_buf, sum_buf, col_buf, sems):
    row = lax.axis_index("row")
    col = lax.axis_index("col")
    barrier = pltpu.get_barrier_semaphore()

    def row_peer(k):
        return lax.rem(row + k, rows)

    def col_peer(k):
        return lax.rem(col + k, cols)

    @pl.loop(1, rows)
    def _(k):
        pl.semaphore_signal(barrier, inc=1, device_id=(row_peer(k), col), device_id_type=MESH)

    @pl.loop(1, cols)
    def _(k):
        pl.semaphore_signal(barrier, inc=1, device_id=(row, col_peer(k)), device_id_type=MESH)

    row_buf[row] = x_ref[...]
    pl.semaphore_wait(barrier, rows + cols - 2)

    @pl.loop(1, rows)
    def _(k):
        pltpu.make_async_remote_copy(
            src_ref=x_ref,
            dst_ref=row_buf.at[row],
            send_sem=sems.at[0],
            recv_sem=sems.at[1],
            device_id=(row_peer(k), col),
            device_id_type=MESH,
        ).start()

    arrived = row_buf.at[pl.ds(0, rows - 1)]
    pltpu.make_async_copy(arrived, arrived, sems.at[1]).wait()
    total = row_buf[0]
    for k in range(1, rows):
        total = total + row_buf[k]
    sum_buf[...] = total
    col_buf[col] = total

    @pl.loop(1, cols)
    def _(k):
        pltpu.make_async_remote_copy(
            src_ref=sum_buf,
            dst_ref=col_buf.at[col],
            send_sem=sems.at[2],
            recv_sem=sems.at[3],
            device_id=(row, col_peer(k)),
            device_id_type=MESH,
        ).start()

    other = col_buf.at[pl.ds(0, cols - 1)]
    pltpu.make_async_copy(other, other, sems.at[3]).wait()
    total = col_buf[0]
    for k in range(1, cols):
        total = total + col_buf[k]
    o_ref[...] = total
    pltpu.make_async_copy(arrived, arrived, sems.at[0]).wait()
    pltpu.make_async_copy(other, other, sems.at[2]).wait()


def small_sum(values, number):
    rows = lax.axis_size("row")
    cols = lax.axis_size("col")
    shape = values.shape
    return pl.pallas_call(
        functools.partial(small_sum_kernel, rows, cols),
        out_shape=jax.ShapeDtypeStruct(shape, jnp.float32),
        in_specs=[pl.BlockSpec(memory_space=pltpu.VMEM)],
        out_specs=pl.BlockSpec(memory_space=pltpu.VMEM),
        scratch_shapes=[
            pltpu.VMEM((rows,) + shape, jnp.float32),
            pltpu.VMEM(shape, jnp.float32),
            pltpu.VMEM((cols,) + shape, jnp.float32),
            pltpu.SemaphoreType.DMA((4,)),
        ],
        compiler_params=pltpu.CompilerParams(collective_id=number, has_side_effects=True),
    )(values)


def swap_kernel(parity, side, cols, x_ref, o_ref, sems):
    row = lax.axis_index("row")
    col = lax.axis_index("col")
    kind = lax.rem(row, parity)
    count = side * cols
    me = (row // parity) * cols + col
    barrier = pltpu.get_barrier_semaphore()

    def place(k):
        peer = lax.rem(me + k, count)
        return peer, ((peer // cols) * parity + kind, lax.rem(peer, cols))

    @pl.loop(1, count)
    def _(k):
        pl.semaphore_signal(barrier, inc=1, device_id=place(k)[1], device_id_type=MESH)

    own = pltpu.make_async_copy(x_ref.at[me], o_ref.at[me], sems.at[2])
    own.start()
    pl.semaphore_wait(barrier, count - 1)

    @pl.loop(1, count)
    def _(k):
        peer, device = place(k)
        pltpu.make_async_remote_copy(
            src_ref=x_ref.at[peer],
            dst_ref=o_ref.at[me],
            send_sem=sems.at[0],
            recv_sem=sems.at[1],
            device_id=device,
            device_id_type=MESH,
        ).start()

    own.wait()
    sent = x_ref.at[pl.ds(0, count - 1)]
    pltpu.make_async_copy(sent, sent, sems.at[0]).wait()
    arrived = o_ref.at[pl.ds(0, count - 1)]
    pltpu.make_async_copy(arrived, arrived, sems.at[1]).wait()


def swap(parts, number):
    parity = lax.axis_size("row") // GRID
    return pl.pallas_call(
        functools.partial(swap_kernel, parity, GRID, lax.axis_size("col")),
        out_shape=jax.ShapeDtypeStruct(parts.shape, parts.dtype),
        in_specs=[pl.BlockSpec(memory_space=pltpu.VMEM)],
        out_specs=pl.BlockSpec(memory_space=pltpu.VMEM),
        scratch_shapes=[pltpu.SemaphoreType.DMA((3,))],
        compiler_params=pltpu.CompilerParams(collective_id=number, has_side_effects=True),
    )(parts)


def pack_tokens(tokens_in):
    channels = tokens_in.shape[-1]
    shaped = tokens_in.reshape(8, 2, 8, 4, 2, channels // 2)
    return shaped.transpose(0, 2, 4, 1, 3, 5).reshape(64, 16, channels // 2)


def unpack_tokens(blocks):
    half = blocks.shape[-1]
    shaped = blocks.reshape(8, 8, 2, 2, 4, half).transpose(0, 3, 1, 4, 2, 5)
    return shaped.reshape(16 * 32, 2 * half)


def split_sum(values):
    rows = lax.axis_size("row")
    parts = values.reshape(rows, -1, 128)
    own = jnp.sum(lax.all_to_all(parts, "row", 0, 0, tiled=True), axis=0)
    own = gather_sum(own.reshape(-1, 128), "col")
    spread = jnp.broadcast_to(own, (rows,) + own.shape)
    return lax.all_to_all(spread, "row", 0, 0, tiled=True)


def weight_grad(left_side, right_side):
    count = lax.axis_size("row") * lax.axis_size("col")
    partial = lax.dot_general(left_side, right_side, CONTRACT, preferred_element_type=jnp.float32)
    height, width = partial.shape
    parts = partial.astype(jnp.bfloat16).reshape(count, height // count, width)
    return jnp.sum(exchange_all(parts).astype(jnp.float32), axis=0)


HEAD_DIM = 32
QUAD = 4
PLACES = 64
GROUPS = 8


def attention_kernel(
    x_ref,
    wqkv_ref,
    wout_ref,
    bias_ref,
    ret_ref,
    normed_ref,
    proj_ref,
    context_ref,
    cot_ref,
    table_ref,
    spread,
    qkv,
    cgrad,
):
    channels = wout_ref.shape[0]
    factor = HEAD_DIM ** (-0.5)

    def gather(first_row, out_ref):
        for tile in range(2):
            block = x_ref[:, first_row : first_row + 16, tile * 128 : (tile + 1) * 128]
            spread[tile] = block.astype(jnp.float32).reshape(1024, 128)
        for group in range(GROUPS):
            for piece in range(4):
                half, tile = piece // 2, piece % 2
                rows = spread[tile, pl.ds(half * 8 + group, PLACES, stride=16), :]
                out_ref[group * PLACES : (group + 1) * PLACES, piece * 128 : (piece + 1) * 128] = (
                    rows.astype(jnp.bfloat16)
                )

    gather(0, normed_ref)
    gather(16, cot_ref)

    @pl.loop(0, 3 * channels // 256)
    def _(n):
        cols = pl.ds(pl.multiple_of(n * 256, 256), 256)
        qkv[:, cols] = jnp.dot(
            normed_ref[...], wqkv_ref[:, cols], preferred_element_type=jnp.float32
        ).astype(jnp.bfloat16)

    @pl.loop(0, channels // 256)
    def _(n):
        cols = pl.ds(pl.multiple_of(n * 256, 256), 256)
        cgrad[:, cols] = lax.dot_general(
            cot_ref[...], wout_ref[cols, :], BACKWARD, preferred_element_type=jnp.float32
        ).astype(jnp.bfloat16)

    table_ref[...] = jnp.zeros_like(table_ref)
    lane_head = lax.broadcasted_iota(jnp.int32, (PLACES, 128), 1) // HEAD_DIM
    masks = [(lane_head == h).astype(jnp.float32).astype(jnp.bfloat16) for h in range(QUAD)]
    masks_f = [(lane_head == h).astype(jnp.float32) for h in range(QUAD)]

    def widen(block):
        return jnp.concatenate([block * masks[h] for h in range(QUAD)], axis=0)

    def narrow(full):
        total = full[:PLACES] * masks_f[0]
        for h in range(1, QUAD):
            total = total + full[h * PLACES : (h + 1) * PLACES] * masks_f[h]
        return total

    @pl.loop(0, GROUPS)
    def _(group):
        rows = pl.ds(pl.multiple_of(group * PLACES, PLACES), PLACES)
        for quad in range(4):
            low = quad * 128
            queries = qkv[rows, low : low + 128]
            keys_in = qkv[rows, channels + low : channels + low + 128]
            values_in = qkv[rows, 2 * channels + low : 2 * channels + low + 128]
            grads = cgrad[rows, low : low + 128]
            queries_wide = widen(queries)
            grads_wide = widen(grads)
            scores = (
                lax.dot_general(keys_in, queries_wide, BACKWARD, preferred_element_type=jnp.float32)
                * factor
                + bias_ref[quad]
            )
            scores = jnp.exp(scores - jnp.max(scores, axis=0, keepdims=True))
            weights = scores * (1.0 / jnp.sum(scores, axis=0, keepdims=True))
            weights_b = weights.astype(jnp.bfloat16)
            context = narrow(
                lax.dot_general(weights_b, values_in, CONTRACT, preferred_element_type=jnp.float32)
            )
            context_ref[rows, low : low + 128] = context.astype(jnp.bfloat16)
            weights_grad = lax.dot_general(
                values_in, grads_wide, BACKWARD, preferred_element_type=jnp.float32
            )
            values_grad = jnp.dot(weights_b, grads_wide, preferred_element_type=jnp.float32)
            scores_grad = weights * (
                weights_grad - jnp.sum(weights * weights_grad, axis=0, keepdims=True)
            )
            table_ref[quad] += scores_grad
            scores_b = (scores_grad * factor).astype(jnp.bfloat16)
            queries_grad = narrow(
                lax.dot_general(scores_b, keys_in, CONTRACT, preferred_element_type=jnp.float32)
            )
            keys_grad = jnp.dot(scores_b, queries_wide, preferred_element_type=jnp.float32)
            proj_ref[rows, low : low + 128] = queries_grad.astype(jnp.bfloat16)
            proj_ref[rows, channels + low : channels + low + 128] = keys_grad.astype(jnp.bfloat16)
            proj_ref[rows, 2 * channels + low : 2 * channels + low + 128] = values_grad.astype(
                jnp.bfloat16
            )

    def scatter(read, first_row):
        for group in range(GROUPS):
            for piece in range(4):
                half, tile = piece // 2, piece % 2
                spread[tile, pl.ds(half * 8 + group, PLACES, stride=16), :] = read(group, piece)
        for tile in range(2):
            ret_ref[:, first_row : first_row + 16, tile * 128 : (tile + 1) * 128] = (
                spread[tile].reshape(64, 16, 128).astype(jnp.bfloat16)
            )

    def read_context(group, piece):
        return context_ref[
            group * PLACES : (group + 1) * PLACES, piece * 128 : (piece + 1) * 128
        ].astype(jnp.float32)

    scatter(read_context, 0)

    for n in range(channels // 256):
        grads = lax.dot_general(
            proj_ref[...],
            wqkv_ref[n * 256 : (n + 1) * 256, :],
            BACKWARD,
            preferred_element_type=jnp.float32,
        )
        for group in range(GROUPS):
            for tile in range(2):
                spread[tile, pl.ds(n * 8 + group, PLACES, stride=16), :] = grads[
                    group * PLACES : (group + 1) * PLACES, tile * 128 : (tile + 1) * 128
                ]
    for tile in range(2):
        ret_ref[:, 16:32, tile * 128 : (tile + 1) * 128] = (
            spread[tile].reshape(64, 16, 128).astype(jnp.bfloat16)
        )


def attention(blocks, w_qkv, w_out, bias):
    channels = w_out.shape[0]
    tokens = GROUPS * PLACES
    shapes = (
        jax.ShapeDtypeStruct(blocks.shape, jnp.bfloat16),
        jax.ShapeDtypeStruct((tokens, channels), jnp.bfloat16),
        jax.ShapeDtypeStruct((tokens, 3 * channels), jnp.bfloat16),
        jax.ShapeDtypeStruct((tokens, channels), jnp.bfloat16),
        jax.ShapeDtypeStruct((tokens, channels), jnp.bfloat16),
        jax.ShapeDtypeStruct(bias.shape, jnp.float32),
    )
    return pl.pallas_call(
        attention_kernel,
        out_shape=shapes,
        in_specs=[pl.BlockSpec(memory_space=pltpu.VMEM)] * 4,
        out_specs=[pl.BlockSpec(memory_space=pltpu.VMEM)] * 6,
        scratch_shapes=[
            pltpu.VMEM((2, 1024, 128), jnp.float32),
            pltpu.VMEM((tokens, 3 * channels), jnp.bfloat16),
            pltpu.VMEM((tokens, channels), jnp.bfloat16),
        ],
        compiler_params=pltpu.CompilerParams(vmem_limit_bytes=40 * 1024 * 1024),
    )(blocks, w_qkv, w_out, bias)


def on_device(
    inputs, out_grad, w_expand, dw_kernel, se_reduce, se_expand, w_project, w_qkv, w_out, pos_table
):
    images, tile_rows, tile_cols, channels = inputs.shape
    hidden_units = w_expand.shape[1]
    heads = pos_table.shape[0]
    places = GRID * GRID
    full_rows = tile_rows * lax.axis_size("row")
    full_cols = tile_cols * lax.axis_size("col")
    cells = full_rows * full_cols
    factor = (images * cells) ** (-0.5)
    tokens = images * tile_rows * tile_cols
    onehot = offset_table(GRID)
    bias = (
        jnp.dot(pos_table, onehot, precision=HIGHEST)
        .reshape(heads // QUAD, QUAD, places, places)
        .transpose(0, 2, 1, 3)
        .reshape(heads // QUAD, places, QUAD * places)
    )
    first_standardized, inverse_deviation_first = layer_normalize(inputs)
    first_normed_input = first_standardized.astype(jnp.bfloat16)
    pre_expand = jnp.dot(
        first_normed_input.reshape(tokens, channels), w_expand, preferred_element_type=jnp.float32
    )
    expanded_f, slope_expand = gelu_slope(
        pre_expand.reshape(images, tile_rows, tile_cols, hidden_units)
    )
    padded = padded_2(expanded_f.astype(jnp.bfloat16), (("row", 1), ("col", 2)), 1)
    pre_mix = depthwise(padded, dw_kernel)
    mixed, slope_mix = gelu_slope(pre_mix)
    pooled = small_sum(jnp.sum(mixed, axis=(1, 2)).reshape(-1, 128), 3).reshape(images, -1) / cells
    squeeze_pre = jnp.dot(pooled, se_reduce, precision=HIGHEST)
    squeeze_sig = jax.nn.sigmoid(squeeze_pre)
    squeezed = squeeze_pre * squeeze_sig
    gate = jax.nn.sigmoid(jnp.dot(squeezed, se_expand, precision=HIGHEST))
    scaled = (mixed * gate[:, None, None, :]).astype(jnp.bfloat16).reshape(tokens, hidden_units)
    middle_activation = inputs.astype(jnp.float32).reshape(tokens, channels) + jnp.dot(
        scaled, w_project, preferred_element_type=jnp.float32
    )
    second_standardized, inverse_deviation_second = layer_normalize(middle_activation)
    second_normed_input = second_standardized.astype(jnp.bfloat16)
    flattened_cotangent = out_grad.reshape(tokens, channels)
    outgoing = jnp.concatenate(
        [
            pack_tokens(second_normed_input.reshape(tile_rows, tile_cols, channels)),
            pack_tokens(out_grad.reshape(tile_rows, tile_cols, channels)),
        ],
        axis=1,
    )
    returned, grid_normed, grid_proj, grid_context, grid_cotangent, scores_sum = attention(
        swap(outgoing, 1), w_qkv, w_out, bias
    )
    table_part = lax.dot_general(
        scores_sum.reshape(heads // QUAD, places, QUAD, places)
        .transpose(0, 2, 1, 3)
        .reshape(heads, places * places),
        onehot,
        BACKWARD,
        precision=HIGHEST,
    )
    out_proj_grad = weight_grad(grid_context, grid_cotangent) * factor
    qkv_grad = weight_grad(grid_normed, grid_proj) * factor
    returned = swap(returned, 2)
    context_flat = unpack_tokens(returned[:, :16])
    second_normed_gradient = unpack_tokens(returned[:, 16:])
    block_out = (
        middle_activation + jnp.dot(context_flat, w_out, preferred_element_type=jnp.float32)
    ).astype(jnp.bfloat16)
    middle_gradient = flattened_cotangent.astype(jnp.float32) + norm_backward_pass(
        second_standardized, inverse_deviation_second, second_normed_gradient
    )
    middle_b = middle_gradient.astype(jnp.bfloat16)
    project_grad = weight_grad(scaled, middle_b) * factor
    scaled_grad = lax.dot_general(
        middle_b, w_project, BACKWARD, preferred_element_type=jnp.float32
    ).reshape(images, tile_rows, tile_cols, hidden_units)
    gate_grad = small_sum(jnp.sum(scaled_grad * mixed, axis=(1, 2)).reshape(-1, 128), 4).reshape(
        images, -1
    )
    excite_grad = gate_grad * gate * (1.0 - gate)
    squeezed_grad = lax.dot_general(excite_grad, se_expand, BACKWARD, precision=HIGHEST)
    squeeze_grad = squeezed_grad * squeeze_sig * (1.0 + squeeze_pre * (1.0 - squeeze_sig))
    pooled_grad = lax.dot_general(squeeze_grad, se_reduce, BACKWARD, precision=HIGHEST)
    se_reduce_grad = lax.dot_general(pooled, squeeze_grad, CONTRACT, precision=HIGHEST) * factor
    se_expand_grad = lax.dot_general(squeezed, excite_grad, CONTRACT, precision=HIGHEST) * factor
    premix_grad = (
        (scaled_grad * gate[:, None, None, :] + pooled_grad[:, None, None, :] / cells) * slope_mix
    ).astype(jnp.bfloat16)
    grad_padded = padded_2(premix_grad, (("row", 1), ("col", 2)), 1)
    kernel_part = kernel_terms(padded, premix_grad)
    expanded_grad = depthwise(grad_padded, dw_kernel[::-1, ::-1])
    preexp_grad = (expanded_grad * slope_expand).astype(jnp.bfloat16).reshape(tokens, hidden_units)
    expand_grad = weight_grad(first_normed_input.reshape(tokens, channels), preexp_grad) * factor
    first_normed_gradient = lax.dot_general(
        preexp_grad, w_expand, BACKWARD, preferred_element_type=jnp.float32
    ).reshape(images, tile_rows, tile_cols, channels)
    input_gradient = (
        middle_gradient.reshape(images, tile_rows, tile_cols, channels)
        + norm_backward_pass(first_standardized, inverse_deviation_first, first_normed_gradient)
    ).astype(jnp.bfloat16)
    small = jnp.concatenate([kernel_part.reshape(-1), table_part.reshape(-1)])
    unit = lax.axis_size("row") * 1024
    room = -small.shape[0] % unit
    small = split_sum(jnp.pad(small, (0, room))).reshape(-1)
    kernel_size = kernel_part.size
    kernel_sum = small[:kernel_size].reshape(kernel_part.shape)
    table_sum = small[kernel_size : kernel_size + table_part.size].reshape(table_part.shape)
    return (
        block_out.reshape(images, tile_rows, tile_cols, channels),
        input_gradient,
        expand_grad,
        project_grad,
        qkv_grad,
        out_proj_grad,
        kernel_sum * factor,
        se_reduce_grad,
        se_expand_grad,
        table_sum * factor,
    )


def solution(mesh):
    placed = (
        P(None, "row", "col", None),
        P(None, "row", "col", None),
        P(),
        P(),
        P(),
        P(),
        P(),
        P(),
        P(),
        P(),
    )
    return jax.shard_map(
        on_device,
        mesh=mesh,
        in_specs=placed,
        out_specs=(
            P(None, "row", "col", None),
            P(None, "row", "col", None),
            P(("row", "col"), None),
            P(("row", "col"), None),
            P(("row", "col"), None),
            P(("row", "col"), None),
            P(),
            P(),
            P(),
            P(),
        ),
        check_vma=False,
    )
```

```python
import functools
import math

import jax
import jax.numpy as jnp
from jax import lax
from jax.experimental import pallas as pl
from jax.experimental.pallas import tpu as pltpu
from jax.sharding import PartitionSpec as P

GRID = 8


EPSILON = 1e-05
GELU_SCALE = math.sqrt(2.0 / math.pi)
HIGHEST = lax.Precision.HIGHEST
MESH = pl.DeviceIdType.MESH
CONTRACT = (((0,), (0,)), ((), ()))
BACKWARD = (((1,), (1,)), ((), ()))


def gelu_slope(values):
    cubic = values * values * values
    bent = jnp.tanh(GELU_SCALE * (values + 0.044715 * cubic))
    result = 0.5 * values * (1.0 + bent)
    slope = 0.5 * (1.0 + bent) + 0.5 * values * (1.0 - bent * bent) * GELU_SCALE * (
        1.0 + 3.0 * 0.044715 * values * values
    )
    return (result, slope)


def layer_normalize(values):
    values = values.astype(jnp.float32)
    centred = values - jnp.mean(values, axis=-1, keepdims=True)
    inverse = lax.rsqrt(jnp.mean(centred * centred, axis=-1, keepdims=True) + EPSILON)
    return (centred * inverse, inverse)


def norm_backward_pass(normal_values, inverse, grads):
    grads = grads.astype(jnp.float32)
    return inverse * (
        grads
        - jnp.mean(grads, axis=-1, keepdims=True)
        - normal_values * jnp.mean(grads * normal_values, axis=-1, keepdims=True)
    )


def offset_table(side):
    places = jnp.arange(side * side, dtype=jnp.int32)
    place_row = places // side
    place_col = places % side
    offset_index = (
        (place_row[None, :] - place_row[:, None] + side - 1) * (2 * side - 1)
        + place_col[None, :]
        - place_col[:, None]
        + side
        - 1
    )
    table_slots = jnp.arange((2 * side - 1) ** 2, dtype=jnp.int32)
    return (table_slots[:, None] == offset_index.reshape(1, -1)).astype(jnp.float32)


AXES = ("row", "col")


def halo_kernel(rows, cols, height, width, top_ref, down_ref, left_ref, right_ref, o_ref, sems):
    row = lax.axis_index("row")
    col = lax.axis_index("col")
    barrier = pltpu.get_barrier_semaphore()
    up, down = lax.rem(row + rows - 1, rows), lax.rem(row + 1, rows)
    left, right = lax.rem(col + cols - 1, cols), lax.rem(col + 1, cols)
    last = width - 16
    sends = (
        (down_ref, 0, width, (down, col)),
        (top_ref, width, width, (up, col)),
        (right_ref, 2 * width, height, (row, right)),
        (left_ref, 2 * width + height, height, (row, left)),
        (down_ref.at[pl.ds(last, 16)], 2 * (width + height), 16, (down, right)),
        (down_ref.at[pl.ds(0, 16)], 2 * (width + height) + 16, 16, (down, left)),
        (top_ref.at[pl.ds(last, 16)], 2 * (width + height) + 32, 16, (up, right)),
        (top_ref.at[pl.ds(0, 16)], 2 * (width + height) + 48, 16, (up, left)),
    )
    for _, _, _, device in sends:
        pl.semaphore_signal(barrier, inc=1, device_id=device, device_id_type=MESH)
    pl.semaphore_wait(barrier, len(sends))
    copies = []
    for number, (source, start, size, device) in enumerate(sends):
        copies.append(
            pltpu.make_async_remote_copy(
                src_ref=source,
                dst_ref=o_ref.at[pl.ds(start, size)],
                send_sem=sems.at[0, number],
                recv_sem=sems.at[1, number],
                device_id=device,
                device_id_type=MESH,
            )
        )
        copies[-1].start()
    for copy in copies:
        copy.wait()


def halo(cells, number):
    height, width, features = cells.shape
    rows, cols = lax.axis_size("row"), lax.axis_size("col")
    total = 2 * (width + height) + 64

    def body(*refs):
        halo_kernel(rows, cols, height, width, *refs)

    return pl.pallas_call(
        body,
        out_shape=jax.ShapeDtypeStruct((total, features), cells.dtype),
        in_specs=[pl.BlockSpec(memory_space=pltpu.VMEM)] * 4,
        out_specs=pl.BlockSpec(memory_space=pltpu.VMEM),
        scratch_shapes=[pltpu.SemaphoreType.DMA((2, 8))],
        compiler_params=pltpu.CompilerParams(collective_id=number, has_side_effects=True),
    )(cells[0], cells[-1], cells[:, 0], cells[:, -1])


def reduce_kernel(rows, cols, w_ref, s_ref, o_ref, so_ref, half, got, rs_buf, own_buf, col_buf, sems):
    row = lax.axis_index("row")
    col = lax.axis_index("col")
    depth = cols // 2
    core = lax.rem(col, 2)
    count = rows * depth
    me = row * depth + col // 2
    steps = 4
    span = count // steps
    barrier = pltpu.get_barrier_semaphore()
    pair = (row, col - core + (1 - core))

    def place(k):
        peer = lax.rem(me + k, count)
        return peer, (peer // depth, lax.rem(peer, depth) * 2 + core)

    def signal(device):
        pl.semaphore_signal(barrier, inc=1, device_id=device, device_id_type=MESH)

    def wait_like(ref, sem):
        pltpu.make_async_copy(ref, ref, sem).wait()

    @pl.loop(1, count)
    def _(k):
        signal(place(k)[1])

    @pl.loop(0, depth)
    def _(k):
        signal((row, lax.rem(col // 2 + k, depth) * 2 + (1 - core)))

    rs_buf[row] = s_ref[row]
    pl.semaphore_wait(barrier, count - 1 + depth)

    for step in range(steps):

        @pl.loop(step * span, (step + 1) * span)
        def _(k):
            peer = lax.rem(me + k, count)
            pltpu.make_async_remote_copy(
                src_ref=w_ref.at[peer, 1 - core],
                dst_ref=half.at[step, k - step * span],
                send_sem=sems.at[0],
                recv_sem=sems.at[1 + step],
                device_id=pair,
                device_id_type=MESH,
            ).start()

    @pl.loop(1, rows)
    def _(k):
        other = lax.rem(row + k, rows)
        pltpu.make_async_remote_copy(
            src_ref=s_ref.at[other],
            dst_ref=rs_buf.at[row],
            send_sem=sems.at[5],
            recv_sem=sems.at[6],
            device_id=(other, col),
            device_id_type=MESH,
        ).start()

    for step in range(steps):
        wait_like(half.at[step], sems.at[1 + step])

        @pl.loop(0, span)
        def _(k):
            peer, device = place(k + step * span)
            mine = w_ref[peer, core].astype(jnp.float32) + half[step, k].astype(jnp.float32)
            half[step, k] = mine.astype(jnp.bfloat16)

            @pl.when(k + step * span > 0)
            def _():
                pltpu.make_async_remote_copy(
                    src_ref=half.at[step, k],
                    dst_ref=got.at[me],
                    send_sem=sems.at[7],
                    recv_sem=sems.at[8],
                    device_id=device,
                    device_id_type=MESH,
                ).start()

        if step == 0:
            got[me] = half[0, 0]
            wait_like(rs_buf.at[pl.ds(0, rows - 1)], sems.at[6])
            total = rs_buf[0]
            for k in range(1, rows):
                total = total + rs_buf[k]
            own_buf[...] = total
            col_buf[col] = total

            @pl.loop(1, cols)
            def _(k):
                pltpu.make_async_remote_copy(
                    src_ref=own_buf,
                    dst_ref=col_buf.at[col],
                    send_sem=sems.at[9],
                    recv_sem=sems.at[10],
                    device_id=(row, lax.rem(col + k, cols)),
                    device_id_type=MESH,
                ).start()

        if step == 2:
            wait_like(col_buf.at[pl.ds(0, cols - 1)], sems.at[10])
            total = col_buf[0]
            for k in range(1, cols):
                total = total + col_buf[k]
            so_ref[row] = total

            @pl.loop(1, rows)
            def _(k):
                pltpu.make_async_remote_copy(
                    src_ref=so_ref.at[row],
                    dst_ref=so_ref.at[row],
                    send_sem=sems.at[11],
                    recv_sem=sems.at[12],
                    device_id=(lax.rem(row + k, rows), col),
                    device_id_type=MESH,
                ).start()

    wait_like(got.at[pl.ds(0, count - 1)], sems.at[8])
    height = o_ref.shape[0]
    for low in range(0, height, 16):

        def add(k, total):
            return total + got[k, low : low + 16, :].astype(jnp.float32)

        o_ref[low : low + 16, :] = lax.fori_loop(
            0, count, add, jnp.zeros((16, o_ref.shape[1]), jnp.float32)
        )
    wait_like(so_ref.at[pl.ds(0, rows - 1)], sems.at[12])
    wait_like(so_ref.at[pl.ds(0, rows - 1)], sems.at[11])
    wait_like(col_buf.at[pl.ds(0, cols - 1)], sems.at[9])
    wait_like(rs_buf.at[pl.ds(0, rows - 1)], sems.at[5])
    wait_like(half, sems.at[0])
    wait_like(got.at[pl.ds(0, count - 1)], sems.at[7])


def reduce_all(parts, small, number):
    rows, cols = lax.axis_size("row"), lax.axis_size("col")
    count, _, height, width = parts.shape
    block = small.shape[1:]
    return pl.pallas_call(
        functools.partial(reduce_kernel, rows, cols),
        out_shape=(
            jax.ShapeDtypeStruct((height, width), jnp.float32),
            jax.ShapeDtypeStruct(small.shape, jnp.float32),
        ),
        in_specs=[pl.BlockSpec(memory_space=pltpu.VMEM)] * 2,
        out_specs=[pl.BlockSpec(memory_space=pltpu.VMEM)] * 2,
        scratch_shapes=[
            pltpu.VMEM((4, count // 4, height, width), jnp.bfloat16),
            pltpu.VMEM((count, height, width), jnp.bfloat16),
            pltpu.VMEM(small.shape, jnp.float32),
            pltpu.VMEM(block, jnp.float32),
            pltpu.VMEM((cols,) + block, jnp.float32),
            pltpu.SemaphoreType.DMA((13,)),
        ],
        compiler_params=pltpu.CompilerParams(
            collective_id=number, has_side_effects=True, vmem_limit_bytes=40 * 1024 * 1024
        ),
    )(parts, small)


def small_sum_kernel(rows, cols, x_ref, o_ref, row_buf, sum_buf, col_buf, sems):
    row = lax.axis_index("row")
    col = lax.axis_index("col")
    barrier = pltpu.get_barrier_semaphore()

    def row_peer(k):
        return lax.rem(row + k, rows)

    def col_peer(k):
        return lax.rem(col + k, cols)

    @pl.loop(1, rows)
    def _(k):
        pl.semaphore_signal(barrier, inc=1, device_id=(row_peer(k), col), device_id_type=MESH)

    @pl.loop(1, cols)
    def _(k):
        pl.semaphore_signal(barrier, inc=1, device_id=(row, col_peer(k)), device_id_type=MESH)

    row_buf[row] = x_ref[...]
    pl.semaphore_wait(barrier, rows + cols - 2)

    @pl.loop(1, rows)
    def _(k):
        pltpu.make_async_remote_copy(
            src_ref=x_ref,
            dst_ref=row_buf.at[row],
            send_sem=sems.at[0],
            recv_sem=sems.at[1],
            device_id=(row_peer(k), col),
            device_id_type=MESH,
        ).start()

    arrived = row_buf.at[pl.ds(0, rows - 1)]
    pltpu.make_async_copy(arrived, arrived, sems.at[1]).wait()
    total = row_buf[0]
    for k in range(1, rows):
        total = total + row_buf[k]
    sum_buf[...] = total
    col_buf[col] = total

    @pl.loop(1, cols)
    def _(k):
        pltpu.make_async_remote_copy(
            src_ref=sum_buf,
            dst_ref=col_buf.at[col],
            send_sem=sems.at[2],
            recv_sem=sems.at[3],
            device_id=(row, col_peer(k)),
            device_id_type=MESH,
        ).start()

    other = col_buf.at[pl.ds(0, cols - 1)]
    pltpu.make_async_copy(other, other, sems.at[3]).wait()
    total = col_buf[0]
    for k in range(1, cols):
        total = total + col_buf[k]
    o_ref[...] = total
    pltpu.make_async_copy(arrived, arrived, sems.at[0]).wait()
    pltpu.make_async_copy(other, other, sems.at[2]).wait()


def small_sum(values, number):
    rows = lax.axis_size("row")
    cols = lax.axis_size("col")
    shape = values.shape
    return pl.pallas_call(
        functools.partial(small_sum_kernel, rows, cols),
        out_shape=jax.ShapeDtypeStruct(shape, jnp.float32),
        in_specs=[pl.BlockSpec(memory_space=pltpu.VMEM)],
        out_specs=pl.BlockSpec(memory_space=pltpu.VMEM),
        scratch_shapes=[
            pltpu.VMEM((rows,) + shape, jnp.float32),
            pltpu.VMEM(shape, jnp.float32),
            pltpu.VMEM((cols,) + shape, jnp.float32),
            pltpu.SemaphoreType.DMA((4,)),
        ],
        compiler_params=pltpu.CompilerParams(collective_id=number, has_side_effects=True),
    )(values)


def swap_kernel(parity, side, cols, x_ref, o_ref, sems):
    row = lax.axis_index("row")
    col = lax.axis_index("col")
    kind = lax.rem(row, parity)
    count = side * cols
    me = (row // parity) * cols + col
    barrier = pltpu.get_barrier_semaphore()

    def place(k):
        peer = lax.rem(me + k, count)
        return peer, ((peer // cols) * parity + kind, lax.rem(peer, cols))

    @pl.loop(1, count)
    def _(k):
        pl.semaphore_signal(barrier, inc=1, device_id=place(k)[1], device_id_type=MESH)

    own = pltpu.make_async_copy(x_ref.at[me], o_ref.at[me], sems.at[2])
    own.start()
    pl.semaphore_wait(barrier, count - 1)

    @pl.loop(1, count)
    def _(k):
        peer, device = place(k)
        pltpu.make_async_remote_copy(
            src_ref=x_ref.at[peer],
            dst_ref=o_ref.at[me],
            send_sem=sems.at[0],
            recv_sem=sems.at[1],
            device_id=device,
            device_id_type=MESH,
        ).start()

    own.wait()
    sent = x_ref.at[pl.ds(0, count - 1)]
    pltpu.make_async_copy(sent, sent, sems.at[0]).wait()
    arrived = o_ref.at[pl.ds(0, count - 1)]
    pltpu.make_async_copy(arrived, arrived, sems.at[1]).wait()


def swap(parts, number):
    parity = lax.axis_size("row") // GRID
    return pl.pallas_call(
        functools.partial(swap_kernel, parity, GRID, lax.axis_size("col")),
        out_shape=jax.ShapeDtypeStruct(parts.shape, parts.dtype),
        in_specs=[pl.BlockSpec(memory_space=pltpu.VMEM)],
        out_specs=pl.BlockSpec(memory_space=pltpu.VMEM),
        scratch_shapes=[pltpu.SemaphoreType.DMA((3,))],
        compiler_params=pltpu.CompilerParams(collective_id=number, has_side_effects=True),
    )(parts)


ROWS = 16
COLS = 32
MAIN = (ROWS + 2) * COLS
SIDE = (ROWS + 2) * 8


def edge_masks():
    row, col = lax.axis_index("row"), lax.axis_index("col")
    rows, cols = lax.axis_size("row"), lax.axis_size("col")
    return tuple(
        jnp.where(present, 1.0, 0.0).astype(jnp.float32)
        for present in (row > 0, row < rows - 1, col > 0, col < cols - 1)
    )


def fill_sides(got_ref, side_ref, masks, tiles):
    up, down, left, right = masks
    start = 2 * COLS
    corner = 2 * (COLS + ROWS)
    for tile in range(tiles):
        lanes = slice(tile * 128, (tile + 1) * 128)
        before = got_ref[start : start + ROWS, lanes].astype(jnp.float32)
        after = got_ref[start + ROWS : start + 2 * ROWS, lanes].astype(jnp.float32)
        side_ref[tile, pl.ds(8, ROWS, stride=8), :] = after * right
        side_ref[tile, pl.ds(15, ROWS, stride=8), :] = before * left
        corners = got_ref[corner : corner + 64, lanes].astype(jnp.float32)
        side_ref[tile, 7:8, :] = corners[15:16] * (up * left)
        side_ref[tile, 0:1, :] = corners[16:17] * (up * right)
        side_ref[tile, SIDE - 1 : SIDE, :] = corners[47:48] * (down * left)
        side_ref[tile, SIDE - 8 : SIDE - 7, :] = corners[48:49] * (down * right)


def expand_kernel(
    x_ref, got_ref, w_ref, taps_ref, mixed_ref, slope_mix_ref, slope_ref, main_ref, side_out_ref,
    pooled_ref, normed, normed_side, side, pre, pre_side, padded
):
    step = pl.program_id(0)

    @pl.when(step == 0)
    def _():
        masks = edge_masks()
        side[...] = jnp.zeros_like(side)
        fill_sides(got_ref, side, masks, 4)
        values = jnp.concatenate([side[tile] for tile in range(4)], axis=-1)
        present = jnp.max(jnp.abs(values), axis=-1, keepdims=True) > 0.0
        standard = layer_normalize(values)[0]
        normed_side[...] = jnp.where(present, standard, 0.0).astype(jnp.bfloat16)
        normed[0:COLS, :] = (layer_normalize(got_ref[0:COLS, :])[0] * masks[0]).astype(jnp.bfloat16)
        normed[MAIN - COLS : MAIN, :] = (
            layer_normalize(got_ref[COLS : 2 * COLS, :])[0] * masks[1]
        ).astype(jnp.bfloat16)

        @pl.loop(0, ROWS)
        def _(y):
            rows = pl.ds(pl.multiple_of(y * COLS, COLS), COLS)
            after = pl.ds(pl.multiple_of((y + 1) * COLS, COLS), COLS)
            normed[after, :] = layer_normalize(x_ref[rows, :])[0].astype(jnp.bfloat16)

    width = w_ref.shape[1]
    pre[...] = jnp.dot(normed[...], w_ref[...], preferred_element_type=jnp.float32)
    pre_side[...] = jnp.dot(normed_side[...], w_ref[...], preferred_element_type=jnp.float32)

    @pl.loop(0, ROWS + 2)
    def _(y):
        rows = pl.ds(pl.multiple_of(y * COLS, COLS), COLS)
        result, slope = gelu_slope(pre[rows, :])
        rounded = result.astype(jnp.bfloat16)
        main_ref[rows, :] = rounded
        padded[y, 8 : 8 + COLS, :] = rounded.astype(jnp.float32)

        @pl.when((y > 0) & (y <= ROWS))
        def _():
            before = pl.ds(pl.multiple_of((y - 1) * COLS, COLS), COLS)
            slope_ref[before, :] = slope

        eight = pl.ds(pl.multiple_of(y * 8, 8), 8)
        edge = gelu_slope(pre_side[eight, :])[0].astype(jnp.bfloat16).astype(jnp.float32)
        pre_side[eight, :] = edge
        padded[y, 0:8, :] = edge
        padded[y, 8 + COLS : 16 + COLS, :] = edge

    side_out_ref[...] = pre_side[...].astype(jnp.bfloat16)

    def mix(y, total):
        summed = jnp.zeros((COLS, width), jnp.float32)
        for r in range(3):
            for c in range(3):
                window = padded[y + r, 7 + c : 7 + c + COLS, :]
                summed = summed + window * taps_ref[3 * r + c : 3 * r + c + 1, :]
        mixed, slope = gelu_slope(summed)
        rows = pl.ds(pl.multiple_of(y * COLS, COLS), COLS)
        mixed_ref[rows, :] = mixed
        slope_mix_ref[rows, :] = slope
        return total + jnp.sum(mixed.reshape(COLS // 8, 8, width), axis=0)

    total = lax.fori_loop(0, ROWS, mix, jnp.zeros((8, width), jnp.float32))
    total = jnp.sum(total, axis=0, keepdims=True)
    for tile in range(width // 128):
        pooled_ref[0, tile : tile + 1, :] = total[:, tile * 128 : (tile + 1) * 128]


def expand_and_mix(tokens_in, got, w_expand, taps):
    tokens, channels = tokens_in.shape
    hidden = w_expand.shape[1]
    width = 256
    steps = hidden // width

    def fixed(shape):
        return pl.BlockSpec(shape, lambda e: (0, 0))

    def moving(height):
        return pl.BlockSpec((height, width), lambda e: (0, e))

    wide = jax.ShapeDtypeStruct((tokens, hidden), jnp.float32)
    return pl.pallas_call(
        expand_kernel,
        grid=(steps,),
        out_shape=(
            wide,
            wide,
            wide,
            jax.ShapeDtypeStruct((MAIN, hidden), jnp.bfloat16),
            jax.ShapeDtypeStruct((SIDE, hidden), jnp.bfloat16),
            jax.ShapeDtypeStruct((steps, width // 128, 128), jnp.float32),
        ),
        in_specs=[fixed(tokens_in.shape), fixed(got.shape), moving(channels), moving(9)],
        out_specs=[
            moving(tokens),
            moving(tokens),
            moving(tokens),
            moving(MAIN),
            moving(SIDE),
            pl.BlockSpec((1, width // 128, 128), lambda e: (e, 0, 0)),
        ],
        scratch_shapes=[
            pltpu.VMEM((MAIN, channels), jnp.bfloat16),
            pltpu.VMEM((SIDE, channels), jnp.bfloat16),
            pltpu.VMEM((4, SIDE, 128), jnp.float32),
            pltpu.VMEM((MAIN, width), jnp.float32),
            pltpu.VMEM((SIDE, width), jnp.float32),
            pltpu.VMEM((ROWS + 2, COLS + 16, width), jnp.float32),
        ],
        compiler_params=pltpu.CompilerParams(vmem_limit_bytes=40 * 1024 * 1024),
    )(tokens_in, got, w_expand, taps)


def project_kernel(
    mixed_ref, gate_ref, x_ref, cot_ref, w_ref, scaled_ref, middle_ref, out_ref, flat, packed
):
    scaled = (mixed_ref[...] * gate_ref[...]).astype(jnp.bfloat16)
    scaled_ref[...] = scaled
    middle = x_ref[...].astype(jnp.float32) + jnp.dot(
        scaled, w_ref[...], preferred_element_type=jnp.float32
    )
    middle_ref[...] = middle

    def pack(values, first_row):
        for piece in range(4):
            flat[piece] = values[:, piece * 128 : (piece + 1) * 128]
        for piece in range(4):
            half, tile = piece // 2, piece % 2
            for a in range(2):
                for place in range(8):
                    source = a * 64 + (place // 4) * 32 + place % 4
                    packed[tile, pl.ds(a * 128 + half * 8 + place, 8, stride=16), :] = flat[
                        piece, pl.ds(source, 8, stride=4), :
                    ]
        for tile in range(2):
            out_ref[:, first_row : first_row + 16, tile * 128 : (tile + 1) * 128] = (
                packed[tile].reshape(16, 16, 128).astype(jnp.bfloat16)
            )

    pack(layer_normalize(middle)[0], 0)
    pack(cot_ref[...].astype(jnp.float32), 16)


def project(mixed, gate, tokens_in, cotangent, w_project):
    tokens, hidden = mixed.shape
    channels = w_project.shape[1]
    height = 128

    def moving(width):
        return pl.BlockSpec((height, width), lambda t: (t, 0))

    def fixed(shape):
        return pl.BlockSpec(shape, lambda t: (0, 0))

    return pl.pallas_call(
        project_kernel,
        grid=(tokens // height,),
        out_shape=(
            jax.ShapeDtypeStruct((tokens, hidden), jnp.bfloat16),
            jax.ShapeDtypeStruct((tokens, channels), jnp.float32),
            jax.ShapeDtypeStruct((64, 32, channels // 2), jnp.bfloat16),
        ),
        in_specs=[
            moving(hidden),
            fixed((1, hidden)),
            moving(channels),
            moving(channels),
            fixed(w_project.shape),
        ],
        out_specs=[
            moving(hidden),
            moving(channels),
            pl.BlockSpec((16, 32, channels // 2), lambda t: (t, 0, 0)),
        ],
        scratch_shapes=[
            pltpu.VMEM((4, height, 128), jnp.float32),
            pltpu.VMEM((2, 256, 128), jnp.float32),
        ],
        compiler_params=pltpu.CompilerParams(vmem_limit_bytes=40 * 1024 * 1024),
    )(mixed, gate, tokens_in, cotangent, w_project)


def middle_kernel(
    ret_ref, middle_ref, cot_ref, mixed_ref, wout_ref, wproj_ref, out_ref, grad_ref, grad_b_ref,
    scaled_grad_ref, gate_ref, flat, packed, total
):
    step = pl.program_id(0)

    def unpack(first_row):
        for tile in range(2):
            block = ret_ref[:, first_row : first_row + 16, tile * 128 : (tile + 1) * 128]
            packed[tile] = block.astype(jnp.float32).reshape(256, 128)
        for piece in range(4):
            half, tile = piece // 2, piece % 2
            for a in range(2):
                for place in range(8):
                    target = a * 64 + (place // 4) * 32 + place % 4
                    flat[piece, pl.ds(target, 8, stride=4), :] = packed[
                        tile, pl.ds(a * 128 + half * 8 + place, 8, stride=16), :
                    ]
        return jnp.concatenate([flat[piece] for piece in range(4)], axis=-1)

    middle = middle_ref[...]
    context = unpack(0).astype(jnp.bfloat16)
    out_ref[...] = (
        middle + jnp.dot(context, wout_ref[...], preferred_element_type=jnp.float32)
    ).astype(jnp.bfloat16)
    standard, inverse = layer_normalize(middle)
    grad = cot_ref[...].astype(jnp.float32) + norm_backward_pass(standard, inverse, unpack(16))
    grad_ref[...] = grad
    grad_b = grad.astype(jnp.bfloat16)
    grad_b_ref[...] = grad_b

    @pl.when(step == 0)
    def _():
        total[...] = jnp.zeros_like(total)

    hidden = wproj_ref.shape[0]
    for low in range(0, hidden, 512):
        scaled_grad = lax.dot_general(
            grad_b, wproj_ref[low : low + 512, :], BACKWARD, preferred_element_type=jnp.float32
        )
        scaled_grad_ref[:, low : low + 512] = scaled_grad
        terms = scaled_grad * mixed_ref[:, low : low + 512]
        total[:, low : low + 512] += jnp.sum(terms.reshape(-1, 8, 512), axis=0)

    @pl.when(step == pl.num_programs(0) - 1)
    def _():
        for tile in range(hidden // 128):
            gate_ref[tile : tile + 1, :] = jnp.sum(
                total[:, tile * 128 : (tile + 1) * 128], axis=0, keepdims=True
            )


def middle_backward(returned, middle, cotangent, mixed, w_out, w_project):
    tokens, hidden = mixed.shape
    channels = middle.shape[1]
    height = 128

    def moving(width):
        return pl.BlockSpec((height, width), lambda t: (t, 0))

    def fixed(shape):
        return pl.BlockSpec(shape, lambda t: (0, 0))

    return pl.pallas_call(
        middle_kernel,
        grid=(tokens // height,),
        out_shape=(
            jax.ShapeDtypeStruct((tokens, channels), jnp.bfloat16),
            jax.ShapeDtypeStruct((tokens, channels), jnp.float32),
            jax.ShapeDtypeStruct((tokens, channels), jnp.bfloat16),
            jax.ShapeDtypeStruct((tokens, hidden), jnp.float32),
            jax.ShapeDtypeStruct((hidden // 128, 128), jnp.float32),
        ),
        in_specs=[
            pl.BlockSpec((16, 32, channels // 2), lambda t: (t, 0, 0)),
            moving(channels),
            moving(channels),
            moving(hidden),
            fixed(w_out.shape),
            fixed(w_project.shape),
        ],
        out_specs=[
            moving(channels),
            moving(channels),
            moving(channels),
            moving(hidden),
            fixed((hidden // 128, 128)),
        ],
        scratch_shapes=[
            pltpu.VMEM((4, height, 128), jnp.float32),
            pltpu.VMEM((2, 256, 128), jnp.float32),
            pltpu.VMEM((8, hidden), jnp.float32),
        ],
        compiler_params=pltpu.CompilerParams(vmem_limit_bytes=40 * 1024 * 1024),
    )(returned, middle, cotangent, mixed, w_out, w_project)


def regroup(values, flat, place, first):
    for tile in range(4):
        flat[tile] = values[:, tile * 128 : (tile + 1) * 128]
    for tile in range(4):
        for r in range(4):
            place[tile, pl.ds(first + r, 128, stride=16), :] = flat[
                tile, pl.ds(r, 128, stride=4), :
            ]


def back_kernel(
    premix_ref, got_ref, main_ref, side_in_ref, slope_ref, w_ref, taps_ref, x_ref, grad_ref,
    out_ref, parts_ref, terms_ref, turned, side, padded, expanded, preexp, total, flat, place
):
    step = pl.program_id(0)
    last = pl.num_programs(0) - 1

    @pl.when(step == 0)
    def _():
        side[...] = jnp.zeros_like(side)
        total[...] = jnp.zeros_like(total)
        turned[...] = layer_normalize(x_ref[...])[0].T.astype(jnp.bfloat16)

    masks = edge_masks()
    fill_sides(got_ref, side, masks, 4)
    padded[0, 8 : 8 + COLS, :] = got_ref[0:COLS, :].astype(jnp.float32) * masks[0]
    padded[ROWS + 1, 8 : 8 + COLS, :] = got_ref[COLS : 2 * COLS, :].astype(jnp.float32) * masks[1]

    @pl.loop(0, ROWS)
    def _(y):
        rows = pl.ds(pl.multiple_of(y * COLS, COLS), COLS)
        padded[y + 1, 8 : 8 + COLS, :] = premix_ref[rows, :].astype(jnp.float32)

    pairs = (ROWS + 2) // 2

    @pl.loop(0, ROWS + 2)
    def _(y):
        rows = pl.ds(pl.multiple_of(y * COLS, COLS), COLS)
        expanded[y, 8 : 8 + COLS, :] = main_ref[rows, :].astype(jnp.float32)
        eight = pl.ds(pl.multiple_of(y * 8, 8), 8)
        edge = jnp.concatenate([side[tile, eight, :] for tile in range(4)], axis=-1)
        padded[y, 0:8, :] = edge
        padded[y, 8 + COLS : 16 + COLS, :] = edge

    @pl.loop(0, pairs)
    def _(y):
        both = side_in_ref[pl.ds(pl.multiple_of(y * 16, 16), 16), :].astype(jnp.float32)
        for k in range(2):
            edge = both[8 * k : 8 * k + 8]
            expanded[2 * y + k, 0:8, :] = edge
            expanded[2 * y + k, 8 + COLS : 16 + COLS, :] = edge

    for low in range(0, 512, 256):
        lanes = slice(low, low + 256)

        def unmix(y, sums):
            rows = pl.ds(pl.multiple_of(y * COLS, COLS), COLS)
            own = padded[y + 1, 8 : 8 + COLS, lanes]
            summed = jnp.zeros((COLS, 256), jnp.float32)
            new = []
            for r in range(3):
                for c in range(3):
                    window = padded[y + 2 - r, 9 - c : 9 - c + COLS, lanes]
                    summed = summed + window * taps_ref[3 * r + c : 3 * r + c + 1, lanes]
                    term = own * expanded[y + r, 7 + c : 7 + c + COLS, lanes]
                    new.append(sums[3 * r + c] + jnp.sum(term.reshape(-1, 8, 256), axis=0))
            preexp[rows, lanes] = (summed * slope_ref[rows, lanes]).astype(jnp.bfloat16)
            return tuple(new)

        sums = lax.fori_loop(0, ROWS, unmix, (jnp.zeros((8, 256), jnp.float32),) * 9)
        for k in range(9):
            terms_ref[k : k + 1, lanes] = jnp.sum(sums[k], axis=0, keepdims=True)

    regroup(
        jnp.dot(turned[...], preexp[...], preferred_element_type=jnp.float32), flat, place, step * 4
    )
    total[...] += lax.dot_general(
        preexp[...], w_ref[...], BACKWARD, preferred_element_type=jnp.float32
    )

    @pl.when(step == last)
    def _():
        for tile in range(4):
            parts_ref[:, :, tile * 128 : (tile + 1) * 128] = (
                place[tile].reshape(128, 16, 128).astype(jnp.bfloat16)
            )

        @pl.loop(0, ROWS)
        def _(y):
            rows = pl.ds(pl.multiple_of(y * COLS, COLS), COLS)
            standard, inverse = layer_normalize(x_ref[rows, :])
            out_ref[rows, :] = (
                grad_ref[rows, :] + norm_backward_pass(standard, inverse, total[rows, :])
            ).astype(jnp.bfloat16)


def mix_backward(premix, got, main, side, slope, w_expand, taps, tokens_in, grad):
    tokens, hidden = premix.shape
    channels = w_expand.shape[0]
    width = 512

    def fixed(shape):
        return pl.BlockSpec(shape, lambda e: (0,) * len(shape))

    def moving(height):
        return pl.BlockSpec((height, width), lambda e: (0, e))

    return pl.pallas_call(
        back_kernel,
        grid=(hidden // width,),
        out_shape=(
            jax.ShapeDtypeStruct((tokens, channels), jnp.bfloat16),
            jax.ShapeDtypeStruct((128, 16, width), jnp.bfloat16),
            jax.ShapeDtypeStruct((9, hidden), jnp.float32),
        ),
        in_specs=[
            moving(tokens),
            moving(got.shape[0]),
            moving(MAIN),
            moving(SIDE),
            moving(tokens),
            moving(channels),
            moving(9),
            fixed(tokens_in.shape),
            fixed(grad.shape),
        ],
        out_specs=[fixed((tokens, channels)), fixed((128, 16, width)), moving(9)],
        scratch_shapes=[
            pltpu.VMEM((channels, tokens), jnp.bfloat16),
            pltpu.VMEM((4, SIDE, 128), jnp.float32),
            pltpu.VMEM((ROWS + 2, COLS + 16, width), jnp.float32),
            pltpu.VMEM((ROWS + 2, COLS + 16, width), jnp.float32),
            pltpu.VMEM((tokens, width), jnp.bfloat16),
            pltpu.VMEM((tokens, channels), jnp.float32),
            pltpu.VMEM((4, tokens, 128), jnp.float32),
            pltpu.VMEM((4, 2048, 128), jnp.float32),
        ],
        compiler_params=pltpu.CompilerParams(vmem_limit_bytes=50 * 1024 * 1024),
    )(premix, got, main, side, slope, w_expand, taps, tokens_in, grad)


HEAD_DIM = 32
QUAD = 4
PLACES = 64
GROUPS = 8


def attention_kernel(
    x_ref,
    wqkv_ref,
    wout_ref,
    bias_ref,
    ret_ref,
    parts_ref,
    table_ref,
    spread,
    qkv,
    cgrad,
    normed_ref,
    proj_ref,
    context_ref,
    cot_ref,
    flat,
    place,
):
    channels = wout_ref.shape[0]
    factor = HEAD_DIM ** (-0.5)

    def gather(first_row, out_ref):
        for tile in range(2):
            block = x_ref[:, first_row : first_row + 16, tile * 128 : (tile + 1) * 128]
            spread[tile] = block.astype(jnp.float32).reshape(1024, 128)
        for group in range(GROUPS):
            for piece in range(4):
                half, tile = piece // 2, piece % 2
                rows = spread[tile, pl.ds(half * 8 + group, PLACES, stride=16), :]
                out_ref[group * PLACES : (group + 1) * PLACES, piece * 128 : (piece + 1) * 128] = (
                    rows.astype(jnp.bfloat16)
                )

    gather(0, normed_ref)
    gather(16, cot_ref)

    @pl.loop(0, 3 * channels // 256)
    def _(n):
        cols = pl.ds(pl.multiple_of(n * 256, 256), 256)
        qkv[:, cols] = jnp.dot(
            normed_ref[...], wqkv_ref[:, cols], preferred_element_type=jnp.float32
        ).astype(jnp.bfloat16)

    @pl.loop(0, channels // 256)
    def _(n):
        cols = pl.ds(pl.multiple_of(n * 256, 256), 256)
        cgrad[:, cols] = lax.dot_general(
            cot_ref[...], wout_ref[cols, :], BACKWARD, preferred_element_type=jnp.float32
        ).astype(jnp.bfloat16)

    table_ref[...] = jnp.zeros_like(table_ref)
    lane_head = lax.broadcasted_iota(jnp.int32, (PLACES, 128), 1) // HEAD_DIM
    masks = [(lane_head == h).astype(jnp.float32).astype(jnp.bfloat16) for h in range(QUAD)]
    masks_f = [(lane_head == h).astype(jnp.float32) for h in range(QUAD)]

    def widen(block):
        return jnp.concatenate([block * masks[h] for h in range(QUAD)], axis=0)

    def narrow(full):
        total = full[:PLACES] * masks_f[0]
        for h in range(1, QUAD):
            total = total + full[h * PLACES : (h + 1) * PLACES] * masks_f[h]
        return total

    @pl.loop(0, GROUPS)
    def _(group):
        rows = pl.ds(pl.multiple_of(group * PLACES, PLACES), PLACES)
        for quad in range(4):
            low = quad * 128
            queries = qkv[rows, low : low + 128]
            keys_in = qkv[rows, channels + low : channels + low + 128]
            values_in = qkv[rows, 2 * channels + low : 2 * channels + low + 128]
            grads = cgrad[rows, low : low + 128]
            queries_wide = widen(queries)
            grads_wide = widen(grads)
            scores = (
                lax.dot_general(keys_in, queries_wide, BACKWARD, preferred_element_type=jnp.float32)
                * factor
                + bias_ref[quad]
            )
            scores = jnp.exp(scores - jnp.max(scores, axis=0, keepdims=True))
            weights = scores * (1.0 / jnp.sum(scores, axis=0, keepdims=True))
            weights_b = weights.astype(jnp.bfloat16)
            context = narrow(
                lax.dot_general(weights_b, values_in, CONTRACT, preferred_element_type=jnp.float32)
            )
            context_ref[rows, low : low + 128] = context.astype(jnp.bfloat16)
            weights_grad = lax.dot_general(
                values_in, grads_wide, BACKWARD, preferred_element_type=jnp.float32
            )
            values_grad = jnp.dot(weights_b, grads_wide, preferred_element_type=jnp.float32)
            scores_grad = weights * (
                weights_grad - jnp.sum(weights * weights_grad, axis=0, keepdims=True)
            )
            table_ref[quad] += scores_grad
            scores_b = (scores_grad * factor).astype(jnp.bfloat16)
            queries_grad = narrow(
                lax.dot_general(scores_b, keys_in, CONTRACT, preferred_element_type=jnp.float32)
            )
            keys_grad = jnp.dot(scores_b, queries_wide, preferred_element_type=jnp.float32)
            proj_ref[rows, low : low + 128] = queries_grad.astype(jnp.bfloat16)
            proj_ref[rows, channels + low : channels + low + 128] = keys_grad.astype(jnp.bfloat16)
            proj_ref[rows, 2 * channels + low : 2 * channels + low + 128] = values_grad.astype(
                jnp.bfloat16
            )

    def scatter(read, first_row):
        for group in range(GROUPS):
            for piece in range(4):
                half, tile = piece // 2, piece % 2
                spread[tile, pl.ds(half * 8 + group, PLACES, stride=16), :] = read(group, piece)
        for tile in range(2):
            ret_ref[:, first_row : first_row + 16, tile * 128 : (tile + 1) * 128] = (
                spread[tile].reshape(64, 16, 128).astype(jnp.bfloat16)
            )

    def read_context(group, piece):
        return context_ref[
            group * PLACES : (group + 1) * PLACES, piece * 128 : (piece + 1) * 128
        ].astype(jnp.float32)

    scatter(read_context, 0)

    for n in range(channels // 256):
        grads = lax.dot_general(
            proj_ref[...],
            wqkv_ref[n * 256 : (n + 1) * 256, :],
            BACKWARD,
            preferred_element_type=jnp.float32,
        )
        for group in range(GROUPS):
            for tile in range(2):
                spread[tile, pl.ds(n * 8 + group, PLACES, stride=16), :] = grads[
                    group * PLACES : (group + 1) * PLACES, tile * 128 : (tile + 1) * 128
                ]
    for tile in range(2):
        ret_ref[:, 16:32, tile * 128 : (tile + 1) * 128] = (
            spread[tile].reshape(64, 16, 128).astype(jnp.bfloat16)
        )

    for q in range(3):
        regroup(
            lax.dot_general(
                normed_ref[...],
                proj_ref[:, q * channels : (q + 1) * channels],
                CONTRACT,
                preferred_element_type=jnp.float32,
            ),
            flat,
            place,
            q * 4,
        )
    regroup(
        lax.dot_general(
            context_ref[...], cot_ref[...], CONTRACT, preferred_element_type=jnp.float32
        ),
        flat,
        place,
        12,
    )
    for tile in range(4):
        parts_ref[:, :, tile * 128 : (tile + 1) * 128] = (
            place[tile].reshape(128, 16, 128).astype(jnp.bfloat16)
        )


def attention(blocks, w_qkv, w_out, bias):
    channels = w_out.shape[0]
    tokens = GROUPS * PLACES
    shapes = (
        jax.ShapeDtypeStruct(blocks.shape, jnp.bfloat16),
        jax.ShapeDtypeStruct((128, 16, channels), jnp.bfloat16),
        jax.ShapeDtypeStruct(bias.shape, jnp.float32),
    )
    return pl.pallas_call(
        attention_kernel,
        out_shape=shapes,
        in_specs=[pl.BlockSpec(memory_space=pltpu.VMEM)] * 4,
        out_specs=[pl.BlockSpec(memory_space=pltpu.VMEM)] * 3,
        scratch_shapes=[
            pltpu.VMEM((2, 1024, 128), jnp.float32),
            pltpu.VMEM((tokens, 3 * channels), jnp.bfloat16),
            pltpu.VMEM((tokens, channels), jnp.bfloat16),
            pltpu.VMEM((tokens, channels), jnp.bfloat16),
            pltpu.VMEM((tokens, 3 * channels), jnp.bfloat16),
            pltpu.VMEM((tokens, channels), jnp.bfloat16),
            pltpu.VMEM((tokens, channels), jnp.bfloat16),
            pltpu.VMEM((4, tokens, 128), jnp.float32),
            pltpu.VMEM((4, 2048, 128), jnp.float32),
        ],
        compiler_params=pltpu.CompilerParams(vmem_limit_bytes=40 * 1024 * 1024),
    )(blocks, w_qkv, w_out, bias)


def on_device(
    inputs, out_grad, w_expand, dw_kernel, se_reduce, se_expand, w_project, w_qkv, w_out, pos_table
):
    images, tile_rows, tile_cols, channels = inputs.shape
    hidden_units = w_expand.shape[1]
    heads = pos_table.shape[0]
    places = GRID * GRID
    full_rows = tile_rows * lax.axis_size("row")
    full_cols = tile_cols * lax.axis_size("col")
    cells = full_rows * full_cols
    factor = (images * cells) ** (-0.5)
    tokens = images * tile_rows * tile_cols
    onehot = offset_table(GRID)
    bias = (
        jnp.dot(pos_table, onehot, precision=HIGHEST)
        .reshape(heads // QUAD, QUAD, places, places)
        .transpose(0, 2, 1, 3)
        .reshape(heads // QUAD, places, QUAD * places)
    )
    flat_inputs = inputs.reshape(tokens, channels)
    flattened_cotangent = out_grad.reshape(tokens, channels)
    taps = dw_kernel.reshape(9, hidden_units)
    mixed, slope_mix, slope_expand, main, side, pooled = expand_and_mix(
        flat_inputs, halo(inputs[0], 5), w_expand, taps
    )
    pooled = small_sum(pooled.reshape(-1, 128), 3).reshape(images, -1) / cells
    squeeze_pre = jnp.dot(pooled, se_reduce, precision=HIGHEST)
    squeeze_sig = jax.nn.sigmoid(squeeze_pre)
    squeezed = squeeze_pre * squeeze_sig
    gate = jax.nn.sigmoid(jnp.dot(squeezed, se_expand, precision=HIGHEST))
    scaled, middle_activation, outgoing = project(
        mixed, gate, flat_inputs, flattened_cotangent, w_project
    )
    returned, attention_parts, scores_sum = attention(swap(outgoing, 1), w_qkv, w_out, bias)
    table_part = lax.dot_general(
        scores_sum.reshape(heads // QUAD, places, QUAD, places)
        .transpose(0, 2, 1, 3)
        .reshape(heads, places * places),
        onehot,
        BACKWARD,
        precision=HIGHEST,
    )
    block_out, middle_gradient, middle_b, scaled_grad, gate_grad = middle_backward(
        swap(returned, 2), middle_activation, flattened_cotangent, mixed, w_out, w_project
    )
    gate_grad = small_sum(gate_grad, 4).reshape(images, -1)
    project_parts = (
        lax.dot_general(scaled, middle_b, CONTRACT, preferred_element_type=jnp.float32)
        .astype(jnp.bfloat16)
        .reshape(128, 16, channels)
    )
    excite_grad = gate_grad * gate * (1.0 - gate)
    squeezed_grad = lax.dot_general(excite_grad, se_expand, BACKWARD, precision=HIGHEST)
    squeeze_grad = squeezed_grad * squeeze_sig * (1.0 + squeeze_pre * (1.0 - squeeze_sig))
    pooled_grad = lax.dot_general(squeeze_grad, se_reduce, BACKWARD, precision=HIGHEST)
    se_reduce_grad = lax.dot_general(pooled, squeeze_grad, CONTRACT, precision=HIGHEST) * factor
    se_expand_grad = lax.dot_general(squeezed, excite_grad, CONTRACT, precision=HIGHEST) * factor
    premix_grad = ((scaled_grad * gate + pooled_grad / cells) * slope_mix).astype(jnp.bfloat16)
    input_gradient, expand_parts, kernel_part = mix_backward(
        premix_grad,
        halo(premix_grad.reshape(tile_rows, tile_cols, hidden_units), 6),
        main,
        side,
        slope_expand,
        w_expand,
        taps,
        flat_inputs,
        middle_gradient,
    )
    small = jnp.concatenate([kernel_part.reshape(-1), table_part.reshape(-1)])
    unit = lax.axis_size("row") * 1024
    room = -small.shape[0] % unit
    small = jnp.pad(small, (0, room)).reshape(lax.axis_size("row"), -1, 128)
    parts = jnp.concatenate([project_parts, expand_parts, attention_parts], axis=1)
    summed, small = reduce_all(parts.reshape(64, 2, 48, channels), small, 7)
    summed = summed * factor
    project_grad = summed[:16]

    def from_blocks(blocks):
        return blocks.reshape(-1, 4, channels).transpose(1, 0, 2).reshape(4, -1)

    expand_grad = from_blocks(summed[16:32])
    qkv_grad = from_blocks(summed[32:44])
    out_proj_grad = summed[44:48]
    small = small.reshape(-1)
    kernel_size = kernel_part.size
    kernel_sum = small[:kernel_size].reshape(dw_kernel.shape)
    table_sum = small[kernel_size : kernel_size + table_part.size].reshape(table_part.shape)
    return (
        block_out.reshape(images, tile_rows, tile_cols, channels),
        input_gradient.reshape(images, tile_rows, tile_cols, channels),
        expand_grad,
        project_grad,
        qkv_grad,
        out_proj_grad,
        kernel_sum * factor,
        se_reduce_grad,
        se_expand_grad,
        table_sum * factor,
    )


def solution(mesh):
    placed = (
        P(None, "row", "col", None),
        P(None, "row", "col", None),
        P(),
        P(),
        P(),
        P(),
        P(),
        P(),
        P(),
        P(),
    )
    return jax.shard_map(
        on_device,
        mesh=mesh,
        in_specs=placed,
        out_specs=(
            P(None, "row", "col", None),
            P(None, "row", "col", None),
            P(("row", "col"), None),
            P(("row", "col"), None),
            P(("row", "col"), None),
            P(("row", "col"), None),
            P(),
            P(),
            P(),
            P(),
        ),
        check_vma=False,
    )
```

```python
import functools
import math

import jax
import jax.numpy as jnp
from jax import lax
from jax.experimental import pallas as pl
from jax.experimental.pallas import tpu as pltpu
from jax.sharding import PartitionSpec as P

GRID = 8


EPSILON = 1e-05
GELU_SCALE = math.sqrt(2.0 / math.pi)
HIGHEST = lax.Precision.HIGHEST
MESH = pl.DeviceIdType.MESH
CONTRACT = (((0,), (0,)), ((), ()))
BACKWARD = (((1,), (1,)), ((), ()))


def gelu_slope(values):
    cubic = values * values * values
    bent = jnp.tanh(GELU_SCALE * (values + 0.044715 * cubic))
    result = 0.5 * values * (1.0 + bent)
    slope = 0.5 * (1.0 + bent) + 0.5 * values * (1.0 - bent * bent) * GELU_SCALE * (
        1.0 + 3.0 * 0.044715 * values * values
    )
    return (result, slope)


def layer_normalize(values):
    values = values.astype(jnp.float32)
    centred = values - jnp.mean(values, axis=-1, keepdims=True)
    inverse = lax.rsqrt(jnp.mean(centred * centred, axis=-1, keepdims=True) + EPSILON)
    return (centred * inverse, inverse)


def norm_backward_pass(normal_values, inverse, grads):
    grads = grads.astype(jnp.float32)
    return inverse * (
        grads
        - jnp.mean(grads, axis=-1, keepdims=True)
        - normal_values * jnp.mean(grads * normal_values, axis=-1, keepdims=True)
    )


def offset_table(side):
    places = jnp.arange(side * side, dtype=jnp.int32)
    place_row = places // side
    place_col = places % side
    offset_index = (
        (place_row[None, :] - place_row[:, None] + side - 1) * (2 * side - 1)
        + place_col[None, :]
        - place_col[:, None]
        + side
        - 1
    )
    table_slots = jnp.arange((2 * side - 1) ** 2, dtype=jnp.int32)
    return (table_slots[:, None] == offset_index.reshape(1, -1)).astype(jnp.float32)


AXES = ("row", "col")


def halo_sends(rows, cols, row, col, parts, o_ref, sems):
    top_ref, down_ref, left_ref, right_ref = parts
    width, height = top_ref.shape[0], left_ref.shape[0]
    up, down = lax.rem(row + rows - 1, rows), lax.rem(row + 1, rows)
    left, right = lax.rem(col + cols - 1, cols), lax.rem(col + 1, cols)
    last = width - 16
    sends = (
        (down_ref, 0, width, (down, col)),
        (top_ref, width, width, (up, col)),
        (right_ref, 2 * width, height, (row, right)),
        (left_ref, 2 * width + height, height, (row, left)),
        (down_ref.at[pl.ds(last, 16)], 2 * (width + height), 16, (down, right)),
        (down_ref.at[pl.ds(0, 16)], 2 * (width + height) + 16, 16, (down, left)),
        (top_ref.at[pl.ds(last, 16)], 2 * (width + height) + 32, 16, (up, right)),
        (top_ref.at[pl.ds(0, 16)], 2 * (width + height) + 48, 16, (up, left)),
    )
    copies = [
        pltpu.make_async_remote_copy(
            src_ref=source,
            dst_ref=o_ref.at[pl.ds(start, size)],
            send_sem=sems.at[0, number],
            recv_sem=sems.at[1, number],
            device_id=device,
            device_id_type=MESH,
        )
        for number, (source, start, size, device) in enumerate(sends)
    ]
    return copies, [device for _, _, _, device in sends]


def halo_kernel(rows, cols, top_ref, down_ref, left_ref, right_ref, o_ref, sems):
    row = lax.axis_index("row")
    col = lax.axis_index("col")
    barrier = pltpu.get_barrier_semaphore()
    copies, devices = halo_sends(
        rows, cols, row, col, (top_ref, down_ref, left_ref, right_ref), o_ref, sems
    )
    for device in devices:
        pl.semaphore_signal(barrier, inc=1, device_id=device, device_id_type=MESH)
    pl.semaphore_wait(barrier, len(devices))
    for copy in copies:
        copy.start()
    for copy in copies:
        copy.wait()


def halo(cells, number):
    height, width, features = cells.shape
    rows, cols = lax.axis_size("row"), lax.axis_size("col")
    total = 2 * (width + height) + 64

    def body(*refs):
        halo_kernel(rows, cols, *refs)

    return pl.pallas_call(
        body,
        out_shape=jax.ShapeDtypeStruct((total, features), cells.dtype),
        in_specs=[pl.BlockSpec(memory_space=pltpu.VMEM)] * 4,
        out_specs=pl.BlockSpec(memory_space=pltpu.VMEM),
        scratch_shapes=[pltpu.SemaphoreType.DMA((2, 8))],
        compiler_params=pltpu.CompilerParams(
            collective_id=number, has_side_effects=True, vmem_limit_bytes=60 * 1024 * 1024
        ),
    )(cells[0], cells[-1], cells[:, 0], cells[:, -1])


def reduce_kernel(
    rows, cols, factor, w0_ref, w1_ref, w2_ref, s_ref, project_ref, expand_ref, qkv_ref, out_ref,
    so_ref, half, buf1, buf2, buf3, sum1, sum2, rs_buf, own_buf, col_buf, sems, pair_sems, axis_sems
):
    row = lax.axis_index("row")
    col = lax.axis_index("col")
    core = lax.rem(col, 2)
    me = (row // 4, lax.rem(row, 4), col // 2)
    w_refs = (w0_ref, w1_ref, w2_ref)
    pair = (row, col + 1 - 2 * core)
    barrier = pltpu.get_barrier_semaphore()

    def device(axis, place):
        if axis == 0:
            return (place * 4 + me[1], col)
        if axis == 1:
            return (me[0] * 4 + place, col)
        return (row, place * 2 + core)

    def signal(target):
        pl.semaphore_signal(barrier, inc=1, device_id=target, device_id_type=MESH)

    def wait_like(ref, sem):
        pltpu.make_async_copy(ref, ref, sem).wait()

    def send(source, target, send_sem, recv_sem, to):
        pltpu.make_async_remote_copy(
            src_ref=source,
            dst_ref=target,
            send_sem=send_sem,
            recv_sem=recv_sem,
            device_id=to,
            device_id_type=MESH,
        ).start()

    signal(pair)
    for axis in range(3):
        for k in range(1, 4):
            signal(device(axis, lax.rem(me[axis] + k, 4)))

    @pl.loop(1, rows)
    def _(k):
        signal((lax.rem(row + k, rows), col))

    @pl.loop(1, cols)
    def _(k):
        signal((row, lax.rem(col + k, cols)))

    rs_buf[row] = s_ref[row]
    pl.semaphore_wait(barrier, 10 + rows - 1 + cols - 1)

    for p in range(3):
        send(
            w_refs[p].at[:, :, :, 1 - core], half.at[p], pair_sems.at[0, p], pair_sems.at[1, p], pair
        )

    @pl.loop(1, rows)
    def _(k):
        other = lax.rem(row + k, rows)
        send(s_ref.at[other], rs_buf.at[row], sems.at[0], sems.at[1], (other, col))

    def at_axis(ref, axis, place):
        if axis == 0:
            return ref.at[place]
        if axis == 1:
            return ref.at[:, place]
        return ref.at[:, :, place]

    orders = ((0, 1, 2), (1, 2, 0), (2, 0, 1))
    for p in range(3):
        first = orders[p][0]
        wait_like(half.at[p], pair_sems.at[1, p])
        w_ref = w_refs[p]

        @pl.loop(0, 16)
        def _(i):
            y, x = i // 4, lax.rem(i, 4)
            for z in range(4):
                mine = w_ref[y, x, z, core].astype(jnp.float32) + half[p, y, x, z].astype(jnp.float32)
                half[p, y, x, z] = mine.astype(jnp.bfloat16)

        for k in range(1, 4):
            place = lax.rem(me[first] + k, 4)
            send(
                at_axis(half.at[p], first, place),
                buf1.at[p, me[first]],
                axis_sems.at[0, 0, p],
                axis_sems.at[1, 0, p],
                device(first, place),
            )

    wait_like(rs_buf.at[pl.ds(0, rows - 1)], sems.at[1])
    total = rs_buf[0]
    for k in range(1, rows):
        total = total + rs_buf[k]
    own_buf[...] = total
    col_buf[col] = total

    @pl.loop(1, cols)
    def _(k):
        send(own_buf, col_buf.at[col], sems.at[2], sems.at[3], (row, lax.rem(col + k, cols)))

    for p in range(3):
        first, second, third = orders[p]
        wait_like(buf1.at[p, pl.ds(0, 3)], axis_sems.at[1, 0, p])
        own = at_axis(half.at[p], first, me[first])

        @pl.loop(0, 16)
        def _(i):
            u, v = i // 4, lax.rem(i, 4)
            total = own[u, v].astype(jnp.float32)
            for k in range(1, 4):
                total = total + buf1[p, lax.rem(me[first] + k, 4), u, v].astype(jnp.float32)
            sum1[p, u, v] = total.astype(jnp.bfloat16)

        for k in range(1, 4):
            place = lax.rem(me[second] + k, 4)
            send(
                at_axis(sum1.at[p], 0 if second < third else 1, place),
                buf2.at[p, me[second]],
                axis_sems.at[0, 1, p],
                axis_sems.at[1, 1, p],
                device(second, place),
            )

    wait_like(col_buf.at[pl.ds(0, cols - 1)], sems.at[3])
    total = col_buf[0]
    for k in range(1, cols):
        total = total + col_buf[k]
    so_ref[row] = total

    @pl.loop(1, rows)
    def _(k):
        send(so_ref.at[row], so_ref.at[row], sems.at[4], sems.at[5], (lax.rem(row + k, rows), col))

    for p in range(3):
        first, second, third = orders[p]
        wait_like(buf2.at[p, pl.ds(0, 3)], axis_sems.at[1, 1, p])
        own = at_axis(sum1.at[p], 0 if second < third else 1, me[second])

        @pl.loop(0, 4)
        def _(u):
            total = own[u].astype(jnp.float32)
            for k in range(1, 4):
                total = total + buf2[p, lax.rem(me[second] + k, 4), u].astype(jnp.float32)
            sum2[p, u] = total.astype(jnp.bfloat16)

        for k in range(1, 4):
            place = lax.rem(me[third] + k, 4)
            send(
                sum2.at[p, place],
                buf3.at[p, me[third]],
                axis_sems.at[0, 2, p],
                axis_sems.at[1, 2, p],
                device(third, place),
            )

    for p in range(3):
        third = orders[p][2]
        wait_like(buf3.at[p, pl.ds(0, 3)], axis_sems.at[1, 2, p])
        total = sum2[p, me[third]].astype(jnp.float32)
        for k in range(1, 4):
            total = total + buf3[p, lax.rem(me[third] + k, 4)].astype(jnp.float32)
        total = total * factor
        if p == 0:
            project_ref[...] = total
        elif p == 1:
            for q in range(4):
                expand_ref[:, q * 512 : (q + 1) * 512] = total[q * 4 : (q + 1) * 4]
        else:
            for q in range(3):
                qkv_ref[:, q * 512 : (q + 1) * 512] = total[q * 4 : (q + 1) * 4]
            out_ref[...] = total[12:16]

    wait_like(so_ref.at[pl.ds(0, rows - 1)], sems.at[5])
    wait_like(so_ref.at[pl.ds(0, rows - 1)], sems.at[4])
    wait_like(col_buf.at[pl.ds(0, cols - 1)], sems.at[2])
    wait_like(rs_buf.at[pl.ds(0, rows - 1)], sems.at[0])
    for p in range(3):
        wait_like(half.at[p], pair_sems.at[0, p])
        wait_like(buf1.at[p, pl.ds(0, 3)], axis_sems.at[0, 0, p])
        wait_like(buf2.at[p, pl.ds(0, 3)], axis_sems.at[0, 1, p])
        wait_like(buf3.at[p, pl.ds(0, 3)], axis_sems.at[0, 2, p])


def reduce_all(parts, small, factor, number):
    rows, cols = lax.axis_size("row"), lax.axis_size("col")
    block = small.shape[1:]
    chunk = parts[0].shape[1:]
    vmem = pl.BlockSpec(memory_space=pltpu.VMEM)

    def held(*lead):
        return pltpu.VMEM((3,) + lead + chunk, jnp.bfloat16)

    return pl.pallas_call(
        functools.partial(reduce_kernel, rows, cols, factor),
        out_shape=(
            jax.ShapeDtypeStruct((16, 512), jnp.float32),
            jax.ShapeDtypeStruct((4, 2048), jnp.float32),
            jax.ShapeDtypeStruct((4, 1536), jnp.float32),
            jax.ShapeDtypeStruct((4, 512), jnp.float32),
            jax.ShapeDtypeStruct(small.shape, jnp.float32),
        ),
        in_specs=[vmem] * 4,
        out_specs=[vmem] * 5,
        scratch_shapes=[
            held(4, 4, 4),
            held(4, 4, 4),
            held(4, 4),
            held(4),
            held(4, 4),
            held(4),
            pltpu.VMEM(small.shape, jnp.float32),
            pltpu.VMEM(block, jnp.float32),
            pltpu.VMEM((cols,) + block, jnp.float32),
            pltpu.SemaphoreType.DMA((6,)),
            pltpu.SemaphoreType.DMA((2, 3)),
            pltpu.SemaphoreType.DMA((2, 3, 3)),
        ],
        compiler_params=pltpu.CompilerParams(
            collective_id=number, has_side_effects=True, vmem_limit_bytes=60 * 1024 * 1024
        ),
    )(*(part.reshape((4, 4, 4, 2) + chunk) for part in parts), small)


def sum_halo_kernel(
    rows, cols, x_ref, edge_ref, o_ref, got_ref, row_buf, sum_buf, col_buf, sems, halo_sems
):
    row = lax.axis_index("row")
    col = lax.axis_index("col")
    barrier = pltpu.get_barrier_semaphore()

    parts = [edge_ref.at[pl.ds(low, size)] for low, size in ((0, 32), (32, 32), (64, 16), (80, 16))]
    copies, devices = halo_sends(rows, cols, row, col, parts, got_ref, halo_sems)
    for device in devices:
        pl.semaphore_signal(barrier, inc=1, device_id=device, device_id_type=MESH)

    def row_peer(k):
        return lax.rem(row + k, rows)

    def col_peer(k):
        return lax.rem(col + k, cols)

    @pl.loop(1, rows)
    def _(k):
        pl.semaphore_signal(barrier, inc=1, device_id=(row_peer(k), col), device_id_type=MESH)

    @pl.loop(1, cols)
    def _(k):
        pl.semaphore_signal(barrier, inc=1, device_id=(row, col_peer(k)), device_id_type=MESH)

    row_buf[row] = x_ref[...]
    pl.semaphore_wait(barrier, rows + cols - 2 + len(devices))

    @pl.loop(1, rows)
    def _(k):
        pltpu.make_async_remote_copy(
            src_ref=x_ref,
            dst_ref=row_buf.at[row],
            send_sem=sems.at[0],
            recv_sem=sems.at[1],
            device_id=(row_peer(k), col),
            device_id_type=MESH,
        ).start()

    for copy in copies:
        copy.start()
    arrived = row_buf.at[pl.ds(0, rows - 1)]
    pltpu.make_async_copy(arrived, arrived, sems.at[1]).wait()
    total = row_buf[0]
    for k in range(1, rows):
        total = total + row_buf[k]
    sum_buf[...] = total
    col_buf[col] = total

    @pl.loop(1, cols)
    def _(k):
        pltpu.make_async_remote_copy(
            src_ref=sum_buf,
            dst_ref=col_buf.at[col],
            send_sem=sems.at[2],
            recv_sem=sems.at[3],
            device_id=(row, col_peer(k)),
            device_id_type=MESH,
        ).start()

    other = col_buf.at[pl.ds(0, cols - 1)]
    pltpu.make_async_copy(other, other, sems.at[3]).wait()
    total = col_buf[0]
    for k in range(1, cols):
        total = total + col_buf[k]
    o_ref[...] = total
    pltpu.make_async_copy(arrived, arrived, sems.at[0]).wait()
    pltpu.make_async_copy(other, other, sems.at[2]).wait()
    for copy in copies:
        copy.wait()


def sum_and_halo(values, edges, number):
    rows = lax.axis_size("row")
    cols = lax.axis_size("col")
    shape = values.shape
    vmem = pl.BlockSpec(memory_space=pltpu.VMEM)
    return pl.pallas_call(
        functools.partial(sum_halo_kernel, rows, cols),
        out_shape=(
            jax.ShapeDtypeStruct(shape, jnp.float32),
            jax.ShapeDtypeStruct((edges.shape[0] + 64, edges.shape[1]), edges.dtype),
        ),
        in_specs=[vmem, vmem],
        out_specs=[vmem, vmem],
        scratch_shapes=[
            pltpu.VMEM((rows,) + shape, jnp.float32),
            pltpu.VMEM(shape, jnp.float32),
            pltpu.VMEM((cols,) + shape, jnp.float32),
            pltpu.SemaphoreType.DMA((4,)),
            pltpu.SemaphoreType.DMA((2, 8)),
        ],
        compiler_params=pltpu.CompilerParams(
            collective_id=number, has_side_effects=True, vmem_limit_bytes=60 * 1024 * 1024
        ),
    )(values, edges)


def swap_kernel(parity, side, cols, x_ref, o_ref, sems):
    row = lax.axis_index("row")
    col = lax.axis_index("col")
    kind = lax.rem(row, parity)
    count = side * cols
    me = (row // parity) * cols + col
    barrier = pltpu.get_barrier_semaphore()

    def place(k):
        peer = lax.rem(me + k, count)
        return peer, ((peer // cols) * parity + kind, lax.rem(peer, cols))

    @pl.loop(1, count)
    def _(k):
        pl.semaphore_signal(barrier, inc=1, device_id=place(k)[1], device_id_type=MESH)

    own = pltpu.make_async_copy(x_ref.at[me], o_ref.at[me], sems.at[2])
    own.start()
    pl.semaphore_wait(barrier, count - 1)

    @pl.loop(1, count)
    def _(k):
        peer, device = place(k)
        pltpu.make_async_remote_copy(
            src_ref=x_ref.at[peer],
            dst_ref=o_ref.at[me],
            send_sem=sems.at[0],
            recv_sem=sems.at[1],
            device_id=device,
            device_id_type=MESH,
        ).start()

    own.wait()
    sent = x_ref.at[pl.ds(0, count - 1)]
    pltpu.make_async_copy(sent, sent, sems.at[0]).wait()
    arrived = o_ref.at[pl.ds(0, count - 1)]
    pltpu.make_async_copy(arrived, arrived, sems.at[1]).wait()


def swap(parts, number):
    parity = lax.axis_size("row") // GRID
    return pl.pallas_call(
        functools.partial(swap_kernel, parity, GRID, lax.axis_size("col")),
        out_shape=jax.ShapeDtypeStruct(parts.shape, parts.dtype),
        in_specs=[pl.BlockSpec(memory_space=pltpu.VMEM)],
        out_specs=pl.BlockSpec(memory_space=pltpu.VMEM),
        scratch_shapes=[pltpu.SemaphoreType.DMA((3,))],
        compiler_params=pltpu.CompilerParams(
            collective_id=number, has_side_effects=True, vmem_limit_bytes=60 * 1024 * 1024
        ),
    )(parts)


ROWS = 16
COLS = 32
MAIN = (ROWS + 2) * COLS
SIDE = (ROWS + 2) * 8
EDGE = 2 * (ROWS + COLS)


def edge_masks():
    row, col = lax.axis_index("row"), lax.axis_index("col")
    rows, cols = lax.axis_size("row"), lax.axis_size("col")
    return tuple(
        jnp.where(present, 1.0, 0.0).astype(jnp.float32)
        for present in (row > 0, row < rows - 1, col > 0, col < cols - 1)
    )


def fill_sides(got_ref, side_ref, masks, tiles):
    up, down, left, right = masks
    start = 2 * COLS
    corner = 2 * (COLS + ROWS)
    for tile in range(tiles):
        lanes = slice(tile * 128, (tile + 1) * 128)
        before = got_ref[start : start + ROWS, lanes].astype(jnp.float32)
        after = got_ref[start + ROWS : start + 2 * ROWS, lanes].astype(jnp.float32)
        side_ref[tile, pl.ds(8, ROWS, stride=8), :] = after * right
        side_ref[tile, pl.ds(15, ROWS, stride=8), :] = before * left
        corners = got_ref[corner : corner + 64, lanes].astype(jnp.float32)
        side_ref[tile, 7:8, :] = corners[15:16] * (up * left)
        side_ref[tile, 0:1, :] = corners[16:17] * (up * right)
        side_ref[tile, SIDE - 1 : SIDE, :] = corners[47:48] * (down * left)
        side_ref[tile, SIDE - 8 : SIDE - 7, :] = corners[48:49] * (down * right)


def expand_kernel(
    x_ref, got_ref, w_ref, taps_ref, mixed_ref, slope_mix_ref, slope_ref, main_ref, side_out_ref,
    pooled_ref, edge_ref, normed, normed_side, side, pre, pre_side, padded, ends
):
    step = pl.program_id(0)

    @pl.when(step == 0)
    def _():
        masks = edge_masks()
        side[...] = jnp.zeros_like(side)
        fill_sides(got_ref, side, masks, 4)
        values = jnp.concatenate([side[tile] for tile in range(4)], axis=-1)
        present = jnp.max(jnp.abs(values), axis=-1, keepdims=True) > 0.0
        standard = layer_normalize(values)[0]
        normed_side[...] = jnp.where(present, standard, 0.0).astype(jnp.bfloat16)
        normed[0:COLS, :] = (layer_normalize(got_ref[0:COLS, :])[0] * masks[0]).astype(jnp.bfloat16)
        normed[MAIN - COLS : MAIN, :] = (
            layer_normalize(got_ref[COLS : 2 * COLS, :])[0] * masks[1]
        ).astype(jnp.bfloat16)

        @pl.loop(0, ROWS)
        def _(y):
            rows = pl.ds(pl.multiple_of(y * COLS, COLS), COLS)
            after = pl.ds(pl.multiple_of((y + 1) * COLS, COLS), COLS)
            normed[after, :] = layer_normalize(x_ref[rows, :])[0].astype(jnp.bfloat16)

    width = w_ref.shape[1]
    pre[...] = jnp.dot(normed[...], w_ref[...], preferred_element_type=jnp.float32)
    pre_side[...] = jnp.dot(normed_side[...], w_ref[...], preferred_element_type=jnp.float32)

    @pl.loop(0, ROWS + 2)
    def _(y):
        rows = pl.ds(pl.multiple_of(y * COLS, COLS), COLS)
        result, slope = gelu_slope(pre[rows, :])
        rounded = result.astype(jnp.bfloat16)
        main_ref[rows, :] = rounded
        padded[y, 8 : 8 + COLS, :] = rounded.astype(jnp.float32)

        @pl.when((y > 0) & (y <= ROWS))
        def _():
            before = pl.ds(pl.multiple_of((y - 1) * COLS, COLS), COLS)
            slope_ref[before, :] = slope

        eight = pl.ds(pl.multiple_of(y * 8, 8), 8)
        edge = gelu_slope(pre_side[eight, :])[0].astype(jnp.bfloat16).astype(jnp.float32)
        pre_side[eight, :] = edge
        padded[y, 0:8, :] = edge
        padded[y, 8 + COLS : 16 + COLS, :] = edge

    side_out_ref[...] = pre_side[...].astype(jnp.bfloat16)

    def mix(y, total):
        summed = jnp.zeros((COLS, width), jnp.float32)
        for r in range(3):
            for c in range(3):
                window = padded[y + r, 7 + c : 7 + c + COLS, :]
                summed = summed + window * taps_ref[3 * r + c : 3 * r + c + 1, :]
        mixed, slope = gelu_slope(summed)
        rows = pl.ds(pl.multiple_of(y * COLS, COLS), COLS)
        mixed_ref[rows, :] = mixed
        slope_mix_ref[rows, :] = slope
        ends[0, pl.ds(y, 1), :] = slope[0:1]
        ends[1, pl.ds(y, 1), :] = slope[COLS - 1 : COLS]
        return total + jnp.sum(mixed.reshape(COLS // 8, 8, width), axis=0)

    total = lax.fori_loop(0, ROWS, mix, jnp.zeros((8, width), jnp.float32))
    tokens = ROWS * COLS
    edge_ref[0:COLS, :] = slope_mix_ref[0:COLS, :].astype(jnp.bfloat16)
    edge_ref[COLS : 2 * COLS, :] = slope_mix_ref[tokens - COLS : tokens, :].astype(jnp.bfloat16)
    edge_ref[2 * COLS : 2 * COLS + ROWS, :] = ends[0].astype(jnp.bfloat16)
    edge_ref[2 * COLS + ROWS : EDGE, :] = ends[1].astype(jnp.bfloat16)
    total = jnp.sum(total, axis=0, keepdims=True)
    for tile in range(width // 128):
        pooled_ref[0, tile : tile + 1, :] = total[:, tile * 128 : (tile + 1) * 128]


def expand_and_mix(tokens_in, got, w_expand, taps):
    tokens, channels = tokens_in.shape
    hidden = w_expand.shape[1]
    width = 256
    steps = hidden // width

    def fixed(shape):
        return pl.BlockSpec(shape, lambda e: (0, 0))

    def moving(height):
        return pl.BlockSpec((height, width), lambda e: (0, e))

    wide = jax.ShapeDtypeStruct((tokens, hidden), jnp.float32)
    return pl.pallas_call(
        expand_kernel,
        grid=(steps,),
        out_shape=(
            wide,
            wide,
            wide,
            jax.ShapeDtypeStruct((MAIN, hidden), jnp.bfloat16),
            jax.ShapeDtypeStruct((SIDE, hidden), jnp.bfloat16),
            jax.ShapeDtypeStruct((steps, width // 128, 128), jnp.float32),
            jax.ShapeDtypeStruct((EDGE, hidden), jnp.bfloat16),
        ),
        in_specs=[fixed(tokens_in.shape), fixed(got.shape), moving(channels), moving(9)],
        out_specs=[
            moving(tokens),
            moving(tokens),
            moving(tokens),
            moving(MAIN),
            moving(SIDE),
            pl.BlockSpec((1, width // 128, 128), lambda e: (e, 0, 0)),
            moving(EDGE),
        ],
        scratch_shapes=[
            pltpu.VMEM((MAIN, channels), jnp.bfloat16),
            pltpu.VMEM((SIDE, channels), jnp.bfloat16),
            pltpu.VMEM((4, SIDE, 128), jnp.float32),
            pltpu.VMEM((MAIN, width), jnp.float32),
            pltpu.VMEM((SIDE, width), jnp.float32),
            pltpu.VMEM((ROWS + 2, COLS + 16, width), jnp.float32),
            pltpu.VMEM((2, ROWS, width), jnp.float32),
        ],
        compiler_params=pltpu.CompilerParams(vmem_limit_bytes=60 * 1024 * 1024),
    )(tokens_in, got, w_expand, taps)


def project_kernel(
    mixed_ref, gate_ref, x_ref, cot_ref, w_ref, scaled_ref, middle_ref, out_ref, flat, packed
):
    scaled = (mixed_ref[...] * gate_ref[...]).astype(jnp.bfloat16)
    scaled_ref[...] = scaled
    middle = x_ref[...].astype(jnp.float32) + jnp.dot(
        scaled, w_ref[...], preferred_element_type=jnp.float32
    )
    middle_ref[...] = middle

    def pack(values, first_row):
        for piece in range(4):
            flat[piece] = values[:, piece * 128 : (piece + 1) * 128]
        for piece in range(4):
            half, tile = piece // 2, piece % 2
            for a in range(2):
                for place in range(8):
                    source = a * 64 + (place // 4) * 32 + place % 4
                    packed[tile, pl.ds(a * 128 + half * 8 + place, 8, stride=16), :] = flat[
                        piece, pl.ds(source, 8, stride=4), :
                    ]
        for tile in range(2):
            out_ref[:, first_row : first_row + 16, tile * 128 : (tile + 1) * 128] = (
                packed[tile].reshape(16, 16, 128).astype(jnp.bfloat16)
            )

    pack(layer_normalize(middle)[0], 0)
    pack(cot_ref[...].astype(jnp.float32), 16)


def project(mixed, gate, tokens_in, cotangent, w_project):
    tokens, hidden = mixed.shape
    channels = w_project.shape[1]
    height = 128

    def moving(width):
        return pl.BlockSpec((height, width), lambda t: (t, 0))

    def fixed(shape):
        return pl.BlockSpec(shape, lambda t: (0, 0))

    return pl.pallas_call(
        project_kernel,
        grid=(tokens // height,),
        out_shape=(
            jax.ShapeDtypeStruct((tokens, hidden), jnp.bfloat16),
            jax.ShapeDtypeStruct((tokens, channels), jnp.float32),
            jax.ShapeDtypeStruct((64, 32, channels // 2), jnp.bfloat16),
        ),
        in_specs=[
            moving(hidden),
            fixed((1, hidden)),
            moving(channels),
            moving(channels),
            fixed(w_project.shape),
        ],
        out_specs=[
            moving(hidden),
            moving(channels),
            pl.BlockSpec((16, 32, channels // 2), lambda t: (t, 0, 0)),
        ],
        scratch_shapes=[
            pltpu.VMEM((4, height, 128), jnp.float32),
            pltpu.VMEM((2, 256, 128), jnp.float32),
        ],
        compiler_params=pltpu.CompilerParams(vmem_limit_bytes=60 * 1024 * 1024),
    )(mixed, gate, tokens_in, cotangent, w_project)


def middle_kernel(
    ret_ref, middle_ref, cot_ref, mixed_ref, wout_ref, wproj_ref, out_ref, grad_ref, grad_b_ref,
    scaled_grad_ref, gate_ref, edge_ref, flat, packed, total, ends
):
    step = pl.program_id(0)

    def unpack(first_row):
        for tile in range(2):
            block = ret_ref[:, first_row : first_row + 16, tile * 128 : (tile + 1) * 128]
            packed[tile] = block.astype(jnp.float32).reshape(256, 128)
        for piece in range(4):
            half, tile = piece // 2, piece % 2
            for a in range(2):
                for place in range(8):
                    target = a * 64 + (place // 4) * 32 + place % 4
                    flat[piece, pl.ds(target, 8, stride=4), :] = packed[
                        tile, pl.ds(a * 128 + half * 8 + place, 8, stride=16), :
                    ]
        return jnp.concatenate([flat[piece] for piece in range(4)], axis=-1)

    middle = middle_ref[...]
    context = unpack(0).astype(jnp.bfloat16)
    out_ref[...] = (
        middle + jnp.dot(context, wout_ref[...], preferred_element_type=jnp.float32)
    ).astype(jnp.bfloat16)
    standard, inverse = layer_normalize(middle)
    grad = cot_ref[...].astype(jnp.float32) + norm_backward_pass(standard, inverse, unpack(16))
    grad_ref[...] = grad
    grad_b = grad.astype(jnp.bfloat16)
    grad_b_ref[...] = grad_b
    height = grad.shape[0]
    lines = height // COLS
    for k in range(lines):
        ends[0, pl.ds(step * lines + k, 1), :] = grad[k * COLS : k * COLS + 1]
        ends[1, pl.ds(step * lines + k, 1), :] = grad[(k + 1) * COLS - 1 : (k + 1) * COLS]

    @pl.when(step == 0)
    def _():
        total[...] = jnp.zeros_like(total)
        edge_ref[0:COLS, :] = grad_b[0:COLS]

    hidden = wproj_ref.shape[0]
    for low in range(0, hidden, 512):
        scaled_grad = lax.dot_general(
            grad_b, wproj_ref[low : low + 512, :], BACKWARD, preferred_element_type=jnp.float32
        )
        scaled_grad_ref[:, low : low + 512] = scaled_grad
        terms = scaled_grad * mixed_ref[:, low : low + 512]
        total[:, low : low + 512] += jnp.sum(terms.reshape(-1, 8, 512), axis=0)

    @pl.when(step == pl.num_programs(0) - 1)
    def _():
        edge_ref[COLS : 2 * COLS, :] = grad_b[height - COLS : height]
        edge_ref[2 * COLS : 2 * COLS + ROWS, :] = ends[0].astype(jnp.bfloat16)
        edge_ref[2 * COLS + ROWS : EDGE, :] = ends[1].astype(jnp.bfloat16)
        for tile in range(hidden // 128):
            gate_ref[tile : tile + 1, :] = jnp.sum(
                total[:, tile * 128 : (tile + 1) * 128], axis=0, keepdims=True
            )


def middle_backward(returned, middle, cotangent, mixed, w_out, w_project):
    tokens, hidden = mixed.shape
    channels = middle.shape[1]
    height = 128

    def moving(width):
        return pl.BlockSpec((height, width), lambda t: (t, 0))

    def fixed(shape):
        return pl.BlockSpec(shape, lambda t: (0, 0))

    return pl.pallas_call(
        middle_kernel,
        grid=(tokens // height,),
        out_shape=(
            jax.ShapeDtypeStruct((tokens, channels), jnp.bfloat16),
            jax.ShapeDtypeStruct((tokens, channels), jnp.float32),
            jax.ShapeDtypeStruct((tokens, channels), jnp.bfloat16),
            jax.ShapeDtypeStruct((tokens, hidden), jnp.float32),
            jax.ShapeDtypeStruct((hidden // 128, 128), jnp.float32),
            jax.ShapeDtypeStruct((EDGE, channels), jnp.bfloat16),
        ),
        in_specs=[
            pl.BlockSpec((16, 32, channels // 2), lambda t: (t, 0, 0)),
            moving(channels),
            moving(channels),
            moving(hidden),
            fixed(w_out.shape),
            fixed(w_project.shape),
        ],
        out_specs=[
            moving(channels),
            moving(channels),
            moving(channels),
            moving(hidden),
            fixed((hidden // 128, 128)),
            fixed((EDGE, channels)),
        ],
        scratch_shapes=[
            pltpu.VMEM((4, height, 128), jnp.float32),
            pltpu.VMEM((2, 256, 128), jnp.float32),
            pltpu.VMEM((8, hidden), jnp.float32),
            pltpu.VMEM((2, ROWS, channels), jnp.float32),
        ],
        compiler_params=pltpu.CompilerParams(vmem_limit_bytes=60 * 1024 * 1024),
    )(returned, middle, cotangent, mixed, w_out, w_project)


def regroup(values, flat, place, first):
    for tile in range(4):
        flat[tile] = values[:, tile * 128 : (tile + 1) * 128]
    for tile in range(4):
        for r in range(4):
            place[tile, pl.ds(first + r, 128, stride=16), :] = flat[
                tile, pl.ds(r, 128, stride=4), :
            ]


def back_kernel(
    scaled_grad_ref, slope_mix_ref, slope_got_ref, grad_got_ref, gate_ref, pooled_ref, project_ref,
    main_ref, side_in_ref, slope_ref, w_ref, taps_ref, x_ref, grad_ref,
    out_ref, parts_ref, terms_ref, got_ref, turned, side, padded, expanded, preexp, total, flat, place
):
    step = pl.program_id(0)
    last = pl.num_programs(0) - 1

    @pl.when(step == 0)
    def _():
        side[...] = jnp.zeros_like(side)
        total[...] = jnp.zeros_like(total)
        turned[...] = layer_normalize(x_ref[...])[0].T.astype(jnp.bfloat16)

    def premix(scaled_grad, slope):
        grads = (scaled_grad * gate_ref[...] + pooled_ref[...]) * slope
        return grads.astype(jnp.bfloat16).astype(jnp.float32)

    got_ref[...] = premix(
        lax.dot_general(
            grad_got_ref[...], project_ref[...], BACKWARD, preferred_element_type=jnp.float32
        ),
        slope_got_ref[...].astype(jnp.float32),
    )
    masks = edge_masks()
    fill_sides(got_ref, side, masks, 4)
    padded[0, 8 : 8 + COLS, :] = got_ref[0:COLS, :].astype(jnp.float32) * masks[0]
    padded[ROWS + 1, 8 : 8 + COLS, :] = got_ref[COLS : 2 * COLS, :].astype(jnp.float32) * masks[1]

    @pl.loop(0, ROWS)
    def _(y):
        rows = pl.ds(pl.multiple_of(y * COLS, COLS), COLS)
        padded[y + 1, 8 : 8 + COLS, :] = premix(scaled_grad_ref[rows, :], slope_mix_ref[rows, :])

    pairs = (ROWS + 2) // 2

    @pl.loop(0, ROWS + 2)
    def _(y):
        rows = pl.ds(pl.multiple_of(y * COLS, COLS), COLS)
        expanded[y, 8 : 8 + COLS, :] = main_ref[rows, :].astype(jnp.float32)
        eight = pl.ds(pl.multiple_of(y * 8, 8), 8)
        edge = jnp.concatenate([side[tile, eight, :] for tile in range(4)], axis=-1)
        padded[y, 0:8, :] = edge
        padded[y, 8 + COLS : 16 + COLS, :] = edge

    @pl.loop(0, pairs)
    def _(y):
        both = side_in_ref[pl.ds(pl.multiple_of(y * 16, 16), 16), :].astype(jnp.float32)
        for k in range(2):
            edge = both[8 * k : 8 * k + 8]
            expanded[2 * y + k, 0:8, :] = edge
            expanded[2 * y + k, 8 + COLS : 16 + COLS, :] = edge

    for low in range(0, 512, 256):
        lanes = slice(low, low + 256)

        def unmix(y, sums):
            rows = pl.ds(pl.multiple_of(y * COLS, COLS), COLS)
            own = padded[y + 1, 8 : 8 + COLS, lanes]
            summed = jnp.zeros((COLS, 256), jnp.float32)
            new = []
            for r in range(3):
                for c in range(3):
                    window = padded[y + 2 - r, 9 - c : 9 - c + COLS, lanes]
                    summed = summed + window * taps_ref[3 * r + c : 3 * r + c + 1, lanes]
                    term = own * expanded[y + r, 7 + c : 7 + c + COLS, lanes]
                    new.append(sums[3 * r + c] + jnp.sum(term.reshape(-1, 8, 256), axis=0))
            preexp[rows, lanes] = (summed * slope_ref[rows, lanes]).astype(jnp.bfloat16)
            return tuple(new)

        sums = lax.fori_loop(0, ROWS, unmix, (jnp.zeros((8, 256), jnp.float32),) * 9)
        for k in range(9):
            terms_ref[k : k + 1, lanes] = jnp.sum(sums[k], axis=0, keepdims=True)

    regroup(
        jnp.dot(turned[...], preexp[...], preferred_element_type=jnp.float32), flat, place, step * 4
    )
    total[...] += lax.dot_general(
        preexp[...], w_ref[...], BACKWARD, preferred_element_type=jnp.float32
    )

    @pl.when(step == last)
    def _():
        for tile in range(4):
            parts_ref[:, :, tile * 128 : (tile + 1) * 128] = (
                place[tile].reshape(128, 16, 128).astype(jnp.bfloat16)
            )

        @pl.loop(0, ROWS)
        def _(y):
            rows = pl.ds(pl.multiple_of(y * COLS, COLS), COLS)
            standard, inverse = layer_normalize(x_ref[rows, :])
            out_ref[rows, :] = (
                grad_ref[rows, :] + norm_backward_pass(standard, inverse, total[rows, :])
            ).astype(jnp.bfloat16)


def mix_backward(
    scaled_grad, slope_mix, slope_got, grad_got, gate, pooled_grad, w_project, main, side, slope,
    w_expand, taps, tokens_in, grad
):
    tokens, hidden = scaled_grad.shape
    channels = w_expand.shape[0]
    width = 512

    def fixed(shape):
        return pl.BlockSpec(shape, lambda e: (0,) * len(shape))

    def moving(height):
        return pl.BlockSpec((height, width), lambda e: (0, e))

    return pl.pallas_call(
        back_kernel,
        grid=(hidden // width,),
        out_shape=(
            jax.ShapeDtypeStruct((tokens, channels), jnp.bfloat16),
            jax.ShapeDtypeStruct((128, 16, width), jnp.bfloat16),
            jax.ShapeDtypeStruct((9, hidden), jnp.float32),
        ),
        in_specs=[
            moving(tokens),
            moving(tokens),
            moving(slope_got.shape[0]),
            fixed(grad_got.shape),
            moving(1),
            moving(1),
            pl.BlockSpec((width, channels), lambda e: (e, 0)),
            moving(MAIN),
            moving(SIDE),
            moving(tokens),
            moving(channels),
            moving(9),
            fixed(tokens_in.shape),
            fixed(grad.shape),
        ],
        out_specs=[fixed((tokens, channels)), fixed((128, 16, width)), moving(9)],
        scratch_shapes=[
            pltpu.VMEM(slope_got.shape[:1] + (width,), jnp.float32),
            pltpu.VMEM((channels, tokens), jnp.bfloat16),
            pltpu.VMEM((4, SIDE, 128), jnp.float32),
            pltpu.VMEM((ROWS + 2, COLS + 16, width), jnp.float32),
            pltpu.VMEM((ROWS + 2, COLS + 16, width), jnp.float32),
            pltpu.VMEM((tokens, width), jnp.bfloat16),
            pltpu.VMEM((tokens, channels), jnp.float32),
            pltpu.VMEM((4, tokens, 128), jnp.float32),
            pltpu.VMEM((4, 2048, 128), jnp.float32),
        ],
        compiler_params=pltpu.CompilerParams(vmem_limit_bytes=60 * 1024 * 1024),
    )(
        scaled_grad, slope_mix, slope_got, grad_got, gate, pooled_grad, w_project, main, side, slope,
        w_expand, taps, tokens_in, grad
    )


HEAD_DIM = 32
QUAD = 4
PLACES = 64
GROUPS = 8


def attention_kernel(
    x_ref,
    wqkv_ref,
    wout_ref,
    bias_ref,
    ret_ref,
    parts_ref,
    table_ref,
    spread,
    qkv,
    cgrad,
    normed_ref,
    proj_ref,
    context_ref,
    cot_ref,
    flat,
    place,
):
    channels = wout_ref.shape[0]
    factor = HEAD_DIM ** (-0.5)

    def gather(first_row, out_ref):
        for tile in range(2):
            block = x_ref[:, first_row : first_row + 16, tile * 128 : (tile + 1) * 128]
            spread[tile] = block.astype(jnp.float32).reshape(1024, 128)
        for group in range(GROUPS):
            for piece in range(4):
                half, tile = piece // 2, piece % 2
                rows = spread[tile, pl.ds(half * 8 + group, PLACES, stride=16), :]
                out_ref[group * PLACES : (group + 1) * PLACES, piece * 128 : (piece + 1) * 128] = (
                    rows.astype(jnp.bfloat16)
                )

    gather(0, normed_ref)
    gather(16, cot_ref)

    @pl.loop(0, 3 * channels // 256)
    def _(n):
        cols = pl.ds(pl.multiple_of(n * 256, 256), 256)
        qkv[:, cols] = jnp.dot(
            normed_ref[...], wqkv_ref[:, cols], preferred_element_type=jnp.float32
        ).astype(jnp.bfloat16)

    @pl.loop(0, channels // 256)
    def _(n):
        cols = pl.ds(pl.multiple_of(n * 256, 256), 256)
        cgrad[:, cols] = lax.dot_general(
            cot_ref[...], wout_ref[cols, :], BACKWARD, preferred_element_type=jnp.float32
        ).astype(jnp.bfloat16)

    table_ref[...] = jnp.zeros_like(table_ref)
    lane_head = lax.broadcasted_iota(jnp.int32, (PLACES, 128), 1) // HEAD_DIM
    masks = [(lane_head == h).astype(jnp.float32).astype(jnp.bfloat16) for h in range(QUAD)]
    masks_f = [(lane_head == h).astype(jnp.float32) for h in range(QUAD)]

    def widen(block):
        return jnp.concatenate([block * masks[h] for h in range(QUAD)], axis=0)

    def narrow(full):
        total = full[:PLACES] * masks_f[0]
        for h in range(1, QUAD):
            total = total + full[h * PLACES : (h + 1) * PLACES] * masks_f[h]
        return total

    @pl.loop(0, GROUPS)
    def _(group):
        rows = pl.ds(pl.multiple_of(group * PLACES, PLACES), PLACES)
        for quad in range(4):
            low = quad * 128
            queries = qkv[rows, low : low + 128]
            keys_in = qkv[rows, channels + low : channels + low + 128]
            values_in = qkv[rows, 2 * channels + low : 2 * channels + low + 128]
            grads = cgrad[rows, low : low + 128]
            queries_wide = widen(queries)
            grads_wide = widen(grads)
            scores = (
                lax.dot_general(keys_in, queries_wide, BACKWARD, preferred_element_type=jnp.float32)
                * factor
                + bias_ref[quad]
            )
            scores = jnp.exp(scores - jnp.max(scores, axis=0, keepdims=True))
            weights = scores * (1.0 / jnp.sum(scores, axis=0, keepdims=True))
            weights_b = weights.astype(jnp.bfloat16)
            context = narrow(
                lax.dot_general(weights_b, values_in, CONTRACT, preferred_element_type=jnp.float32)
            )
            context_ref[rows, low : low + 128] = context.astype(jnp.bfloat16)
            weights_grad = lax.dot_general(
                values_in, grads_wide, BACKWARD, preferred_element_type=jnp.float32
            )
            values_grad = jnp.dot(weights_b, grads_wide, preferred_element_type=jnp.float32)
            scores_grad = weights * (
                weights_grad - jnp.sum(weights * weights_grad, axis=0, keepdims=True)
            )
            table_ref[quad] += scores_grad
            scores_b = (scores_grad * factor).astype(jnp.bfloat16)
            queries_grad = narrow(
                lax.dot_general(scores_b, keys_in, CONTRACT, preferred_element_type=jnp.float32)
            )
            keys_grad = jnp.dot(scores_b, queries_wide, preferred_element_type=jnp.float32)
            proj_ref[rows, low : low + 128] = queries_grad.astype(jnp.bfloat16)
            proj_ref[rows, channels + low : channels + low + 128] = keys_grad.astype(jnp.bfloat16)
            proj_ref[rows, 2 * channels + low : 2 * channels + low + 128] = values_grad.astype(
                jnp.bfloat16
            )

    def scatter(read, first_row):
        for group in range(GROUPS):
            for piece in range(4):
                half, tile = piece // 2, piece % 2
                spread[tile, pl.ds(half * 8 + group, PLACES, stride=16), :] = read(group, piece)
        for tile in range(2):
            ret_ref[:, first_row : first_row + 16, tile * 128 : (tile + 1) * 128] = (
                spread[tile].reshape(64, 16, 128).astype(jnp.bfloat16)
            )

    def read_context(group, piece):
        return context_ref[
            group * PLACES : (group + 1) * PLACES, piece * 128 : (piece + 1) * 128
        ].astype(jnp.float32)

    scatter(read_context, 0)

    for n in range(channels // 256):
        grads = lax.dot_general(
            proj_ref[...],
            wqkv_ref[n * 256 : (n + 1) * 256, :],
            BACKWARD,
            preferred_element_type=jnp.float32,
        )
        for group in range(GROUPS):
            for tile in range(2):
                spread[tile, pl.ds(n * 8 + group, PLACES, stride=16), :] = grads[
                    group * PLACES : (group + 1) * PLACES, tile * 128 : (tile + 1) * 128
                ]
    for tile in range(2):
        ret_ref[:, 16:32, tile * 128 : (tile + 1) * 128] = (
            spread[tile].reshape(64, 16, 128).astype(jnp.bfloat16)
        )

    for q in range(3):
        regroup(
            lax.dot_general(
                normed_ref[...],
                proj_ref[:, q * channels : (q + 1) * channels],
                CONTRACT,
                preferred_element_type=jnp.float32,
            ),
            flat,
            place,
            q * 4,
        )
    regroup(
        lax.dot_general(
            context_ref[...], cot_ref[...], CONTRACT, preferred_element_type=jnp.float32
        ),
        flat,
        place,
        12,
    )
    for tile in range(4):
        parts_ref[:, :, tile * 128 : (tile + 1) * 128] = (
            place[tile].reshape(128, 16, 128).astype(jnp.bfloat16)
        )


def attention(blocks, w_qkv, w_out, bias):
    channels = w_out.shape[0]
    tokens = GROUPS * PLACES
    shapes = (
        jax.ShapeDtypeStruct(blocks.shape, jnp.bfloat16),
        jax.ShapeDtypeStruct((128, 16, channels), jnp.bfloat16),
        jax.ShapeDtypeStruct(bias.shape, jnp.float32),
    )
    return pl.pallas_call(
        attention_kernel,
        out_shape=shapes,
        in_specs=[pl.BlockSpec(memory_space=pltpu.VMEM)] * 4,
        out_specs=[pl.BlockSpec(memory_space=pltpu.VMEM)] * 3,
        scratch_shapes=[
            pltpu.VMEM((2, 1024, 128), jnp.float32),
            pltpu.VMEM((tokens, 3 * channels), jnp.bfloat16),
            pltpu.VMEM((tokens, channels), jnp.bfloat16),
            pltpu.VMEM((tokens, channels), jnp.bfloat16),
            pltpu.VMEM((tokens, 3 * channels), jnp.bfloat16),
            pltpu.VMEM((tokens, channels), jnp.bfloat16),
            pltpu.VMEM((tokens, channels), jnp.bfloat16),
            pltpu.VMEM((4, tokens, 128), jnp.float32),
            pltpu.VMEM((4, 2048, 128), jnp.float32),
        ],
        compiler_params=pltpu.CompilerParams(vmem_limit_bytes=60 * 1024 * 1024),
    )(blocks, w_qkv, w_out, bias)


def on_device(
    inputs, out_grad, w_expand, dw_kernel, se_reduce, se_expand, w_project, w_qkv, w_out, pos_table
):
    images, tile_rows, tile_cols, channels = inputs.shape
    hidden_units = w_expand.shape[1]
    heads = pos_table.shape[0]
    places = GRID * GRID
    full_rows = tile_rows * lax.axis_size("row")
    full_cols = tile_cols * lax.axis_size("col")
    cells = full_rows * full_cols
    factor = (images * cells) ** (-0.5)
    tokens = images * tile_rows * tile_cols
    onehot = offset_table(GRID)
    bias = (
        jnp.dot(pos_table, onehot, precision=HIGHEST)
        .reshape(heads // QUAD, QUAD, places, places)
        .transpose(0, 2, 1, 3)
        .reshape(heads // QUAD, places, QUAD * places)
    )
    flat_inputs = inputs.reshape(tokens, channels)
    flattened_cotangent = out_grad.reshape(tokens, channels)
    taps = dw_kernel.reshape(9, hidden_units)
    mixed, slope_mix, slope_expand, main, side, pooled, slope_edges = expand_and_mix(
        flat_inputs, halo(inputs[0], 5), w_expand, taps
    )
    pooled, slope_got = sum_and_halo(pooled.reshape(-1, 128), slope_edges, 3)
    pooled = pooled.reshape(images, -1) / cells
    squeeze_pre = jnp.dot(pooled, se_reduce, precision=HIGHEST)
    squeeze_sig = jax.nn.sigmoid(squeeze_pre)
    squeezed = squeeze_pre * squeeze_sig
    gate = jax.nn.sigmoid(jnp.dot(squeezed, se_expand, precision=HIGHEST))
    scaled, middle_activation, outgoing = project(
        mixed, gate, flat_inputs, flattened_cotangent, w_project
    )
    returned, attention_parts, scores_sum = attention(swap(outgoing, 1), w_qkv, w_out, bias)
    table_part = lax.dot_general(
        scores_sum.reshape(heads // QUAD, places, QUAD, places)
        .transpose(0, 2, 1, 3)
        .reshape(heads, places * places),
        onehot,
        BACKWARD,
        precision=HIGHEST,
    )
    block_out, middle_gradient, middle_b, scaled_grad, gate_grad, grad_edges = middle_backward(
        swap(returned, 2), middle_activation, flattened_cotangent, mixed, w_out, w_project
    )
    gate_grad, grad_got = sum_and_halo(gate_grad, grad_edges, 4)
    gate_grad = gate_grad.reshape(images, -1)
    project_parts = (
        lax.dot_general(scaled, middle_b, CONTRACT, preferred_element_type=jnp.float32)
        .astype(jnp.bfloat16)
        .reshape(128, 16, channels)
    )
    excite_grad = gate_grad * gate * (1.0 - gate)
    squeezed_grad = lax.dot_general(excite_grad, se_expand, BACKWARD, precision=HIGHEST)
    squeeze_grad = squeezed_grad * squeeze_sig * (1.0 + squeeze_pre * (1.0 - squeeze_sig))
    pooled_grad = lax.dot_general(squeeze_grad, se_reduce, BACKWARD, precision=HIGHEST)
    se_reduce_grad = lax.dot_general(pooled, squeeze_grad, CONTRACT, precision=HIGHEST) * factor
    se_expand_grad = lax.dot_general(squeezed, excite_grad, CONTRACT, precision=HIGHEST) * factor
    input_gradient, expand_parts, kernel_part = mix_backward(
        scaled_grad,
        slope_mix,
        slope_got,
        grad_got,
        gate,
        pooled_grad / cells,
        w_project,
        main,
        side,
        slope_expand,
        w_expand,
        taps,
        flat_inputs,
        middle_gradient,
    )
    small = jnp.concatenate([kernel_part.reshape(-1), table_part.reshape(-1)])
    unit = lax.axis_size("row") * 1024
    room = -small.shape[0] % unit
    small = jnp.pad(small, (0, room)).reshape(lax.axis_size("row"), -1, 128)
    project_grad, expand_grad, qkv_grad, out_proj_grad, small = reduce_all(
        (project_parts, expand_parts, attention_parts), small, factor, 7
    )
    small = small.reshape(-1)
    kernel_size = kernel_part.size
    kernel_sum = small[:kernel_size].reshape(dw_kernel.shape)
    table_sum = small[kernel_size : kernel_size + table_part.size].reshape(table_part.shape)
    return (
        block_out.reshape(images, tile_rows, tile_cols, channels),
        input_gradient.reshape(images, tile_rows, tile_cols, channels),
        expand_grad,
        project_grad,
        qkv_grad,
        out_proj_grad,
        kernel_sum * factor,
        se_reduce_grad,
        se_expand_grad,
        table_sum * factor,
    )


def solution(mesh):
    placed = (
        P(None, "row", "col", None),
        P(None, "row", "col", None),
        P(),
        P(),
        P(),
        P(),
        P(),
        P(),
        P(),
        P(),
    )
    return jax.shard_map(
        on_device,
        mesh=mesh,
        in_specs=placed,
        out_specs=(
            P(None, "row", "col", None),
            P(None, "row", "col", None),
            P(("row", "col"), None),
            P(("row", "col"), None),
            P(("row", "col"), None),
            P(("row", "col"), None),
            P(),
            P(),
            P(),
            P(),
        ),
        check_vma=False,
    )
```

```python
import functools
import math

import jax
import jax.numpy as jnp
from jax import lax
from jax.experimental import pallas as pl
from jax.experimental.pallas import tpu as pltpu
from jax.sharding import PartitionSpec as P

GRID = 8


EPSILON = 1e-05
GELU_SCALE = math.sqrt(2.0 / math.pi)
HIGHEST = lax.Precision.HIGHEST
MESH = pl.DeviceIdType.MESH
CONTRACT = (((0,), (0,)), ((), ()))
BACKWARD = (((1,), (1,)), ((), ()))


def gelu_slope(values):
    cubic = values * values * values
    bent = jnp.tanh(GELU_SCALE * (values + 0.044715 * cubic))
    result = 0.5 * values * (1.0 + bent)
    slope = 0.5 * (1.0 + bent) + 0.5 * values * (1.0 - bent * bent) * GELU_SCALE * (
        1.0 + 3.0 * 0.044715 * values * values
    )
    return (result, slope)


def layer_normalize(values):
    values = values.astype(jnp.float32)
    centred = values - jnp.mean(values, axis=-1, keepdims=True)
    inverse = lax.rsqrt(jnp.mean(centred * centred, axis=-1, keepdims=True) + EPSILON)
    return (centred * inverse, inverse)


def norm_backward_pass(normal_values, inverse, grads):
    grads = grads.astype(jnp.float32)
    return inverse * (
        grads
        - jnp.mean(grads, axis=-1, keepdims=True)
        - normal_values * jnp.mean(grads * normal_values, axis=-1, keepdims=True)
    )


def offset_table(side):
    places = jnp.arange(side * side, dtype=jnp.int32)
    place_row = places // side
    place_col = places % side
    offset_index = (
        (place_row[None, :] - place_row[:, None] + side - 1) * (2 * side - 1)
        + place_col[None, :]
        - place_col[:, None]
        + side
        - 1
    )
    table_slots = jnp.arange((2 * side - 1) ** 2, dtype=jnp.int32)
    return (table_slots[:, None] == offset_index.reshape(1, -1)).astype(jnp.float32)


AXES = ("row", "col")


def halo_sends(rows, cols, row, col, parts, o_ref, sems):
    top_ref, down_ref, left_ref, right_ref = parts
    width, height = top_ref.shape[0], left_ref.shape[0]
    up, down = lax.rem(row + rows - 1, rows), lax.rem(row + 1, rows)
    left, right = lax.rem(col + cols - 1, cols), lax.rem(col + 1, cols)
    last = width - 16
    sends = (
        (down_ref, 0, width, (down, col)),
        (top_ref, width, width, (up, col)),
        (right_ref, 2 * width, height, (row, right)),
        (left_ref, 2 * width + height, height, (row, left)),
        (down_ref.at[pl.ds(last, 16)], 2 * (width + height), 16, (down, right)),
        (down_ref.at[pl.ds(0, 16)], 2 * (width + height) + 16, 16, (down, left)),
        (top_ref.at[pl.ds(last, 16)], 2 * (width + height) + 32, 16, (up, right)),
        (top_ref.at[pl.ds(0, 16)], 2 * (width + height) + 48, 16, (up, left)),
    )
    copies = [
        pltpu.make_async_remote_copy(
            src_ref=source,
            dst_ref=o_ref.at[pl.ds(start, size)],
            send_sem=sems.at[0, number],
            recv_sem=sems.at[1, number],
            device_id=device,
            device_id_type=MESH,
        )
        for number, (source, start, size, device) in enumerate(sends)
    ]
    return copies, [device for _, _, _, device in sends]


def halo_kernel(rows, cols, top_ref, down_ref, left_ref, right_ref, o_ref, sems):
    row = lax.axis_index("row")
    col = lax.axis_index("col")
    barrier = pltpu.get_barrier_semaphore()
    copies, devices = halo_sends(
        rows, cols, row, col, (top_ref, down_ref, left_ref, right_ref), o_ref, sems
    )
    for device in devices:
        pl.semaphore_signal(barrier, inc=1, device_id=device, device_id_type=MESH)
    pl.semaphore_wait(barrier, len(devices))
    for copy in copies:
        copy.start()
    for copy in copies:
        copy.wait()


def halo(cells, number):
    height, width, features = cells.shape
    rows, cols = lax.axis_size("row"), lax.axis_size("col")
    total = 2 * (width + height) + 64

    def body(*refs):
        halo_kernel(rows, cols, *refs)

    return pl.pallas_call(
        body,
        out_shape=jax.ShapeDtypeStruct((total, features), cells.dtype),
        in_specs=[pl.BlockSpec(memory_space=pltpu.VMEM)] * 4,
        out_specs=pl.BlockSpec(memory_space=pltpu.VMEM),
        scratch_shapes=[pltpu.SemaphoreType.DMA((2, 8))],
        compiler_params=pltpu.CompilerParams(
            collective_id=number, has_side_effects=True, vmem_limit_bytes=60 * 1024 * 1024
        ),
    )(cells[0], cells[-1], cells[:, 0], cells[:, -1])


def reduce_kernel(
    rows, cols, factor, w0_ref, w1_ref, w2_ref, s_ref, project_ref, expand_ref, qkv_ref, out_ref,
    so_ref, half, buf1, buf2, buf3, sum1, sum2, rs_buf, own_buf, col_buf, sems, pair_sems, axis_sems
):
    row = lax.axis_index("row")
    col = lax.axis_index("col")
    core = lax.rem(col, 2)
    me = (row // 4, lax.rem(row, 4), col // 2)
    w_refs = (w0_ref, w1_ref, w2_ref)
    pair = (row, col + 1 - 2 * core)
    barrier = pltpu.get_barrier_semaphore()

    def device(axis, place):
        if axis == 0:
            return (place * 4 + me[1], col)
        if axis == 1:
            return (me[0] * 4 + place, col)
        return (row, place * 2 + core)

    def signal(target):
        pl.semaphore_signal(barrier, inc=1, device_id=target, device_id_type=MESH)

    def wait_like(ref, sem):
        pltpu.make_async_copy(ref, ref, sem).wait()

    def send(source, target, send_sem, recv_sem, to):
        pltpu.make_async_remote_copy(
            src_ref=source,
            dst_ref=target,
            send_sem=send_sem,
            recv_sem=recv_sem,
            device_id=to,
            device_id_type=MESH,
        ).start()

    signal(pair)
    for axis in range(3):
        for k in range(1, 4):
            signal(device(axis, lax.rem(me[axis] + k, 4)))

    @pl.loop(1, rows)
    def _(k):
        signal((lax.rem(row + k, rows), col))

    @pl.loop(1, cols)
    def _(k):
        signal((row, lax.rem(col + k, cols)))

    rs_buf[row] = s_ref[row]
    pl.semaphore_wait(barrier, 10 + rows - 1 + cols - 1)

    for p in range(3):
        send(
            w_refs[p].at[:, :, :, 1 - core], half.at[p], pair_sems.at[0, p], pair_sems.at[1, p], pair
        )

    @pl.loop(1, rows)
    def _(k):
        other = lax.rem(row + k, rows)
        send(s_ref.at[other], rs_buf.at[row], sems.at[0], sems.at[1], (other, col))

    def at_axis(ref, axis, place):
        if axis == 0:
            return ref.at[place]
        if axis == 1:
            return ref.at[:, place]
        return ref.at[:, :, place]

    orders = ((0, 1, 2), (1, 2, 0), (2, 0, 1))
    for p in range(3):
        first = orders[p][0]
        wait_like(half.at[p], pair_sems.at[1, p])
        w_ref = w_refs[p]

        @pl.loop(0, 16)
        def _(i):
            y, x = i // 4, lax.rem(i, 4)
            for z in range(4):
                mine = w_ref[y, x, z, core].astype(jnp.float32) + half[p, y, x, z].astype(jnp.float32)
                half[p, y, x, z] = mine.astype(jnp.bfloat16)

        for k in range(1, 4):
            place = lax.rem(me[first] + k, 4)
            send(
                at_axis(half.at[p], first, place),
                buf1.at[p, me[first]],
                axis_sems.at[0, 0, p],
                axis_sems.at[1, 0, p],
                device(first, place),
            )

    wait_like(rs_buf.at[pl.ds(0, rows - 1)], sems.at[1])
    total = rs_buf[0]
    for k in range(1, rows):
        total = total + rs_buf[k]
    own_buf[...] = total
    col_buf[col] = total

    @pl.loop(1, cols)
    def _(k):
        send(own_buf, col_buf.at[col], sems.at[2], sems.at[3], (row, lax.rem(col + k, cols)))

    for p in range(3):
        first, second, third = orders[p]
        wait_like(buf1.at[p, pl.ds(0, 3)], axis_sems.at[1, 0, p])
        own = at_axis(half.at[p], first, me[first])

        @pl.loop(0, 16)
        def _(i):
            u, v = i // 4, lax.rem(i, 4)
            total = own[u, v].astype(jnp.float32)
            for k in range(1, 4):
                total = total + buf1[p, lax.rem(me[first] + k, 4), u, v].astype(jnp.float32)
            sum1[p, u, v] = total.astype(jnp.bfloat16)

        for k in range(1, 4):
            place = lax.rem(me[second] + k, 4)
            send(
                at_axis(sum1.at[p], 0 if second < third else 1, place),
                buf2.at[p, me[second]],
                axis_sems.at[0, 1, p],
                axis_sems.at[1, 1, p],
                device(second, place),
            )

    wait_like(col_buf.at[pl.ds(0, cols - 1)], sems.at[3])
    total = col_buf[0]
    for k in range(1, cols):
        total = total + col_buf[k]
    so_ref[row] = total

    @pl.loop(1, rows)
    def _(k):
        send(so_ref.at[row], so_ref.at[row], sems.at[4], sems.at[5], (lax.rem(row + k, rows), col))

    for p in range(3):
        first, second, third = orders[p]
        wait_like(buf2.at[p, pl.ds(0, 3)], axis_sems.at[1, 1, p])
        own = at_axis(sum1.at[p], 0 if second < third else 1, me[second])

        @pl.loop(0, 4)
        def _(u):
            total = own[u].astype(jnp.float32)
            for k in range(1, 4):
                total = total + buf2[p, lax.rem(me[second] + k, 4), u].astype(jnp.float32)
            sum2[p, u] = total.astype(jnp.bfloat16)

        for k in range(1, 4):
            place = lax.rem(me[third] + k, 4)
            send(
                sum2.at[p, place],
                buf3.at[p, me[third]],
                axis_sems.at[0, 2, p],
                axis_sems.at[1, 2, p],
                device(third, place),
            )

    for p in range(3):
        third = orders[p][2]
        wait_like(buf3.at[p, pl.ds(0, 3)], axis_sems.at[1, 2, p])
        total = sum2[p, me[third]].astype(jnp.float32)
        for k in range(1, 4):
            total = total + buf3[p, lax.rem(me[third] + k, 4)].astype(jnp.float32)
        total = total * factor
        if p == 0:
            project_ref[...] = total
        elif p == 1:
            for q in range(4):
                expand_ref[:, q * 512 : (q + 1) * 512] = total[q * 4 : (q + 1) * 4]
        else:
            for q in range(3):
                qkv_ref[:, q * 512 : (q + 1) * 512] = total[q * 4 : (q + 1) * 4]
            out_ref[...] = total[12:16]

    wait_like(so_ref.at[pl.ds(0, rows - 1)], sems.at[5])
    wait_like(so_ref.at[pl.ds(0, rows - 1)], sems.at[4])
    wait_like(col_buf.at[pl.ds(0, cols - 1)], sems.at[2])
    wait_like(rs_buf.at[pl.ds(0, rows - 1)], sems.at[0])
    for p in range(3):
        wait_like(half.at[p], pair_sems.at[0, p])
        wait_like(buf1.at[p, pl.ds(0, 3)], axis_sems.at[0, 0, p])
        wait_like(buf2.at[p, pl.ds(0, 3)], axis_sems.at[0, 1, p])
        wait_like(buf3.at[p, pl.ds(0, 3)], axis_sems.at[0, 2, p])


def reduce_all(parts, small, factor, number):
    rows, cols = lax.axis_size("row"), lax.axis_size("col")
    block = small.shape[1:]
    chunk = parts[0].shape[1:]
    vmem = pl.BlockSpec(memory_space=pltpu.VMEM)

    def held(*lead):
        return pltpu.VMEM((3,) + lead + chunk, jnp.bfloat16)

    return pl.pallas_call(
        functools.partial(reduce_kernel, rows, cols, factor),
        out_shape=(
            jax.ShapeDtypeStruct((16, 512), jnp.float32),
            jax.ShapeDtypeStruct((4, 2048), jnp.float32),
            jax.ShapeDtypeStruct((4, 1536), jnp.float32),
            jax.ShapeDtypeStruct((4, 512), jnp.float32),
            jax.ShapeDtypeStruct(small.shape, jnp.float32),
        ),
        in_specs=[vmem] * 4,
        out_specs=[vmem] * 5,
        scratch_shapes=[
            held(4, 4, 4),
            held(4, 4, 4),
            held(4, 4),
            held(4),
            held(4, 4),
            held(4),
            pltpu.VMEM(small.shape, jnp.float32),
            pltpu.VMEM(block, jnp.float32),
            pltpu.VMEM((cols,) + block, jnp.float32),
            pltpu.SemaphoreType.DMA((6,)),
            pltpu.SemaphoreType.DMA((2, 3)),
            pltpu.SemaphoreType.DMA((2, 3, 3)),
        ],
        compiler_params=pltpu.CompilerParams(
            collective_id=number, has_side_effects=True, vmem_limit_bytes=60 * 1024 * 1024
        ),
    )(*(part.reshape((4, 4, 4, 2) + chunk) for part in parts), small)


def sum_halo_kernel(
    rows, cols, x_ref, edge_ref, o_ref, got_ref, row_buf, sum_buf, col_buf, sems, halo_sems
):
    row = lax.axis_index("row")
    col = lax.axis_index("col")
    barrier = pltpu.get_barrier_semaphore()

    parts = [edge_ref.at[pl.ds(low, size)] for low, size in ((0, 32), (32, 32), (64, 16), (80, 16))]
    copies, devices = halo_sends(rows, cols, row, col, parts, got_ref, halo_sems)
    for device in devices:
        pl.semaphore_signal(barrier, inc=1, device_id=device, device_id_type=MESH)

    def row_peer(k):
        return lax.rem(row + k, rows)

    def col_peer(k):
        return lax.rem(col + k, cols)

    @pl.loop(1, rows)
    def _(k):
        pl.semaphore_signal(barrier, inc=1, device_id=(row_peer(k), col), device_id_type=MESH)

    @pl.loop(1, cols)
    def _(k):
        pl.semaphore_signal(barrier, inc=1, device_id=(row, col_peer(k)), device_id_type=MESH)

    row_buf[row] = x_ref[...]
    pl.semaphore_wait(barrier, rows + cols - 2 + len(devices))

    @pl.loop(1, rows)
    def _(k):
        pltpu.make_async_remote_copy(
            src_ref=x_ref,
            dst_ref=row_buf.at[row],
            send_sem=sems.at[0],
            recv_sem=sems.at[1],
            device_id=(row_peer(k), col),
            device_id_type=MESH,
        ).start()

    for copy in copies:
        copy.start()
    arrived = row_buf.at[pl.ds(0, rows - 1)]
    pltpu.make_async_copy(arrived, arrived, sems.at[1]).wait()
    total = row_buf[0]
    for k in range(1, rows):
        total = total + row_buf[k]
    sum_buf[...] = total
    col_buf[col] = total

    @pl.loop(1, cols)
    def _(k):
        pltpu.make_async_remote_copy(
            src_ref=sum_buf,
            dst_ref=col_buf.at[col],
            send_sem=sems.at[2],
            recv_sem=sems.at[3],
            device_id=(row, col_peer(k)),
            device_id_type=MESH,
        ).start()

    other = col_buf.at[pl.ds(0, cols - 1)]
    pltpu.make_async_copy(other, other, sems.at[3]).wait()
    total = col_buf[0]
    for k in range(1, cols):
        total = total + col_buf[k]
    o_ref[...] = total
    pltpu.make_async_copy(arrived, arrived, sems.at[0]).wait()
    pltpu.make_async_copy(other, other, sems.at[2]).wait()
    for copy in copies:
        copy.wait()


def sum_and_halo(values, edges, number):
    rows = lax.axis_size("row")
    cols = lax.axis_size("col")
    shape = values.shape
    vmem = pl.BlockSpec(memory_space=pltpu.VMEM)
    return pl.pallas_call(
        functools.partial(sum_halo_kernel, rows, cols),
        out_shape=(
            jax.ShapeDtypeStruct(shape, jnp.float32),
            jax.ShapeDtypeStruct((edges.shape[0] + 64, edges.shape[1]), edges.dtype),
        ),
        in_specs=[vmem, vmem],
        out_specs=[vmem, vmem],
        scratch_shapes=[
            pltpu.VMEM((rows,) + shape, jnp.float32),
            pltpu.VMEM(shape, jnp.float32),
            pltpu.VMEM((cols,) + shape, jnp.float32),
            pltpu.SemaphoreType.DMA((4,)),
            pltpu.SemaphoreType.DMA((2, 8)),
        ],
        compiler_params=pltpu.CompilerParams(
            collective_id=number, has_side_effects=True, vmem_limit_bytes=60 * 1024 * 1024
        ),
    )(values, edges)


def swap_kernel(parity, side, cols, x_ref, o_ref, sems):
    row = lax.axis_index("row")
    col = lax.axis_index("col")
    kind = lax.rem(row, parity)
    count = side * cols
    me = (row // parity) * cols + col
    barrier = pltpu.get_barrier_semaphore()

    def place(k):
        peer = lax.rem(me + k, count)
        return peer, ((peer // cols) * parity + kind, lax.rem(peer, cols))

    @pl.loop(1, count)
    def _(k):
        pl.semaphore_signal(barrier, inc=1, device_id=place(k)[1], device_id_type=MESH)

    own = pltpu.make_async_copy(x_ref.at[me], o_ref.at[me], sems.at[2])
    own.start()
    pl.semaphore_wait(barrier, count - 1)

    @pl.loop(1, count)
    def _(k):
        peer, device = place(k)
        pltpu.make_async_remote_copy(
            src_ref=x_ref.at[peer],
            dst_ref=o_ref.at[me],
            send_sem=sems.at[0],
            recv_sem=sems.at[1],
            device_id=device,
            device_id_type=MESH,
        ).start()

    own.wait()
    sent = x_ref.at[pl.ds(0, count - 1)]
    pltpu.make_async_copy(sent, sent, sems.at[0]).wait()
    arrived = o_ref.at[pl.ds(0, count - 1)]
    pltpu.make_async_copy(arrived, arrived, sems.at[1]).wait()


def swap(parts, number):
    parity = lax.axis_size("row") // GRID
    return pl.pallas_call(
        functools.partial(swap_kernel, parity, GRID, lax.axis_size("col")),
        out_shape=jax.ShapeDtypeStruct(parts.shape, parts.dtype),
        in_specs=[pl.BlockSpec(memory_space=pltpu.VMEM)],
        out_specs=pl.BlockSpec(memory_space=pltpu.VMEM),
        scratch_shapes=[pltpu.SemaphoreType.DMA((3,))],
        compiler_params=pltpu.CompilerParams(
            collective_id=number, has_side_effects=True, vmem_limit_bytes=60 * 1024 * 1024
        ),
    )(parts)


ROWS = 16
COLS = 32
MAIN = (ROWS + 2) * COLS
SIDE = (ROWS + 2) * 8
EDGE = 2 * (ROWS + COLS)


def edge_masks():
    row, col = lax.axis_index("row"), lax.axis_index("col")
    rows, cols = lax.axis_size("row"), lax.axis_size("col")
    return tuple(
        jnp.where(present, 1.0, 0.0).astype(jnp.float32)
        for present in (row > 0, row < rows - 1, col > 0, col < cols - 1)
    )


def fill_sides(got_ref, side_ref, masks, tiles):
    up, down, left, right = masks
    start = 2 * COLS
    corner = 2 * (COLS + ROWS)
    for tile in range(tiles):
        lanes = slice(tile * 128, (tile + 1) * 128)
        before = got_ref[start : start + ROWS, lanes].astype(jnp.float32)
        after = got_ref[start + ROWS : start + 2 * ROWS, lanes].astype(jnp.float32)
        side_ref[tile, pl.ds(8, ROWS, stride=8), :] = after * right
        side_ref[tile, pl.ds(15, ROWS, stride=8), :] = before * left
        corners = got_ref[corner : corner + 64, lanes].astype(jnp.float32)
        side_ref[tile, 7:8, :] = corners[15:16] * (up * left)
        side_ref[tile, 0:1, :] = corners[16:17] * (up * right)
        side_ref[tile, SIDE - 1 : SIDE, :] = corners[47:48] * (down * left)
        side_ref[tile, SIDE - 8 : SIDE - 7, :] = corners[48:49] * (down * right)


def expand_kernel(
    x_ref, got_ref, w_ref, taps_ref, mixed_ref, slope_mix_ref, slope_ref, main_ref,
    pooled_ref, edge_ref, normed, normed_side, side, pre, pre_side, padded, ends, slopes, mains, shifted
):
    step = pl.program_id(0)

    @pl.when(step == 0)
    def _():
        masks = edge_masks()
        side[...] = jnp.zeros_like(side)
        fill_sides(got_ref, side, masks, 4)
        values = jnp.concatenate([side[tile] for tile in range(4)], axis=-1)
        present = jnp.max(jnp.abs(values), axis=-1, keepdims=True) > 0.0
        standard = layer_normalize(values)[0]
        normed_side[...] = jnp.where(present, standard, 0.0).astype(jnp.bfloat16)
        normed[0:COLS, :] = (layer_normalize(got_ref[0:COLS, :])[0] * masks[0]).astype(jnp.bfloat16)
        normed[MAIN - COLS : MAIN, :] = (
            layer_normalize(got_ref[COLS : 2 * COLS, :])[0] * masks[1]
        ).astype(jnp.bfloat16)

        @pl.loop(0, ROWS, unroll=2)
        def _(y):
            rows = pl.ds(pl.multiple_of(y * COLS, COLS), COLS)
            after = pl.ds(pl.multiple_of((y + 1) * COLS, COLS), COLS)
            normed[after, :] = layer_normalize(x_ref[rows, :])[0].astype(jnp.bfloat16)

    width = w_ref.shape[1]
    pre[...] = jnp.dot(normed[...], w_ref[...], preferred_element_type=jnp.float32)
    pre_side[...] = jnp.dot(normed_side[...], w_ref[...], preferred_element_type=jnp.float32)

    @pl.loop(0, ROWS + 2, unroll=3)
    def _(y):
        rows = pl.ds(pl.multiple_of(y * COLS, COLS), COLS)
        result, slope = gelu_slope(pre[rows, :])
        rounded = result.astype(jnp.bfloat16)
        mains[rows, :] = rounded
        wide = rounded.astype(jnp.float32)
        padded[y, 8 : 8 + COLS, :] = wide
        shifted[1, y] = wide
        slopes[rows, :] = slope
        eight = pl.ds(pl.multiple_of(y * 8, 8), 8)
        edge = gelu_slope(pre_side[eight, :])[0].astype(jnp.bfloat16).astype(jnp.float32)
        padded[y, 0:8, :] = edge
        padded[y, 8 + COLS : 16 + COLS, :] = edge
        shifted[0, y] = padded[y, 7 : 7 + COLS, :]
        shifted[2, y] = padded[y, 9 : 9 + COLS, :]

    slope_ref[...] = slopes[COLS : MAIN - COLS, :]
    main_ref[...] = mains[COLS : MAIN - COLS, :]

    def mix(y, total):
        summed = jnp.zeros((COLS, width), jnp.float32)
        for r in range(3):
            for c in range(3):
                summed = summed + shifted[c, y + r] * taps_ref[3 * r + c : 3 * r + c + 1, :]
        mixed, slope = gelu_slope(summed)
        rows = pl.ds(pl.multiple_of(y * COLS, COLS), COLS)
        mixed_ref[rows, :] = mixed
        slope_mix_ref[rows, :] = slope
        ends[0, pl.ds(y, 1), :] = slope[0:1]
        ends[1, pl.ds(y, 1), :] = slope[COLS - 1 : COLS]
        return total + jnp.sum(mixed.reshape(COLS // 8, 8, width), axis=0)

    total = lax.fori_loop(0, ROWS, mix, jnp.zeros((8, width), jnp.float32))
    tokens = ROWS * COLS
    edge_ref[0:COLS, :] = slope_mix_ref[0:COLS, :].astype(jnp.bfloat16)
    edge_ref[COLS : 2 * COLS, :] = slope_mix_ref[tokens - COLS : tokens, :].astype(jnp.bfloat16)
    edge_ref[2 * COLS : 2 * COLS + ROWS, :] = ends[0].astype(jnp.bfloat16)
    edge_ref[2 * COLS + ROWS : EDGE, :] = ends[1].astype(jnp.bfloat16)
    total = jnp.sum(total, axis=0, keepdims=True)
    for tile in range(width // 128):
        pooled_ref[0, tile : tile + 1, :] = total[:, tile * 128 : (tile + 1) * 128]


def expand_and_mix(tokens_in, got, w_expand, taps):
    tokens, channels = tokens_in.shape
    hidden = w_expand.shape[1]
    width = 256
    steps = hidden // width

    def fixed(shape):
        return pl.BlockSpec(shape, lambda e: (0, 0))

    def moving(height):
        return pl.BlockSpec((height, width), lambda e: (0, e))

    wide = jax.ShapeDtypeStruct((tokens, hidden), jnp.float32)
    return pl.pallas_call(
        expand_kernel,
        grid=(steps,),
        out_shape=(
            wide,
            wide,
            wide,
            jax.ShapeDtypeStruct((tokens, hidden), jnp.bfloat16),
            jax.ShapeDtypeStruct((steps, width // 128, 128), jnp.float32),
            jax.ShapeDtypeStruct((EDGE, hidden), jnp.bfloat16),
        ),
        in_specs=[fixed(tokens_in.shape), fixed(got.shape), moving(channels), moving(9)],
        out_specs=[
            moving(tokens),
            moving(tokens),
            moving(tokens),
            moving(tokens),
            pl.BlockSpec((1, width // 128, 128), lambda e: (e, 0, 0)),
            moving(EDGE),
        ],
        scratch_shapes=[
            pltpu.VMEM((MAIN, channels), jnp.bfloat16),
            pltpu.VMEM((SIDE, channels), jnp.bfloat16),
            pltpu.VMEM((4, SIDE, 128), jnp.float32),
            pltpu.VMEM((MAIN, width), jnp.float32),
            pltpu.VMEM((SIDE, width), jnp.float32),
            pltpu.VMEM((ROWS + 2, COLS + 16, width), jnp.float32),
            pltpu.VMEM((2, ROWS, width), jnp.float32),
            pltpu.VMEM((MAIN, width), jnp.float32),
            pltpu.VMEM((MAIN, width), jnp.bfloat16),
            pltpu.VMEM((3, ROWS + 2, COLS, width), jnp.float32),
        ],
        compiler_params=pltpu.CompilerParams(vmem_limit_bytes=60 * 1024 * 1024),
    )(tokens_in, got, w_expand, taps)


def project_kernel(
    mixed_ref, gate_ref, x_ref, cot_ref, w_ref, scaled_ref, middle_ref, out_ref, flat, packed
):
    scaled = (mixed_ref[...] * gate_ref[...]).astype(jnp.bfloat16)
    scaled_ref[...] = scaled
    middle = x_ref[...].astype(jnp.float32) + jnp.dot(
        scaled, w_ref[...], preferred_element_type=jnp.float32
    )
    middle_ref[...] = middle

    def pack(values, first_row):
        for piece in range(4):
            flat[piece] = values[:, piece * 128 : (piece + 1) * 128]
        for piece in range(4):
            half, tile = piece // 2, piece % 2
            for a in range(2):
                for place in range(8):
                    source = a * 64 + (place // 4) * 32 + place % 4
                    packed[tile, pl.ds(a * 128 + half * 8 + place, 8, stride=16), :] = flat[
                        piece, pl.ds(source, 8, stride=4), :
                    ]
        for tile in range(2):
            out_ref[:, first_row : first_row + 16, tile * 128 : (tile + 1) * 128] = (
                packed[tile].reshape(16, 16, 128).astype(jnp.bfloat16)
            )

    pack(layer_normalize(middle)[0], 0)
    pack(cot_ref[...].astype(jnp.float32), 16)


def project(mixed, gate, tokens_in, cotangent, w_project):
    tokens, hidden = mixed.shape
    channels = w_project.shape[1]
    height = 128

    def moving(width):
        return pl.BlockSpec((height, width), lambda t: (t, 0))

    def fixed(shape):
        return pl.BlockSpec(shape, lambda t: (0, 0))

    return pl.pallas_call(
        project_kernel,
        grid=(tokens // height,),
        out_shape=(
            jax.ShapeDtypeStruct((tokens, hidden), jnp.bfloat16),
            jax.ShapeDtypeStruct((tokens, channels), jnp.float32),
            jax.ShapeDtypeStruct((64, 32, channels // 2), jnp.bfloat16),
        ),
        in_specs=[
            moving(hidden),
            fixed((1, hidden)),
            moving(channels),
            moving(channels),
            fixed(w_project.shape),
        ],
        out_specs=[
            moving(hidden),
            moving(channels),
            pl.BlockSpec((16, 32, channels // 2), lambda t: (t, 0, 0)),
        ],
        scratch_shapes=[
            pltpu.VMEM((4, height, 128), jnp.float32),
            pltpu.VMEM((2, 256, 128), jnp.float32),
        ],
        compiler_params=pltpu.CompilerParams(vmem_limit_bytes=60 * 1024 * 1024),
    )(mixed, gate, tokens_in, cotangent, w_project)


def middle_kernel(
    ret_ref, middle_ref, cot_ref, mixed_ref, wout_ref, wproj_ref, out_ref, grad_ref, grad_b_ref,
    scaled_grad_ref, gate_ref, edge_ref, flat, packed, total, ends
):
    step = pl.program_id(0)

    def unpack(first_row):
        for tile in range(2):
            block = ret_ref[:, first_row : first_row + 16, tile * 128 : (tile + 1) * 128]
            packed[tile] = block.astype(jnp.float32).reshape(256, 128)
        for piece in range(4):
            half, tile = piece // 2, piece % 2
            for a in range(2):
                for place in range(8):
                    target = a * 64 + (place // 4) * 32 + place % 4
                    flat[piece, pl.ds(target, 8, stride=4), :] = packed[
                        tile, pl.ds(a * 128 + half * 8 + place, 8, stride=16), :
                    ]
        return jnp.concatenate([flat[piece] for piece in range(4)], axis=-1)

    middle = middle_ref[...]
    context = unpack(0).astype(jnp.bfloat16)
    out_ref[...] = (
        middle + jnp.dot(context, wout_ref[...], preferred_element_type=jnp.float32)
    ).astype(jnp.bfloat16)
    standard, inverse = layer_normalize(middle)
    grad = cot_ref[...].astype(jnp.float32) + norm_backward_pass(standard, inverse, unpack(16))
    grad_ref[...] = grad
    grad_b = grad.astype(jnp.bfloat16)
    grad_b_ref[...] = grad_b
    height = grad.shape[0]
    lines = height // COLS
    for k in range(lines):
        ends[0, pl.ds(step * lines + k, 1), :] = grad[k * COLS : k * COLS + 1]
        ends[1, pl.ds(step * lines + k, 1), :] = grad[(k + 1) * COLS - 1 : (k + 1) * COLS]

    @pl.when(step == 0)
    def _():
        total[...] = jnp.zeros_like(total)
        edge_ref[0:COLS, :] = grad_b[0:COLS]

    hidden = wproj_ref.shape[0]
    for low in range(0, hidden, 512):
        scaled_grad = lax.dot_general(
            grad_b, wproj_ref[low : low + 512, :], BACKWARD, preferred_element_type=jnp.float32
        )
        scaled_grad_ref[:, low : low + 512] = scaled_grad
        terms = scaled_grad * mixed_ref[:, low : low + 512]
        total[:, low : low + 512] += jnp.sum(terms.reshape(-1, 8, 512), axis=0)

    @pl.when(step == pl.num_programs(0) - 1)
    def _():
        edge_ref[COLS : 2 * COLS, :] = grad_b[height - COLS : height]
        edge_ref[2 * COLS : 2 * COLS + ROWS, :] = ends[0].astype(jnp.bfloat16)
        edge_ref[2 * COLS + ROWS : EDGE, :] = ends[1].astype(jnp.bfloat16)
        for tile in range(hidden // 128):
            gate_ref[tile : tile + 1, :] = jnp.sum(
                total[:, tile * 128 : (tile + 1) * 128], axis=0, keepdims=True
            )


def middle_backward(returned, middle, cotangent, mixed, w_out, w_project):
    tokens, hidden = mixed.shape
    channels = middle.shape[1]
    height = 128

    def moving(width):
        return pl.BlockSpec((height, width), lambda t: (t, 0))

    def fixed(shape):
        return pl.BlockSpec(shape, lambda t: (0, 0))

    return pl.pallas_call(
        middle_kernel,
        grid=(tokens // height,),
        out_shape=(
            jax.ShapeDtypeStruct((tokens, channels), jnp.bfloat16),
            jax.ShapeDtypeStruct((tokens, channels), jnp.float32),
            jax.ShapeDtypeStruct((tokens, channels), jnp.bfloat16),
            jax.ShapeDtypeStruct((tokens, hidden), jnp.float32),
            jax.ShapeDtypeStruct((hidden // 128, 128), jnp.float32),
            jax.ShapeDtypeStruct((EDGE, channels), jnp.bfloat16),
        ),
        in_specs=[
            pl.BlockSpec((16, 32, channels // 2), lambda t: (t, 0, 0)),
            moving(channels),
            moving(channels),
            moving(hidden),
            fixed(w_out.shape),
            fixed(w_project.shape),
        ],
        out_specs=[
            moving(channels),
            moving(channels),
            moving(channels),
            moving(hidden),
            fixed((hidden // 128, 128)),
            fixed((EDGE, channels)),
        ],
        scratch_shapes=[
            pltpu.VMEM((4, height, 128), jnp.float32),
            pltpu.VMEM((2, 256, 128), jnp.float32),
            pltpu.VMEM((8, hidden), jnp.float32),
            pltpu.VMEM((2, ROWS, channels), jnp.float32),
        ],
        compiler_params=pltpu.CompilerParams(vmem_limit_bytes=60 * 1024 * 1024),
    )(returned, middle, cotangent, mixed, w_out, w_project)


def regroup(values, flat, place, first):
    for tile in range(4):
        flat[tile] = values[:, tile * 128 : (tile + 1) * 128]
    for tile in range(4):
        for r in range(4):
            place[tile, pl.ds(first + r, 128, stride=16), :] = flat[
                tile, pl.ds(r, 128, stride=4), :
            ]


def back_kernel(
    scaled_grad_ref, slope_mix_ref, slope_got_ref, grad_got_ref, gate_ref, pooled_ref, project_ref,
    main_ref, slope_ref, w_ref, taps_ref, x_ref, grad_ref,
    out_ref, parts_ref, terms_ref, got_ref, turned, side, padded, shifted, preexp, total, flat, place
):
    step = pl.program_id(0)
    last = pl.num_programs(0) - 1

    @pl.when(step == 0)
    def _():
        side[...] = jnp.zeros_like(side)
        total[...] = jnp.zeros_like(total)
        turned[...] = layer_normalize(x_ref[...])[0].T.astype(jnp.bfloat16)

    def premix(scaled_grad, slope):
        grads = (scaled_grad * gate_ref[...] + pooled_ref[...]) * slope
        return grads.astype(jnp.bfloat16).astype(jnp.float32)

    got_ref[...] = premix(
        lax.dot_general(
            grad_got_ref[...], project_ref[...], BACKWARD, preferred_element_type=jnp.float32
        ),
        slope_got_ref[...].astype(jnp.float32),
    )
    masks = edge_masks()
    fill_sides(got_ref, side, masks, 4)
    padded[0, 8 : 8 + COLS, :] = got_ref[0:COLS, :] * masks[0]
    padded[ROWS + 1, 8 : 8 + COLS, :] = got_ref[COLS : 2 * COLS, :] * masks[1]

    @pl.loop(0, ROWS, unroll=2)
    def _(y):
        rows = pl.ds(pl.multiple_of(y * COLS, COLS), COLS)
        padded[y + 1, 8 : 8 + COLS, :] = premix(scaled_grad_ref[rows, :], slope_mix_ref[rows, :])

    @pl.loop(0, ROWS + 2, unroll=3)
    def _(y):
        eight = pl.ds(pl.multiple_of(y * 8, 8), 8)
        edge = jnp.concatenate([side[tile, eight, :] for tile in range(4)], axis=-1)
        padded[y, 0:8, :] = edge
        padded[y, 8 + COLS : 16 + COLS, :] = edge
        shifted[0, y] = padded[y, 7 : 7 + COLS, :]
        shifted[1, y] = padded[y, 8 : 8 + COLS, :]
        shifted[2, y] = padded[y, 9 : 9 + COLS, :]

    for low in range(0, 512, 256):
        lanes = slice(low, low + 256)

        def unmix(y, sums):
            rows = pl.ds(pl.multiple_of(y * COLS, COLS), COLS)
            own = main_ref[rows, lanes].astype(jnp.float32)
            summed = jnp.zeros((COLS, 256), jnp.float32)
            new = []
            for r in range(3):
                for c in range(3):
                    window = shifted[2 - c, y + 2 - r, :, lanes]
                    summed = summed + window * taps_ref[3 * r + c : 3 * r + c + 1, lanes]
                    term = own * window
                    new.append(sums[3 * r + c] + jnp.sum(term.reshape(-1, 8, 256), axis=0))
            preexp[rows, lanes] = (summed * slope_ref[rows, lanes]).astype(jnp.bfloat16)
            return tuple(new)

        sums = lax.fori_loop(0, ROWS, unmix, (jnp.zeros((8, 256), jnp.float32),) * 9, unroll=2)
        for k in range(9):
            terms_ref[k : k + 1, lanes] = jnp.sum(sums[k], axis=0, keepdims=True)

    regroup(
        jnp.dot(turned[...], preexp[...], preferred_element_type=jnp.float32), flat, place, step * 4
    )
    total[...] += lax.dot_general(
        preexp[...], w_ref[...], BACKWARD, preferred_element_type=jnp.float32
    )

    @pl.when(step == last)
    def _():
        for tile in range(4):
            parts_ref[:, :, tile * 128 : (tile + 1) * 128] = (
                place[tile].reshape(128, 16, 128).astype(jnp.bfloat16)
            )

        @pl.loop(0, ROWS, unroll=2)
        def _(y):
            rows = pl.ds(pl.multiple_of(y * COLS, COLS), COLS)
            standard, inverse = layer_normalize(x_ref[rows, :])
            out_ref[rows, :] = (
                grad_ref[rows, :] + norm_backward_pass(standard, inverse, total[rows, :])
            ).astype(jnp.bfloat16)


def mix_backward(
    scaled_grad, slope_mix, slope_got, grad_got, gate, pooled_grad, w_project, main, slope,
    w_expand, taps, tokens_in, grad
):
    tokens, hidden = scaled_grad.shape
    channels = w_expand.shape[0]
    width = 512

    def fixed(shape):
        return pl.BlockSpec(shape, lambda e: (0,) * len(shape))

    def moving(height):
        return pl.BlockSpec((height, width), lambda e: (0, e))

    return pl.pallas_call(
        back_kernel,
        grid=(hidden // width,),
        out_shape=(
            jax.ShapeDtypeStruct((tokens, channels), jnp.bfloat16),
            jax.ShapeDtypeStruct((128, 16, width), jnp.bfloat16),
            jax.ShapeDtypeStruct((9, hidden), jnp.float32),
        ),
        in_specs=[
            moving(tokens),
            moving(tokens),
            moving(slope_got.shape[0]),
            fixed(grad_got.shape),
            moving(1),
            moving(1),
            pl.BlockSpec((width, channels), lambda e: (e, 0)),
            moving(tokens),
            moving(tokens),
            moving(channels),
            moving(9),
            fixed(tokens_in.shape),
            fixed(grad.shape),
        ],
        out_specs=[fixed((tokens, channels)), fixed((128, 16, width)), moving(9)],
        scratch_shapes=[
            pltpu.VMEM(slope_got.shape[:1] + (width,), jnp.float32),
            pltpu.VMEM((channels, tokens), jnp.bfloat16),
            pltpu.VMEM((4, SIDE, 128), jnp.float32),
            pltpu.VMEM((ROWS + 2, COLS + 16, width), jnp.float32),
            pltpu.VMEM((3, ROWS + 2, COLS, width), jnp.float32),
            pltpu.VMEM((tokens, width), jnp.bfloat16),
            pltpu.VMEM((tokens, channels), jnp.float32),
            pltpu.VMEM((4, tokens, 128), jnp.float32),
            pltpu.VMEM((4, 2048, 128), jnp.float32),
        ],
        compiler_params=pltpu.CompilerParams(vmem_limit_bytes=60 * 1024 * 1024),
    )(
        scaled_grad, slope_mix, slope_got, grad_got, gate, pooled_grad, w_project, main, slope,
        w_expand, taps, tokens_in, grad
    )


HEAD_DIM = 32
QUAD = 4
PLACES = 64
GROUPS = 8
STAGE = 4


def attention_kernel(
    x_ref,
    wqkv_ref,
    wout_ref,
    bias_ref,
    ret_ref,
    parts_ref,
    table_ref,
    spread,
    qkv,
    cgrad,
    normed_ref,
    proj_ref,
    context_ref,
    cot_ref,
    flat,
    place,
    turned,
):
    channels = wout_ref.shape[0]
    factor = HEAD_DIM ** (-0.5)

    def gather(first_row, out_ref):
        for tile in range(2):
            block = x_ref[:, first_row : first_row + 16, tile * 128 : (tile + 1) * 128]
            spread[tile] = block.astype(jnp.float32).reshape(1024, 128)
        for group in range(GROUPS):
            for piece in range(4):
                half, tile = piece // 2, piece % 2
                rows = spread[tile, pl.ds(half * 8 + group, PLACES, stride=16), :]
                out_ref[group * PLACES : (group + 1) * PLACES, piece * 128 : (piece + 1) * 128] = (
                    rows.astype(jnp.bfloat16)
                )

    gather(0, normed_ref)
    gather(16, cot_ref)

    @pl.loop(0, 3 * channels // 256)
    def _(n):
        cols = pl.ds(pl.multiple_of(n * 256, 256), 256)
        qkv[:, cols] = jnp.dot(
            normed_ref[...], wqkv_ref[:, cols], preferred_element_type=jnp.float32
        ).astype(jnp.bfloat16)

    @pl.loop(0, channels // 256)
    def _(n):
        cols = pl.ds(pl.multiple_of(n * 256, 256), 256)
        cgrad[:, cols] = lax.dot_general(
            cot_ref[...], wout_ref[cols, :], BACKWARD, preferred_element_type=jnp.float32
        ).astype(jnp.bfloat16)

    table_ref[...] = jnp.zeros_like(table_ref)
    lane_head = lax.broadcasted_iota(jnp.int32, (PLACES, 128), 1) // HEAD_DIM
    masks = [(lane_head == h).astype(jnp.float32).astype(jnp.bfloat16) for h in range(QUAD)]
    masks_f = [(lane_head == h).astype(jnp.float32) for h in range(QUAD)]

    def widen(block):
        return jnp.concatenate([block * masks[h] for h in range(QUAD)], axis=0)

    def narrow(full):
        total = full[:PLACES] * masks_f[0]
        for h in range(1, QUAD):
            total = total + full[h * PLACES : (h + 1) * PLACES] * masks_f[h]
        return total

    @pl.loop(0, GROUPS)
    def _(group):
        rows = pl.ds(pl.multiple_of(group * PLACES, PLACES), PLACES)
        for first in range(0, 4, STAGE):
            quads = range(first, first + STAGE)
            lows = [quad * 128 for quad in quads]
            queries = [qkv[rows, low : low + 128] for low in lows]
            keys_in = [qkv[rows, channels + low : channels + low + 128] for low in lows]
            values_in = [qkv[rows, 2 * channels + low : 2 * channels + low + 128] for low in lows]
            grads = [cgrad[rows, low : low + 128] for low in lows]
            queries_wide = [widen(block) for block in queries]
            grads_wide = [widen(block) for block in grads]

            def product(left, right, dims):
                return [
                    lax.dot_general(x, y, dims, preferred_element_type=jnp.float32)
                    for x, y in zip(left, right)
                ]

            plain = (((1,), (0,)), ((), ()))
            scores = product(keys_in, queries_wide, BACKWARD)
            weights_grad = product(values_in, grads_wide, BACKWARD)
            scores = [x * factor + bias_ref[quad] for x, quad in zip(scores, quads)]
            scores = [jnp.exp(x - jnp.max(x, axis=0, keepdims=True)) for x in scores]
            weights = [x * (1.0 / jnp.sum(x, axis=0, keepdims=True)) for x in scores]
            weights_b = [x.astype(jnp.bfloat16) for x in weights]
            context = product(weights_b, values_in, CONTRACT)
            values_grad = product(weights_b, grads_wide, plain)
            scores_grad = [
                x * (y - jnp.sum(x * y, axis=0, keepdims=True))
                for x, y in zip(weights, weights_grad)
            ]
            scores_b = [(x * factor).astype(jnp.bfloat16) for x in scores_grad]
            queries_grad = product(scores_b, keys_in, CONTRACT)
            keys_grad = product(scores_b, queries_wide, plain)
            for k, (quad, low) in enumerate(zip(quads, lows)):
                table_ref[quad] += scores_grad[k]
                context_ref[rows, low : low + 128] = narrow(context[k]).astype(jnp.bfloat16)
                proj_ref[rows, low : low + 128] = narrow(queries_grad[k]).astype(jnp.bfloat16)
                proj_ref[rows, channels + low : channels + low + 128] = keys_grad[k].astype(
                    jnp.bfloat16
                )
                proj_ref[rows, 2 * channels + low : 2 * channels + low + 128] = values_grad[
                    k
                ].astype(jnp.bfloat16)

    def scatter(read, first_row):
        for group in range(GROUPS):
            for piece in range(4):
                half, tile = piece // 2, piece % 2
                spread[tile, pl.ds(half * 8 + group, PLACES, stride=16), :] = read(group, piece)
        for tile in range(2):
            ret_ref[:, first_row : first_row + 16, tile * 128 : (tile + 1) * 128] = (
                spread[tile].reshape(64, 16, 128).astype(jnp.bfloat16)
            )

    def read_context(group, piece):
        return context_ref[
            group * PLACES : (group + 1) * PLACES, piece * 128 : (piece + 1) * 128
        ].astype(jnp.float32)

    scatter(read_context, 0)

    for n in range(channels // 256):
        grads = lax.dot_general(
            proj_ref[...],
            wqkv_ref[n * 256 : (n + 1) * 256, :],
            BACKWARD,
            preferred_element_type=jnp.float32,
        )
        for group in range(GROUPS):
            for tile in range(2):
                spread[tile, pl.ds(n * 8 + group, PLACES, stride=16), :] = grads[
                    group * PLACES : (group + 1) * PLACES, tile * 128 : (tile + 1) * 128
                ]
    for tile in range(2):
        ret_ref[:, 16:32, tile * 128 : (tile + 1) * 128] = (
            spread[tile].reshape(64, 16, 128).astype(jnp.bfloat16)
        )

    turned[...] = normed_ref[...].T
    for q in range(3):
        regroup(
            jnp.dot(
                turned[...],
                proj_ref[:, q * channels : (q + 1) * channels],
                preferred_element_type=jnp.float32,
            ),
            flat,
            place,
            q * 4,
        )
    regroup(
        lax.dot_general(
            context_ref[...], cot_ref[...], CONTRACT, preferred_element_type=jnp.float32
        ),
        flat,
        place,
        12,
    )
    for tile in range(4):
        parts_ref[:, :, tile * 128 : (tile + 1) * 128] = (
            place[tile].reshape(128, 16, 128).astype(jnp.bfloat16)
        )


def attention(blocks, w_qkv, w_out, bias):
    channels = w_out.shape[0]
    tokens = GROUPS * PLACES
    shapes = (
        jax.ShapeDtypeStruct(blocks.shape, jnp.bfloat16),
        jax.ShapeDtypeStruct((128, 16, channels), jnp.bfloat16),
        jax.ShapeDtypeStruct(bias.shape, jnp.float32),
    )
    return pl.pallas_call(
        attention_kernel,
        out_shape=shapes,
        in_specs=[pl.BlockSpec(memory_space=pltpu.VMEM)] * 4,
        out_specs=[pl.BlockSpec(memory_space=pltpu.VMEM)] * 3,
        scratch_shapes=[
            pltpu.VMEM((2, 1024, 128), jnp.float32),
            pltpu.VMEM((tokens, 3 * channels), jnp.bfloat16),
            pltpu.VMEM((tokens, channels), jnp.bfloat16),
            pltpu.VMEM((tokens, channels), jnp.bfloat16),
            pltpu.VMEM((tokens, 3 * channels), jnp.bfloat16),
            pltpu.VMEM((tokens, channels), jnp.bfloat16),
            pltpu.VMEM((tokens, channels), jnp.bfloat16),
            pltpu.VMEM((4, tokens, 128), jnp.float32),
            pltpu.VMEM((4, 2048, 128), jnp.float32),
            pltpu.VMEM((channels, tokens), jnp.bfloat16),
        ],
        compiler_params=pltpu.CompilerParams(vmem_limit_bytes=60 * 1024 * 1024),
    )(blocks, w_qkv, w_out, bias)


def on_device(
    inputs, out_grad, w_expand, dw_kernel, se_reduce, se_expand, w_project, w_qkv, w_out, pos_table
):
    images, tile_rows, tile_cols, channels = inputs.shape
    hidden_units = w_expand.shape[1]
    heads = pos_table.shape[0]
    places = GRID * GRID
    full_rows = tile_rows * lax.axis_size("row")
    full_cols = tile_cols * lax.axis_size("col")
    cells = full_rows * full_cols
    factor = (images * cells) ** (-0.5)
    tokens = images * tile_rows * tile_cols
    onehot = offset_table(GRID)
    bias = (
        jnp.dot(pos_table, onehot, precision=HIGHEST)
        .reshape(heads // QUAD, QUAD, places, places)
        .transpose(0, 2, 1, 3)
        .reshape(heads // QUAD, places, QUAD * places)
    )
    flat_inputs = inputs.reshape(tokens, channels)
    flattened_cotangent = out_grad.reshape(tokens, channels)
    taps = dw_kernel.reshape(9, hidden_units)
    mixed, slope_mix, slope_expand, main, pooled, slope_edges = expand_and_mix(
        flat_inputs, halo(inputs[0], 5), w_expand, taps
    )
    pooled, slope_got = sum_and_halo(pooled.reshape(-1, 128), slope_edges, 3)
    pooled = pooled.reshape(images, -1) / cells
    squeeze_pre = jnp.dot(pooled, se_reduce, precision=HIGHEST)
    squeeze_sig = jax.nn.sigmoid(squeeze_pre)
    squeezed = squeeze_pre * squeeze_sig
    gate = jax.nn.sigmoid(jnp.dot(squeezed, se_expand, precision=HIGHEST))
    scaled, middle_activation, outgoing = project(
        mixed, gate, flat_inputs, flattened_cotangent, w_project
    )
    returned, attention_parts, scores_sum = attention(swap(outgoing, 1), w_qkv, w_out, bias)
    table_part = lax.dot_general(
        scores_sum.reshape(heads // QUAD, places, QUAD, places)
        .transpose(0, 2, 1, 3)
        .reshape(heads, places * places),
        onehot,
        BACKWARD,
        precision=HIGHEST,
    )
    block_out, middle_gradient, middle_b, scaled_grad, gate_grad, grad_edges = middle_backward(
        swap(returned, 2), middle_activation, flattened_cotangent, mixed, w_out, w_project
    )
    gate_grad, grad_got = sum_and_halo(gate_grad, grad_edges, 4)
    gate_grad = gate_grad.reshape(images, -1)
    project_parts = (
        lax.dot_general(scaled, middle_b, CONTRACT, preferred_element_type=jnp.float32)
        .astype(jnp.bfloat16)
        .reshape(128, 16, channels)
    )
    excite_grad = gate_grad * gate * (1.0 - gate)
    squeezed_grad = lax.dot_general(excite_grad, se_expand, BACKWARD, precision=HIGHEST)
    squeeze_grad = squeezed_grad * squeeze_sig * (1.0 + squeeze_pre * (1.0 - squeeze_sig))
    pooled_grad = lax.dot_general(squeeze_grad, se_reduce, BACKWARD, precision=HIGHEST)
    se_reduce_grad = lax.dot_general(pooled, squeeze_grad, CONTRACT, precision=HIGHEST) * factor
    se_expand_grad = lax.dot_general(squeezed, excite_grad, CONTRACT, precision=HIGHEST) * factor
    input_gradient, expand_parts, kernel_part = mix_backward(
        scaled_grad,
        slope_mix,
        slope_got,
        grad_got,
        gate,
        pooled_grad / cells,
        w_project,
        main,
        slope_expand,
        w_expand,
        taps,
        flat_inputs,
        middle_gradient,
    )
    small = jnp.concatenate([kernel_part.reshape(-1), table_part.reshape(-1)])
    unit = lax.axis_size("row") * 1024
    room = -small.shape[0] % unit
    small = jnp.pad(small, (0, room)).reshape(lax.axis_size("row"), -1, 128)
    project_grad, expand_grad, qkv_grad, out_proj_grad, small = reduce_all(
        (project_parts, expand_parts, attention_parts), small, factor, 7
    )
    small = small.reshape(-1)
    kernel_size = kernel_part.size
    kernel_sum = small[:kernel_size].reshape(dw_kernel.shape)
    table_sum = small[kernel_size : kernel_size + table_part.size].reshape(table_part.shape)
    return (
        block_out.reshape(images, tile_rows, tile_cols, channels),
        input_gradient.reshape(images, tile_rows, tile_cols, channels),
        expand_grad,
        project_grad,
        qkv_grad,
        out_proj_grad,
        kernel_sum * factor,
        se_reduce_grad,
        se_expand_grad,
        table_sum * factor,
    )


def solution(mesh):
    placed = (
        P(None, "row", "col", None),
        P(None, "row", "col", None),
        P(),
        P(),
        P(),
        P(),
        P(),
        P(),
        P(),
        P(),
    )
    return jax.shard_map(
        on_device,
        mesh=mesh,
        in_specs=placed,
        out_specs=(
            P(None, "row", "col", None),
            P(None, "row", "col", None),
            P(("row", "col"), None),
            P(("row", "col"), None),
            P(("row", "col"), None),
            P(("row", "col"), None),
            P(),
            P(),
            P(),
            P(),
        ),
        check_vma=False,
    )
```

```python
import functools
import math

import jax
import jax.numpy as jnp
from jax import lax
from jax.experimental import pallas as pl
from jax.experimental.pallas import tpu as pltpu
from jax.sharding import PartitionSpec as P

GRID = 8


EPSILON = 1e-05
GELU_SCALE = math.sqrt(2.0 / math.pi)
HIGHEST = lax.Precision.HIGHEST
MESH = pl.DeviceIdType.MESH
CONTRACT = (((0,), (0,)), ((), ()))
BACKWARD = (((1,), (1,)), ((), ()))


def gelu_slope(values):
    cubic = values * values * values
    bent = jnp.tanh(GELU_SCALE * (values + 0.044715 * cubic))
    result = 0.5 * values * (1.0 + bent)
    slope = 0.5 * (1.0 + bent) + 0.5 * values * (1.0 - bent * bent) * GELU_SCALE * (
        1.0 + 3.0 * 0.044715 * values * values
    )
    return (result, slope)


def layer_normalize(values):
    values = values.astype(jnp.float32)
    centred = values - jnp.mean(values, axis=-1, keepdims=True)
    inverse = lax.rsqrt(jnp.mean(centred * centred, axis=-1, keepdims=True) + EPSILON)
    return (centred * inverse, inverse)


def norm_backward_pass(normal_values, inverse, grads):
    grads = grads.astype(jnp.float32)
    return inverse * (
        grads
        - jnp.mean(grads, axis=-1, keepdims=True)
        - normal_values * jnp.mean(grads * normal_values, axis=-1, keepdims=True)
    )


def offset_table(side):
    places = jnp.arange(side * side, dtype=jnp.int32)
    place_row = places // side
    place_col = places % side
    offset_index = (
        (place_row[None, :] - place_row[:, None] + side - 1) * (2 * side - 1)
        + place_col[None, :]
        - place_col[:, None]
        + side
        - 1
    )
    table_slots = jnp.arange((2 * side - 1) ** 2, dtype=jnp.int32)
    return (table_slots[:, None] == offset_index.reshape(1, -1)).astype(jnp.float32)


AXES = ("row", "col")


def halo_sends(rows, cols, row, col, parts, o_ref, sems):
    top_ref, down_ref, left_ref, right_ref = parts
    width, height = top_ref.shape[0], left_ref.shape[0]
    up, down = lax.rem(row + rows - 1, rows), lax.rem(row + 1, rows)
    left, right = lax.rem(col + cols - 1, cols), lax.rem(col + 1, cols)
    last = width - 16
    sends = (
        (down_ref, 0, width, (down, col)),
        (top_ref, width, width, (up, col)),
        (right_ref, 2 * width, height, (row, right)),
        (left_ref, 2 * width + height, height, (row, left)),
        (down_ref.at[pl.ds(last, 16)], 2 * (width + height), 16, (down, right)),
        (down_ref.at[pl.ds(0, 16)], 2 * (width + height) + 16, 16, (down, left)),
        (top_ref.at[pl.ds(last, 16)], 2 * (width + height) + 32, 16, (up, right)),
        (top_ref.at[pl.ds(0, 16)], 2 * (width + height) + 48, 16, (up, left)),
    )
    copies = [
        pltpu.make_async_remote_copy(
            src_ref=source,
            dst_ref=o_ref.at[pl.ds(start, size)],
            send_sem=sems.at[0, number],
            recv_sem=sems.at[1, number],
            device_id=device,
            device_id_type=MESH,
        )
        for number, (source, start, size, device) in enumerate(sends)
    ]
    return copies, [device for _, _, _, device in sends]


def halo_kernel(rows, cols, top_ref, down_ref, left_ref, right_ref, o_ref, sems):
    row = lax.axis_index("row")
    col = lax.axis_index("col")
    barrier = pltpu.get_barrier_semaphore()
    copies, devices = halo_sends(
        rows, cols, row, col, (top_ref, down_ref, left_ref, right_ref), o_ref, sems
    )
    for device in devices:
        pl.semaphore_signal(barrier, inc=1, device_id=device, device_id_type=MESH)
    pl.semaphore_wait(barrier, len(devices))
    for copy in copies:
        copy.start()
    for copy in copies:
        copy.wait()


def halo(cells, number):
    height, width, features = cells.shape
    rows, cols = lax.axis_size("row"), lax.axis_size("col")
    total = 2 * (width + height) + 64

    def body(*refs):
        halo_kernel(rows, cols, *refs)

    return pl.pallas_call(
        body,
        out_shape=jax.ShapeDtypeStruct((total, features), cells.dtype),
        in_specs=[pl.BlockSpec(memory_space=pltpu.VMEM)] * 4,
        out_specs=pl.BlockSpec(memory_space=pltpu.VMEM),
        scratch_shapes=[pltpu.SemaphoreType.DMA((2, 8))],
        compiler_params=pltpu.CompilerParams(
            collective_id=number, has_side_effects=True, vmem_limit_bytes=60 * 1024 * 1024
        ),
    )(cells[0], cells[-1], cells[:, 0], cells[:, -1])


def reduce_kernel(
    rows, cols, factor, w0_ref, w1_ref, w2_ref, s_ref, project_ref, expand_ref, qkv_ref, out_ref,
    so_ref, mine, half, buf1, buf2, buf3, sum1, sum2, rs_buf, own_buf, col_buf, sems, pair_sems,
    axis_sems
):
    row = lax.axis_index("row")
    col = lax.axis_index("col")
    core = lax.rem(col, 2)
    me = (row // 4, lax.rem(row, 4), col // 2)
    w_refs = (w0_ref, w1_ref, w2_ref)
    pair = (row, col + 1 - 2 * core)
    barrier = pltpu.get_barrier_semaphore()

    def device(axis, place):
        if axis == 0:
            return (place * 4 + me[1], col)
        if axis == 1:
            return (me[0] * 4 + place, col)
        return (row, place * 2 + core)

    def signal(target):
        pl.semaphore_signal(barrier, inc=1, device_id=target, device_id_type=MESH)

    def wait_like(ref, sem):
        pltpu.make_async_copy(ref, ref, sem).wait()

    def send(source, target, send_sem, recv_sem, to):
        pltpu.make_async_remote_copy(
            src_ref=source,
            dst_ref=target,
            send_sem=send_sem,
            recv_sem=recv_sem,
            device_id=to,
            device_id_type=MESH,
        ).start()

    kept = [
        pltpu.make_async_copy(w_refs[p].at[:, :, :, core], mine.at[p], pair_sems.at[2, p])
        for p in range(3)
    ]
    for copy in kept:
        copy.start()
    signal(pair)
    for axis in range(3):
        for k in range(1, 4):
            signal(device(axis, lax.rem(me[axis] + k, 4)))

    @pl.loop(1, rows)
    def _(k):
        signal((lax.rem(row + k, rows), col))

    @pl.loop(1, cols)
    def _(k):
        signal((row, lax.rem(col + k, cols)))

    rs_buf[row] = s_ref[row]
    pl.semaphore_wait(barrier, 10 + rows - 1 + cols - 1)

    for p in range(3):
        send(
            w_refs[p].at[:, :, :, 1 - core], half.at[p], pair_sems.at[0, p], pair_sems.at[1, p], pair
        )

    @pl.loop(1, rows)
    def _(k):
        other = lax.rem(row + k, rows)
        send(s_ref.at[other], rs_buf.at[row], sems.at[0], sems.at[1], (other, col))

    def at_axis(ref, axis, place):
        if axis == 0:
            return ref.at[place]
        if axis == 1:
            return ref.at[:, place]
        return ref.at[:, :, place]

    orders = ((0, 1, 2), (1, 2, 0), (2, 0, 1))
    for p in range(3):
        first = orders[p][0]
        kept[p].wait()
        wait_like(half.at[p], pair_sems.at[1, p])

        @pl.loop(0, 16)
        def _(i):
            y, x = i // 4, lax.rem(i, 4)
            for z in range(4):
                both = mine[p, y, x, z].astype(jnp.float32) + half[p, y, x, z].astype(jnp.float32)
                half[p, y, x, z] = both.astype(jnp.bfloat16)

        for k in range(1, 4):
            place = lax.rem(me[first] + k, 4)
            send(
                at_axis(half.at[p], first, place),
                buf1.at[p, me[first]],
                axis_sems.at[0, 0, p],
                axis_sems.at[1, 0, p],
                device(first, place),
            )

    wait_like(rs_buf.at[pl.ds(0, rows - 1)], sems.at[1])
    total = rs_buf[0]
    for k in range(1, rows):
        total = total + rs_buf[k]
    own_buf[...] = total
    col_buf[col] = total

    @pl.loop(1, cols)
    def _(k):
        send(own_buf, col_buf.at[col], sems.at[2], sems.at[3], (row, lax.rem(col + k, cols)))

    for p in range(3):
        first, second, third = orders[p]
        wait_like(buf1.at[p, pl.ds(0, 3)], axis_sems.at[1, 0, p])
        own = at_axis(half.at[p], first, me[first])

        @pl.loop(0, 16)
        def _(i):
            u, v = i // 4, lax.rem(i, 4)
            total = own[u, v].astype(jnp.float32)
            for k in range(1, 4):
                total = total + buf1[p, lax.rem(me[first] + k, 4), u, v].astype(jnp.float32)
            sum1[p, u, v] = total.astype(jnp.bfloat16)

        for k in range(1, 4):
            place = lax.rem(me[second] + k, 4)
            send(
                at_axis(sum1.at[p], 0 if second < third else 1, place),
                buf2.at[p, me[second]],
                axis_sems.at[0, 1, p],
                axis_sems.at[1, 1, p],
                device(second, place),
            )

    wait_like(col_buf.at[pl.ds(0, cols - 1)], sems.at[3])
    total = col_buf[0]
    for k in range(1, cols):
        total = total + col_buf[k]
    so_ref[row] = total

    @pl.loop(1, rows)
    def _(k):
        send(so_ref.at[row], so_ref.at[row], sems.at[4], sems.at[5], (lax.rem(row + k, rows), col))

    for p in range(3):
        first, second, third = orders[p]
        wait_like(buf2.at[p, pl.ds(0, 3)], axis_sems.at[1, 1, p])
        own = at_axis(sum1.at[p], 0 if second < third else 1, me[second])

        @pl.loop(0, 4)
        def _(u):
            total = own[u].astype(jnp.float32)
            for k in range(1, 4):
                total = total + buf2[p, lax.rem(me[second] + k, 4), u].astype(jnp.float32)
            sum2[p, u] = total.astype(jnp.bfloat16)

        for k in range(1, 4):
            place = lax.rem(me[third] + k, 4)
            send(
                sum2.at[p, place],
                buf3.at[p, me[third]],
                axis_sems.at[0, 2, p],
                axis_sems.at[1, 2, p],
                device(third, place),
            )

    for p in range(3):
        third = orders[p][2]
        wait_like(buf3.at[p, pl.ds(0, 3)], axis_sems.at[1, 2, p])
        total = sum2[p, me[third]].astype(jnp.float32)
        for k in range(1, 4):
            total = total + buf3[p, lax.rem(me[third] + k, 4)].astype(jnp.float32)
        total = total * factor
        if p == 0:
            project_ref[...] = total
        elif p == 1:
            for q in range(4):
                expand_ref[:, q * 512 : (q + 1) * 512] = total[q * 4 : (q + 1) * 4]
        else:
            for q in range(3):
                qkv_ref[:, q * 512 : (q + 1) * 512] = total[q * 4 : (q + 1) * 4]
            out_ref[...] = total[12:16]

    wait_like(so_ref.at[pl.ds(0, rows - 1)], sems.at[5])
    wait_like(so_ref.at[pl.ds(0, rows - 1)], sems.at[4])
    wait_like(col_buf.at[pl.ds(0, cols - 1)], sems.at[2])
    wait_like(rs_buf.at[pl.ds(0, rows - 1)], sems.at[0])
    for p in range(3):
        wait_like(half.at[p], pair_sems.at[0, p])
        wait_like(buf1.at[p, pl.ds(0, 3)], axis_sems.at[0, 0, p])
        wait_like(buf2.at[p, pl.ds(0, 3)], axis_sems.at[0, 1, p])
        wait_like(buf3.at[p, pl.ds(0, 3)], axis_sems.at[0, 2, p])


def reduce_all(parts, small, factor, number):
    rows, cols = lax.axis_size("row"), lax.axis_size("col")
    block = small.shape[1:]
    chunk = parts[0].shape[1:]
    vmem = pl.BlockSpec(memory_space=pltpu.VMEM)

    def held(*lead):
        return pltpu.VMEM((3,) + lead + chunk, jnp.bfloat16)

    return pl.pallas_call(
        functools.partial(reduce_kernel, rows, cols, factor),
        out_shape=(
            jax.ShapeDtypeStruct((16, 512), jnp.float32),
            jax.ShapeDtypeStruct((4, 2048), jnp.float32),
            jax.ShapeDtypeStruct((4, 1536), jnp.float32),
            jax.ShapeDtypeStruct((4, 512), jnp.float32),
            jax.ShapeDtypeStruct(small.shape, jnp.float32),
        ),
        in_specs=[pl.BlockSpec(memory_space=pl.ANY)] * 3 + [vmem],
        out_specs=[vmem] * 5,
        scratch_shapes=[
            held(4, 4, 4),
            held(4, 4, 4),
            held(4, 4, 4),
            held(4, 4),
            held(4),
            held(4, 4),
            held(4),
            pltpu.VMEM(small.shape, jnp.float32),
            pltpu.VMEM(block, jnp.float32),
            pltpu.VMEM((cols,) + block, jnp.float32),
            pltpu.SemaphoreType.DMA((6,)),
            pltpu.SemaphoreType.DMA((3, 3)),
            pltpu.SemaphoreType.DMA((2, 3, 3)),
        ],
        compiler_params=pltpu.CompilerParams(
            collective_id=number, has_side_effects=True, vmem_limit_bytes=60 * 1024 * 1024
        ),
    )(*(part.reshape((4, 4, 4, 2) + chunk) for part in parts), small)


def sum_halo_kernel(
    rows, cols, x_ref, edge_ref, o_ref, got_ref, row_buf, sum_buf, col_buf, sems, halo_sems
):
    row = lax.axis_index("row")
    col = lax.axis_index("col")
    barrier = pltpu.get_barrier_semaphore()

    parts = [edge_ref.at[pl.ds(low, size)] for low, size in ((0, 32), (32, 32), (64, 16), (80, 16))]
    copies, devices = halo_sends(rows, cols, row, col, parts, got_ref, halo_sems)
    for device in devices:
        pl.semaphore_signal(barrier, inc=1, device_id=device, device_id_type=MESH)

    def row_peer(k):
        return lax.rem(row + k, rows)

    def col_peer(k):
        return lax.rem(col + k, cols)

    @pl.loop(1, rows)
    def _(k):
        pl.semaphore_signal(barrier, inc=1, device_id=(row_peer(k), col), device_id_type=MESH)

    @pl.loop(1, cols)
    def _(k):
        pl.semaphore_signal(barrier, inc=1, device_id=(row, col_peer(k)), device_id_type=MESH)

    row_buf[row] = x_ref[...]
    pl.semaphore_wait(barrier, rows + cols - 2 + len(devices))

    @pl.loop(1, rows)
    def _(k):
        pltpu.make_async_remote_copy(
            src_ref=x_ref,
            dst_ref=row_buf.at[row],
            send_sem=sems.at[0],
            recv_sem=sems.at[1],
            device_id=(row_peer(k), col),
            device_id_type=MESH,
        ).start()

    for copy in copies:
        copy.start()
    arrived = row_buf.at[pl.ds(0, rows - 1)]
    pltpu.make_async_copy(arrived, arrived, sems.at[1]).wait()
    total = row_buf[0]
    for k in range(1, rows):
        total = total + row_buf[k]
    sum_buf[...] = total
    col_buf[col] = total

    @pl.loop(1, cols)
    def _(k):
        pltpu.make_async_remote_copy(
            src_ref=sum_buf,
            dst_ref=col_buf.at[col],
            send_sem=sems.at[2],
            recv_sem=sems.at[3],
            device_id=(row, col_peer(k)),
            device_id_type=MESH,
        ).start()

    other = col_buf.at[pl.ds(0, cols - 1)]
    pltpu.make_async_copy(other, other, sems.at[3]).wait()
    total = col_buf[0]
    for k in range(1, cols):
        total = total + col_buf[k]
    o_ref[...] = total
    pltpu.make_async_copy(arrived, arrived, sems.at[0]).wait()
    pltpu.make_async_copy(other, other, sems.at[2]).wait()
    for copy in copies:
        copy.wait()


def sum_and_halo(values, edges, number):
    rows = lax.axis_size("row")
    cols = lax.axis_size("col")
    shape = values.shape
    vmem = pl.BlockSpec(memory_space=pltpu.VMEM)
    return pl.pallas_call(
        functools.partial(sum_halo_kernel, rows, cols),
        out_shape=(
            jax.ShapeDtypeStruct(shape, jnp.float32),
            jax.ShapeDtypeStruct((edges.shape[0] + 64, edges.shape[1]), edges.dtype),
        ),
        in_specs=[vmem, vmem],
        out_specs=[vmem, vmem],
        scratch_shapes=[
            pltpu.VMEM((rows,) + shape, jnp.float32),
            pltpu.VMEM(shape, jnp.float32),
            pltpu.VMEM((cols,) + shape, jnp.float32),
            pltpu.SemaphoreType.DMA((4,)),
            pltpu.SemaphoreType.DMA((2, 8)),
        ],
        compiler_params=pltpu.CompilerParams(
            collective_id=number, has_side_effects=True, vmem_limit_bytes=60 * 1024 * 1024
        ),
    )(values, edges)


def swap_kernel(parity, side, cols, x_ref, o_ref, sems):
    row = lax.axis_index("row")
    col = lax.axis_index("col")
    kind = lax.rem(row, parity)
    count = side * cols
    me = (row // parity) * cols + col
    barrier = pltpu.get_barrier_semaphore()

    def place(k):
        peer = lax.rem(me + k, count)
        return peer, ((peer // cols) * parity + kind, lax.rem(peer, cols))

    @pl.loop(1, count)
    def _(k):
        pl.semaphore_signal(barrier, inc=1, device_id=place(k)[1], device_id_type=MESH)

    own = pltpu.make_async_copy(x_ref.at[me], o_ref.at[me], sems.at[2])
    own.start()
    pl.semaphore_wait(barrier, count - 1)

    @pl.loop(1, count)
    def _(k):
        peer, device = place(k)
        pltpu.make_async_remote_copy(
            src_ref=x_ref.at[peer],
            dst_ref=o_ref.at[me],
            send_sem=sems.at[0],
            recv_sem=sems.at[1],
            device_id=device,
            device_id_type=MESH,
        ).start()

    own.wait()
    sent = x_ref.at[pl.ds(0, count - 1)]
    pltpu.make_async_copy(sent, sent, sems.at[0]).wait()
    arrived = o_ref.at[pl.ds(0, count - 1)]
    pltpu.make_async_copy(arrived, arrived, sems.at[1]).wait()


def swap(parts, number):
    parity = lax.axis_size("row") // GRID
    return pl.pallas_call(
        functools.partial(swap_kernel, parity, GRID, lax.axis_size("col")),
        out_shape=jax.ShapeDtypeStruct(parts.shape, parts.dtype),
        in_specs=[pl.BlockSpec(memory_space=pl.ANY)],
        out_specs=pl.BlockSpec(memory_space=pl.ANY),
        scratch_shapes=[pltpu.SemaphoreType.DMA((3,))],
        compiler_params=pltpu.CompilerParams(
            collective_id=number, has_side_effects=True, vmem_limit_bytes=60 * 1024 * 1024
        ),
    )(parts)


ROWS = 16
COLS = 32
MAIN = (ROWS + 2) * COLS
SIDE = (ROWS + 2) * 8
EDGE = 2 * (ROWS + COLS)


def edge_masks():
    row, col = lax.axis_index("row"), lax.axis_index("col")
    rows, cols = lax.axis_size("row"), lax.axis_size("col")
    return tuple(
        jnp.where(present, 1.0, 0.0).astype(jnp.float32)
        for present in (row > 0, row < rows - 1, col > 0, col < cols - 1)
    )


def fill_sides(got_ref, side_ref, masks, tiles):
    up, down, left, right = masks
    start = 2 * COLS
    corner = 2 * (COLS + ROWS)
    for tile in range(tiles):
        lanes = slice(tile * 128, (tile + 1) * 128)
        before = got_ref[start : start + ROWS, lanes].astype(jnp.float32)
        after = got_ref[start + ROWS : start + 2 * ROWS, lanes].astype(jnp.float32)
        side_ref[tile, pl.ds(8, ROWS, stride=8), :] = after * right
        side_ref[tile, pl.ds(15, ROWS, stride=8), :] = before * left
        corners = got_ref[corner : corner + 64, lanes].astype(jnp.float32)
        side_ref[tile, 7:8, :] = corners[15:16] * (up * left)
        side_ref[tile, 0:1, :] = corners[16:17] * (up * right)
        side_ref[tile, SIDE - 1 : SIDE, :] = corners[47:48] * (down * left)
        side_ref[tile, SIDE - 8 : SIDE - 7, :] = corners[48:49] * (down * right)


def expand_kernel(
    x_ref, got_ref, w_ref, taps_ref, mixed_ref, slope_mix_ref, slope_ref, main_ref,
    pooled_ref, edge_ref, normed, normed_side, side, pre, pre_side, padded, ends, slopes, mains, shifted
):
    step = pl.program_id(0)

    @pl.when(step == 0)
    def _():
        masks = edge_masks()
        side[...] = jnp.zeros_like(side)
        fill_sides(got_ref, side, masks, 4)
        values = jnp.concatenate([side[tile] for tile in range(4)], axis=-1)
        present = jnp.max(jnp.abs(values), axis=-1, keepdims=True) > 0.0
        standard = layer_normalize(values)[0]
        normed_side[...] = jnp.where(present, standard, 0.0).astype(jnp.bfloat16)
        normed[0:COLS, :] = (layer_normalize(got_ref[0:COLS, :])[0] * masks[0]).astype(jnp.bfloat16)
        normed[MAIN - COLS : MAIN, :] = (
            layer_normalize(got_ref[COLS : 2 * COLS, :])[0] * masks[1]
        ).astype(jnp.bfloat16)

        @pl.loop(0, ROWS, unroll=2)
        def _(y):
            rows = pl.ds(pl.multiple_of(y * COLS, COLS), COLS)
            after = pl.ds(pl.multiple_of((y + 1) * COLS, COLS), COLS)
            normed[after, :] = layer_normalize(x_ref[rows, :])[0].astype(jnp.bfloat16)

    width = w_ref.shape[1]
    pre[...] = jnp.dot(normed[...], w_ref[...], preferred_element_type=jnp.float32)
    pre_side[...] = jnp.dot(normed_side[...], w_ref[...], preferred_element_type=jnp.float32)

    @pl.loop(0, ROWS + 2, unroll=6)
    def _(y):
        rows = pl.ds(pl.multiple_of(y * COLS, COLS), COLS)
        result, slope = gelu_slope(pre[rows, :])
        rounded = result.astype(jnp.bfloat16)
        mains[rows, :] = rounded
        wide = rounded.astype(jnp.float32)
        padded[y, 8 : 8 + COLS, :] = wide
        shifted[1, y] = wide
        slopes[rows, :] = slope
        eight = pl.ds(pl.multiple_of(y * 8, 8), 8)
        edge = gelu_slope(pre_side[eight, :])[0].astype(jnp.bfloat16).astype(jnp.float32)
        padded[y, 0:8, :] = edge
        padded[y, 8 + COLS : 16 + COLS, :] = edge
        shifted[0, y] = padded[y, 7 : 7 + COLS, :]
        shifted[2, y] = padded[y, 9 : 9 + COLS, :]

    slope_ref[...] = slopes[COLS : MAIN - COLS, :]
    main_ref[...] = mains[COLS : MAIN - COLS, :]

    def mix(y, total):
        summed = jnp.zeros((COLS, width), jnp.float32)
        for r in range(3):
            for c in range(3):
                summed = summed + shifted[c, y + r] * taps_ref[r, c : c + 1, :]
        mixed, slope = gelu_slope(summed)
        rows = pl.ds(pl.multiple_of(y * COLS, COLS), COLS)
        mixed_ref[rows, :] = mixed
        slope_mix_ref[rows, :] = slope
        ends[0, pl.ds(y, 1), :] = slope[0:1]
        ends[1, pl.ds(y, 1), :] = slope[COLS - 1 : COLS]
        return total + jnp.sum(mixed.reshape(COLS // 8, 8, width), axis=0)

    total = lax.fori_loop(0, ROWS, mix, jnp.zeros((8, width), jnp.float32))
    tokens = ROWS * COLS
    edge_ref[0:COLS, :] = slope_mix_ref[0:COLS, :].astype(jnp.bfloat16)
    edge_ref[COLS : 2 * COLS, :] = slope_mix_ref[tokens - COLS : tokens, :].astype(jnp.bfloat16)
    edge_ref[2 * COLS : 2 * COLS + ROWS, :] = ends[0].astype(jnp.bfloat16)
    edge_ref[2 * COLS + ROWS : EDGE, :] = ends[1].astype(jnp.bfloat16)
    total = jnp.sum(total, axis=0, keepdims=True)
    for tile in range(width // 128):
        pooled_ref[0, tile : tile + 1, :] = total[:, tile * 128 : (tile + 1) * 128]


def expand_and_mix(tokens_in, got, w_expand, taps):
    tokens, channels = tokens_in.shape
    hidden = w_expand.shape[1]
    width = 256
    steps = hidden // width

    def fixed(shape):
        return pl.BlockSpec(shape, lambda e: (0, 0))

    def moving(height):
        return pl.BlockSpec((height, width), lambda e: (0, e))

    taps_spec = pl.BlockSpec((3, 3, width), lambda e: (0, 0, e))
    wide = jax.ShapeDtypeStruct((tokens, hidden), jnp.float32)
    return pl.pallas_call(
        expand_kernel,
        grid=(steps,),
        out_shape=(
            wide,
            wide,
            wide,
            jax.ShapeDtypeStruct((tokens, hidden), jnp.bfloat16),
            jax.ShapeDtypeStruct((steps, width // 128, 128), jnp.float32),
            jax.ShapeDtypeStruct((EDGE, hidden), jnp.bfloat16),
        ),
        in_specs=[fixed(tokens_in.shape), fixed(got.shape), moving(channels), taps_spec],
        out_specs=[
            moving(tokens),
            moving(tokens),
            moving(tokens),
            moving(tokens),
            pl.BlockSpec((1, width // 128, 128), lambda e: (e, 0, 0)),
            moving(EDGE),
        ],
        scratch_shapes=[
            pltpu.VMEM((MAIN, channels), jnp.bfloat16),
            pltpu.VMEM((SIDE, channels), jnp.bfloat16),
            pltpu.VMEM((4, SIDE, 128), jnp.float32),
            pltpu.VMEM((MAIN, width), jnp.float32),
            pltpu.VMEM((SIDE, width), jnp.float32),
            pltpu.VMEM((ROWS + 2, COLS + 16, width), jnp.float32),
            pltpu.VMEM((2, ROWS, width), jnp.float32),
            pltpu.VMEM((MAIN, width), jnp.float32),
            pltpu.VMEM((MAIN, width), jnp.bfloat16),
            pltpu.VMEM((3, ROWS + 2, COLS, width), jnp.float32),
        ],
        compiler_params=pltpu.CompilerParams(vmem_limit_bytes=60 * 1024 * 1024),
    )(tokens_in, got, w_expand, taps)


def project_kernel(
    mixed_ref, gate_ref, x_ref, cot_ref, w_ref, scaled_ref, middle_ref, out_ref, flat, packed
):
    scaled = (mixed_ref[...] * gate_ref[...]).astype(jnp.bfloat16)
    scaled_ref[...] = scaled
    middle = x_ref[...].astype(jnp.float32) + jnp.dot(
        scaled, w_ref[...], preferred_element_type=jnp.float32
    )
    middle_ref[...] = middle

    def pack(values, first_row):
        for piece in range(4):
            flat[piece] = values[:, piece * 128 : (piece + 1) * 128]
        for piece in range(4):
            half, tile = piece // 2, piece % 2
            for a in range(2):
                for place in range(8):
                    source = a * 64 + (place // 4) * 32 + place % 4
                    packed[tile, pl.ds(a * 128 + half * 8 + place, 8, stride=16), :] = flat[
                        piece, pl.ds(source, 8, stride=4), :
                    ]
        for tile in range(2):
            out_ref[:, first_row : first_row + 16, tile * 128 : (tile + 1) * 128] = (
                packed[tile].reshape(16, 16, 128).astype(jnp.bfloat16)
            )

    pack(layer_normalize(middle)[0], 0)
    pack(cot_ref[...].astype(jnp.float32), 16)


def project(mixed, gate, tokens_in, cotangent, w_project):
    tokens, hidden = mixed.shape
    channels = w_project.shape[1]
    height = 128

    def moving(width):
        return pl.BlockSpec((height, width), lambda t: (t, 0))

    def fixed(shape):
        return pl.BlockSpec(shape, lambda t: (0, 0))

    return pl.pallas_call(
        project_kernel,
        grid=(tokens // height,),
        out_shape=(
            jax.ShapeDtypeStruct((tokens, hidden), jnp.bfloat16),
            jax.ShapeDtypeStruct((tokens, channels), jnp.float32),
            jax.ShapeDtypeStruct((64, 32, channels // 2), jnp.bfloat16),
        ),
        in_specs=[
            moving(hidden),
            fixed((1, hidden)),
            moving(channels),
            moving(channels),
            fixed(w_project.shape),
        ],
        out_specs=[
            moving(hidden),
            moving(channels),
            pl.BlockSpec((16, 32, channels // 2), lambda t: (t, 0, 0)),
        ],
        scratch_shapes=[
            pltpu.VMEM((4, height, 128), jnp.float32),
            pltpu.VMEM((2, 256, 128), jnp.float32),
        ],
        compiler_params=pltpu.CompilerParams(vmem_limit_bytes=60 * 1024 * 1024),
    )(mixed, gate, tokens_in, cotangent, w_project)


def middle_kernel(
    ret_ref, middle_ref, cot_ref, mixed_ref, wout_ref, wproj_ref, out_ref, grad_ref, grad_b_ref,
    scaled_grad_ref, gate_ref, edge_ref, flat, packed, total, ends
):
    step = pl.program_id(0)

    def unpack(first_row):
        for tile in range(2):
            block = ret_ref[:, first_row : first_row + 16, tile * 128 : (tile + 1) * 128]
            packed[tile] = block.astype(jnp.float32).reshape(256, 128)
        for piece in range(4):
            half, tile = piece // 2, piece % 2
            for a in range(2):
                for place in range(8):
                    target = a * 64 + (place // 4) * 32 + place % 4
                    flat[piece, pl.ds(target, 8, stride=4), :] = packed[
                        tile, pl.ds(a * 128 + half * 8 + place, 8, stride=16), :
                    ]
        return jnp.concatenate([flat[piece] for piece in range(4)], axis=-1)

    middle = middle_ref[...]
    context = unpack(0).astype(jnp.bfloat16)
    out_ref[...] = (
        middle + jnp.dot(context, wout_ref[...], preferred_element_type=jnp.float32)
    ).astype(jnp.bfloat16)
    standard, inverse = layer_normalize(middle)
    grad = cot_ref[...].astype(jnp.float32) + norm_backward_pass(standard, inverse, unpack(16))
    grad_ref[...] = grad
    grad_b = grad.astype(jnp.bfloat16)
    grad_b_ref[...] = grad_b
    height = grad.shape[0]
    lines = height // COLS
    for k in range(lines):
        ends[0, pl.ds(step * lines + k, 1), :] = grad[k * COLS : k * COLS + 1]
        ends[1, pl.ds(step * lines + k, 1), :] = grad[(k + 1) * COLS - 1 : (k + 1) * COLS]

    @pl.when(step == 0)
    def _():
        total[...] = jnp.zeros_like(total)
        edge_ref[0:COLS, :] = grad_b[0:COLS]

    hidden = wproj_ref.shape[0]
    for low in range(0, hidden, 512):
        scaled_grad = lax.dot_general(
            grad_b, wproj_ref[low : low + 512, :], BACKWARD, preferred_element_type=jnp.float32
        )
        scaled_grad_ref[:, low : low + 512] = scaled_grad
        terms = scaled_grad * mixed_ref[:, low : low + 512]
        total[:, low : low + 512] += jnp.sum(terms.reshape(-1, 8, 512), axis=0)

    @pl.when(step == pl.num_programs(0) - 1)
    def _():
        edge_ref[COLS : 2 * COLS, :] = grad_b[height - COLS : height]
        edge_ref[2 * COLS : 2 * COLS + ROWS, :] = ends[0].astype(jnp.bfloat16)
        edge_ref[2 * COLS + ROWS : EDGE, :] = ends[1].astype(jnp.bfloat16)
        for tile in range(hidden // 128):
            gate_ref[tile : tile + 1, :] = jnp.sum(
                total[:, tile * 128 : (tile + 1) * 128], axis=0, keepdims=True
            )


def middle_backward(returned, middle, cotangent, mixed, w_out, w_project):
    tokens, hidden = mixed.shape
    channels = middle.shape[1]
    height = 128

    def moving(width):
        return pl.BlockSpec((height, width), lambda t: (t, 0))

    def fixed(shape):
        return pl.BlockSpec(shape, lambda t: (0, 0))

    return pl.pallas_call(
        middle_kernel,
        grid=(tokens // height,),
        out_shape=(
            jax.ShapeDtypeStruct((tokens, channels), jnp.bfloat16),
            jax.ShapeDtypeStruct((tokens, channels), jnp.float32),
            jax.ShapeDtypeStruct((tokens, channels), jnp.bfloat16),
            jax.ShapeDtypeStruct((tokens, hidden), jnp.float32),
            jax.ShapeDtypeStruct((hidden // 128, 128), jnp.float32),
            jax.ShapeDtypeStruct((EDGE, channels), jnp.bfloat16),
        ),
        in_specs=[
            pl.BlockSpec((16, 32, channels // 2), lambda t: (t, 0, 0)),
            moving(channels),
            moving(channels),
            moving(hidden),
            fixed(w_out.shape),
            fixed(w_project.shape),
        ],
        out_specs=[
            moving(channels),
            moving(channels),
            moving(channels),
            moving(hidden),
            fixed((hidden // 128, 128)),
            fixed((EDGE, channels)),
        ],
        scratch_shapes=[
            pltpu.VMEM((4, height, 128), jnp.float32),
            pltpu.VMEM((2, 256, 128), jnp.float32),
            pltpu.VMEM((8, hidden), jnp.float32),
            pltpu.VMEM((2, ROWS, channels), jnp.float32),
        ],
        compiler_params=pltpu.CompilerParams(vmem_limit_bytes=60 * 1024 * 1024),
    )(returned, middle, cotangent, mixed, w_out, w_project)


def regroup(values, flat, place, first):
    for tile in range(4):
        flat[tile] = values[:, tile * 128 : (tile + 1) * 128]
    for tile in range(4):
        for r in range(4):
            place[tile, pl.ds(first + r, 128, stride=16), :] = flat[
                tile, pl.ds(r, 128, stride=4), :
            ]


def back_kernel(
    scaled_grad_ref, slope_mix_ref, slope_got_ref, grad_got_ref, gate_ref, pooled_ref, project_ref,
    main_ref, slope_ref, w_ref, taps_ref, x_ref, grad_ref, scaled_ref, grad_b_ref,
    out_ref, parts_ref, terms_ref, project_parts_ref, got_ref, turned, side, padded, shifted, preexp, total, flat, place
):
    step = pl.program_id(0)
    last = pl.num_programs(0) - 1

    @pl.when(step == 0)
    def _():
        side[...] = jnp.zeros_like(side)
        total[...] = jnp.zeros_like(total)
        turned[...] = layer_normalize(x_ref[...])[0].T.astype(jnp.bfloat16)

    def premix(scaled_grad, slope):
        grads = (scaled_grad * gate_ref[...] + pooled_ref[...]) * slope
        return grads.astype(jnp.bfloat16).astype(jnp.float32)

    got_ref[...] = premix(
        lax.dot_general(
            grad_got_ref[...], project_ref[...], BACKWARD, preferred_element_type=jnp.float32
        ),
        slope_got_ref[...].astype(jnp.float32),
    )
    masks = edge_masks()
    fill_sides(got_ref, side, masks, 4)
    padded[0, 8 : 8 + COLS, :] = got_ref[0:COLS, :] * masks[0]
    padded[ROWS + 1, 8 : 8 + COLS, :] = got_ref[COLS : 2 * COLS, :] * masks[1]

    @pl.loop(0, ROWS, unroll=4)
    def _(y):
        rows = pl.ds(pl.multiple_of(y * COLS, COLS), COLS)
        padded[y + 1, 8 : 8 + COLS, :] = premix(scaled_grad_ref[rows, :], slope_mix_ref[rows, :])

    @pl.loop(0, ROWS + 2, unroll=6)
    def _(y):
        eight = pl.ds(pl.multiple_of(y * 8, 8), 8)
        edge = jnp.concatenate([side[tile, eight, :] for tile in range(4)], axis=-1)
        padded[y, 0:8, :] = edge
        padded[y, 8 + COLS : 16 + COLS, :] = edge
        shifted[0, y] = padded[y, 7 : 7 + COLS, :]
        shifted[1, y] = padded[y, 8 : 8 + COLS, :]
        shifted[2, y] = padded[y, 9 : 9 + COLS, :]

    for low in range(0, 512, 256):
        lanes = slice(low, low + 256)

        def unmix(y, sums):
            rows = pl.ds(pl.multiple_of(y * COLS, COLS), COLS)
            own = main_ref[rows, lanes].astype(jnp.float32)
            summed = jnp.zeros((COLS, 256), jnp.float32)
            new = []
            for r in range(3):
                for c in range(3):
                    window = shifted[2 - c, y + 2 - r, :, lanes]
                    summed = summed + window * taps_ref[r, c : c + 1, lanes]
                    term = own * window
                    new.append(sums[3 * r + c] + jnp.sum(term.reshape(-1, 8, 256), axis=0))
            preexp[rows, lanes] = (summed * slope_ref[rows, lanes]).astype(jnp.bfloat16)
            return tuple(new)

        sums = lax.fori_loop(0, ROWS, unmix, (jnp.zeros((8, 256), jnp.float32),) * 9, unroll=4)
        for k in range(9):
            terms_ref[k : k + 1, lanes] = jnp.sum(sums[k], axis=0, keepdims=True)

    project_parts_ref[...] = (
        lax.dot_general(
            scaled_ref[...], grad_b_ref[...], CONTRACT, preferred_element_type=jnp.float32
        )
        .astype(jnp.bfloat16)
        .reshape(project_parts_ref.shape)
    )
    regroup(
        jnp.dot(turned[...], preexp[...], preferred_element_type=jnp.float32), flat, place, step * 4
    )
    total[...] += lax.dot_general(
        preexp[...], w_ref[...], BACKWARD, preferred_element_type=jnp.float32
    )

    @pl.when(step == last)
    def _():
        for tile in range(4):
            parts_ref[:, :, tile * 128 : (tile + 1) * 128] = (
                place[tile].reshape(128, 16, 128).astype(jnp.bfloat16)
            )

        @pl.loop(0, ROWS, unroll=4)
        def _(y):
            rows = pl.ds(pl.multiple_of(y * COLS, COLS), COLS)
            standard, inverse = layer_normalize(x_ref[rows, :])
            out_ref[rows, :] = (
                grad_ref[rows, :] + norm_backward_pass(standard, inverse, total[rows, :])
            ).astype(jnp.bfloat16)


def mix_backward(
    scaled_grad, slope_mix, slope_got, grad_got, gate, pooled_grad, w_project, main, slope,
    w_expand, taps, tokens_in, grad, scaled, grad_b
):
    tokens, hidden = scaled_grad.shape
    channels = w_expand.shape[0]
    width = 512

    def fixed(shape):
        return pl.BlockSpec(shape, lambda e: (0,) * len(shape))

    def moving(height):
        return pl.BlockSpec((height, width), lambda e: (0, e))

    return pl.pallas_call(
        back_kernel,
        grid=(hidden // width,),
        out_shape=(
            jax.ShapeDtypeStruct((tokens, channels), jnp.bfloat16),
            jax.ShapeDtypeStruct((128, 16, width), jnp.bfloat16),
            jax.ShapeDtypeStruct((9, hidden), jnp.float32),
            jax.ShapeDtypeStruct((hidden // 16, 16, channels), jnp.bfloat16),
        ),
        in_specs=[
            moving(tokens),
            moving(tokens),
            moving(slope_got.shape[0]),
            fixed(grad_got.shape),
            moving(1),
            moving(1),
            pl.BlockSpec((width, channels), lambda e: (e, 0)),
            moving(tokens),
            moving(tokens),
            moving(channels),
            pl.BlockSpec((3, 3, width), lambda e: (0, 0, e)),
            fixed(tokens_in.shape),
            fixed(grad.shape),
            moving(tokens),
            fixed(grad_b.shape),
        ],
        out_specs=[
            fixed((tokens, channels)),
            fixed((128, 16, width)),
            moving(9),
            pl.BlockSpec((width // 16, 16, channels), lambda e: (e, 0, 0)),
        ],
        scratch_shapes=[
            pltpu.VMEM(slope_got.shape[:1] + (width,), jnp.float32),
            pltpu.VMEM((channels, tokens), jnp.bfloat16),
            pltpu.VMEM((4, SIDE, 128), jnp.float32),
            pltpu.VMEM((ROWS + 2, COLS + 16, width), jnp.float32),
            pltpu.VMEM((3, ROWS + 2, COLS, width), jnp.float32),
            pltpu.VMEM((tokens, width), jnp.bfloat16),
            pltpu.VMEM((tokens, channels), jnp.float32),
            pltpu.VMEM((4, tokens, 128), jnp.float32),
            pltpu.VMEM((4, 2048, 128), jnp.float32),
        ],
        compiler_params=pltpu.CompilerParams(vmem_limit_bytes=60 * 1024 * 1024),
    )(
        scaled_grad, slope_mix, slope_got, grad_got, gate, pooled_grad, w_project, main, slope,
        w_expand, taps, tokens_in, grad, scaled, grad_b
    )


HEAD_DIM = 32
QUAD = 4
PLACES = 64
GROUPS = 8
STAGE = 4


def attention_kernel(
    x_ref,
    wqkv_ref,
    wout_ref,
    bias_ref,
    ret_ref,
    parts_ref,
    table_ref,
    spread,
    qkv,
    cgrad,
    normed_ref,
    proj_ref,
    context_ref,
    cot_ref,
    flat,
    place,
    turned,
):
    channels = wout_ref.shape[0]
    factor = HEAD_DIM ** (-0.5)

    def gather(first_row, out_ref):
        for tile in range(2):
            block = x_ref[:, first_row : first_row + 16, tile * 128 : (tile + 1) * 128]
            spread[tile] = block.astype(jnp.float32).reshape(1024, 128)
        for group in range(GROUPS):
            for piece in range(4):
                half, tile = piece // 2, piece % 2
                rows = spread[tile, pl.ds(half * 8 + group, PLACES, stride=16), :]
                out_ref[group * PLACES : (group + 1) * PLACES, piece * 128 : (piece + 1) * 128] = (
                    rows.astype(jnp.bfloat16)
                )

    gather(0, normed_ref)
    gather(16, cot_ref)

    @pl.loop(0, 3 * channels // 256)
    def _(n):
        cols = pl.ds(pl.multiple_of(n * 256, 256), 256)
        qkv[:, cols] = jnp.dot(
            normed_ref[...], wqkv_ref[:, cols], preferred_element_type=jnp.float32
        ).astype(jnp.bfloat16)

    @pl.loop(0, channels // 256)
    def _(n):
        cols = pl.ds(pl.multiple_of(n * 256, 256), 256)
        cgrad[:, cols] = lax.dot_general(
            cot_ref[...], wout_ref[cols, :], BACKWARD, preferred_element_type=jnp.float32
        ).astype(jnp.bfloat16)

    table_ref[...] = jnp.zeros_like(table_ref)
    lane_head = lax.broadcasted_iota(jnp.int32, (PLACES, 128), 1) // HEAD_DIM
    masks = [(lane_head == h).astype(jnp.float32).astype(jnp.bfloat16) for h in range(QUAD)]
    masks_f = [(lane_head == h).astype(jnp.float32) for h in range(QUAD)]

    def widen(block):
        return jnp.concatenate([block * masks[h] for h in range(QUAD)], axis=0)

    def narrow(full):
        total = full[:PLACES] * masks_f[0]
        for h in range(1, QUAD):
            total = total + full[h * PLACES : (h + 1) * PLACES] * masks_f[h]
        return total

    @pl.loop(0, GROUPS)
    def _(group):
        rows = pl.ds(pl.multiple_of(group * PLACES, PLACES), PLACES)
        for first in range(0, 4, STAGE):
            quads = range(first, first + STAGE)
            lows = [quad * 128 for quad in quads]
            queries = [qkv[rows, low : low + 128] for low in lows]
            keys_in = [qkv[rows, channels + low : channels + low + 128] for low in lows]
            values_in = [qkv[rows, 2 * channels + low : 2 * channels + low + 128] for low in lows]
            grads = [cgrad[rows, low : low + 128] for low in lows]
            queries_wide = [widen(block) for block in queries]
            grads_wide = [widen(block) for block in grads]

            def product(left, right, dims):
                return [
                    lax.dot_general(x, y, dims, preferred_element_type=jnp.float32)
                    for x, y in zip(left, right)
                ]

            plain = (((1,), (0,)), ((), ()))
            scores = product(keys_in, queries_wide, BACKWARD)
            weights_grad = product(values_in, grads_wide, BACKWARD)
            scores = [x * factor + bias_ref[quad] for x, quad in zip(scores, quads)]
            scores = [jnp.exp(x - jnp.max(x, axis=0, keepdims=True)) for x in scores]
            weights = [x * (1.0 / jnp.sum(x, axis=0, keepdims=True)) for x in scores]
            weights_b = [x.astype(jnp.bfloat16) for x in weights]
            context = product(weights_b, values_in, CONTRACT)
            values_grad = product(weights_b, grads_wide, plain)
            scores_grad = [
                x * (y - jnp.sum(x * y, axis=0, keepdims=True))
                for x, y in zip(weights, weights_grad)
            ]
            scores_b = [(x * factor).astype(jnp.bfloat16) for x in scores_grad]
            queries_grad = product(scores_b, keys_in, CONTRACT)
            keys_grad = product(scores_b, queries_wide, plain)
            for k, (quad, low) in enumerate(zip(quads, lows)):
                table_ref[quad] += scores_grad[k]
                context_ref[rows, low : low + 128] = narrow(context[k]).astype(jnp.bfloat16)
                proj_ref[rows, low : low + 128] = narrow(queries_grad[k]).astype(jnp.bfloat16)
                proj_ref[rows, channels + low : channels + low + 128] = keys_grad[k].astype(
                    jnp.bfloat16
                )
                proj_ref[rows, 2 * channels + low : 2 * channels + low + 128] = values_grad[
                    k
                ].astype(jnp.bfloat16)

    def scatter(read, first_row):
        for group in range(GROUPS):
            for piece in range(4):
                half, tile = piece // 2, piece % 2
                spread[tile, pl.ds(half * 8 + group, PLACES, stride=16), :] = read(group, piece)
        for tile in range(2):
            ret_ref[:, first_row : first_row + 16, tile * 128 : (tile + 1) * 128] = (
                spread[tile].reshape(64, 16, 128).astype(jnp.bfloat16)
            )

    def read_context(group, piece):
        return context_ref[
            group * PLACES : (group + 1) * PLACES, piece * 128 : (piece + 1) * 128
        ].astype(jnp.float32)

    scatter(read_context, 0)

    for n in range(channels // 256):
        grads = lax.dot_general(
            proj_ref[...],
            wqkv_ref[n * 256 : (n + 1) * 256, :],
            BACKWARD,
            preferred_element_type=jnp.float32,
        )
        for group in range(GROUPS):
            for tile in range(2):
                spread[tile, pl.ds(n * 8 + group, PLACES, stride=16), :] = grads[
                    group * PLACES : (group + 1) * PLACES, tile * 128 : (tile + 1) * 128
                ]
    for tile in range(2):
        ret_ref[:, 16:32, tile * 128 : (tile + 1) * 128] = (
            spread[tile].reshape(64, 16, 128).astype(jnp.bfloat16)
        )

    turned[...] = normed_ref[...].T
    for q in range(3):
        regroup(
            jnp.dot(
                turned[...],
                proj_ref[:, q * channels : (q + 1) * channels],
                preferred_element_type=jnp.float32,
            ),
            flat,
            place,
            q * 4,
        )
    regroup(
        lax.dot_general(
            context_ref[...], cot_ref[...], CONTRACT, preferred_element_type=jnp.float32
        ),
        flat,
        place,
        12,
    )
    for tile in range(4):
        parts_ref[:, :, tile * 128 : (tile + 1) * 128] = (
            place[tile].reshape(128, 16, 128).astype(jnp.bfloat16)
        )


def attention(blocks, w_qkv, w_out, bias):
    channels = w_out.shape[0]
    tokens = GROUPS * PLACES
    shapes = (
        jax.ShapeDtypeStruct(blocks.shape, jnp.bfloat16),
        jax.ShapeDtypeStruct((128, 16, channels), jnp.bfloat16),
        jax.ShapeDtypeStruct(bias.shape, jnp.float32),
    )
    return pl.pallas_call(
        attention_kernel,
        out_shape=shapes,
        in_specs=[pl.BlockSpec(memory_space=pltpu.VMEM)] * 4,
        out_specs=[pl.BlockSpec(memory_space=pltpu.VMEM)] * 3,
        scratch_shapes=[
            pltpu.VMEM((2, 1024, 128), jnp.float32),
            pltpu.VMEM((tokens, 3 * channels), jnp.bfloat16),
            pltpu.VMEM((tokens, channels), jnp.bfloat16),
            pltpu.VMEM((tokens, channels), jnp.bfloat16),
            pltpu.VMEM((tokens, 3 * channels), jnp.bfloat16),
            pltpu.VMEM((tokens, channels), jnp.bfloat16),
            pltpu.VMEM((tokens, channels), jnp.bfloat16),
            pltpu.VMEM((4, tokens, 128), jnp.float32),
            pltpu.VMEM((4, 2048, 128), jnp.float32),
            pltpu.VMEM((channels, tokens), jnp.bfloat16),
        ],
        compiler_params=pltpu.CompilerParams(vmem_limit_bytes=60 * 1024 * 1024),
    )(blocks, w_qkv, w_out, bias)


def on_device(
    inputs, out_grad, w_expand, dw_kernel, se_reduce, se_expand, w_project, w_qkv, w_out, pos_table
):
    images, tile_rows, tile_cols, channels = inputs.shape
    hidden_units = w_expand.shape[1]
    heads = pos_table.shape[0]
    places = GRID * GRID
    full_rows = tile_rows * lax.axis_size("row")
    full_cols = tile_cols * lax.axis_size("col")
    cells = full_rows * full_cols
    factor = (images * cells) ** (-0.5)
    tokens = images * tile_rows * tile_cols
    onehot = offset_table(GRID)
    bias = (
        jnp.dot(pos_table, onehot, precision=HIGHEST)
        .reshape(heads // QUAD, QUAD, places, places)
        .transpose(0, 2, 1, 3)
        .reshape(heads // QUAD, places, QUAD * places)
    )
    flat_inputs = inputs.reshape(tokens, channels)
    flattened_cotangent = out_grad.reshape(tokens, channels)
    mixed, slope_mix, slope_expand, main, pooled, slope_edges = expand_and_mix(
        flat_inputs, halo(inputs[0], 5), w_expand, dw_kernel
    )
    pooled, slope_got = sum_and_halo(pooled.reshape(-1, 128), slope_edges, 3)
    pooled = pooled.reshape(images, -1) / cells
    squeeze_pre = jnp.dot(pooled, se_reduce, precision=HIGHEST)
    squeeze_sig = jax.nn.sigmoid(squeeze_pre)
    squeezed = squeeze_pre * squeeze_sig
    gate = jax.nn.sigmoid(jnp.dot(squeezed, se_expand, precision=HIGHEST))
    scaled, middle_activation, outgoing = project(
        mixed, gate, flat_inputs, flattened_cotangent, w_project
    )
    returned, attention_parts, scores_sum = attention(swap(outgoing, 1), w_qkv, w_out, bias)
    table_part = lax.dot_general(
        scores_sum.reshape(heads // QUAD, places, QUAD, places)
        .transpose(0, 2, 1, 3)
        .reshape(heads, places * places),
        onehot,
        BACKWARD,
        precision=HIGHEST,
    )
    block_out, middle_gradient, middle_b, scaled_grad, gate_grad, grad_edges = middle_backward(
        swap(returned, 2), middle_activation, flattened_cotangent, mixed, w_out, w_project
    )
    gate_grad, grad_got = sum_and_halo(gate_grad, grad_edges, 4)
    gate_grad = gate_grad.reshape(images, -1)
    excite_grad = gate_grad * gate * (1.0 - gate)
    squeezed_grad = lax.dot_general(excite_grad, se_expand, BACKWARD, precision=HIGHEST)
    squeeze_grad = squeezed_grad * squeeze_sig * (1.0 + squeeze_pre * (1.0 - squeeze_sig))
    pooled_grad = lax.dot_general(squeeze_grad, se_reduce, BACKWARD, precision=HIGHEST)
    se_reduce_grad = lax.dot_general(pooled, squeeze_grad, CONTRACT, precision=HIGHEST) * factor
    se_expand_grad = lax.dot_general(squeezed, excite_grad, CONTRACT, precision=HIGHEST) * factor
    input_gradient, expand_parts, kernel_part, project_parts = mix_backward(
        scaled_grad,
        slope_mix,
        slope_got,
        grad_got,
        gate,
        pooled_grad / cells,
        w_project,
        main,
        slope_expand,
        w_expand,
        dw_kernel,
        flat_inputs,
        middle_gradient,
        scaled,
        middle_b,
    )
    small = jnp.concatenate([kernel_part.reshape(-1), table_part.reshape(-1)])
    unit = lax.axis_size("row") * 1024
    room = -small.shape[0] % unit
    small = jnp.pad(small, (0, room)).reshape(lax.axis_size("row"), -1, 128)
    project_grad, expand_grad, qkv_grad, out_proj_grad, small = reduce_all(
        (project_parts, expand_parts, attention_parts), small, factor, 7
    )
    small = small.reshape(-1)
    kernel_size = kernel_part.size
    kernel_sum = small[:kernel_size].reshape(dw_kernel.shape)
    table_sum = small[kernel_size : kernel_size + table_part.size].reshape(table_part.shape)
    return (
        block_out.reshape(images, tile_rows, tile_cols, channels),
        input_gradient.reshape(images, tile_rows, tile_cols, channels),
        expand_grad,
        project_grad,
        qkv_grad,
        out_proj_grad,
        kernel_sum * factor,
        se_reduce_grad,
        se_expand_grad,
        table_sum * factor,
    )


def solution(mesh):
    placed = (
        P(None, "row", "col", None),
        P(None, "row", "col", None),
        P(),
        P(),
        P(),
        P(),
        P(),
        P(),
        P(),
        P(),
    )
    return jax.shard_map(
        on_device,
        mesh=mesh,
        in_specs=placed,
        out_specs=(
            P(None, "row", "col", None),
            P(None, "row", "col", None),
            P(("row", "col"), None),
            P(("row", "col"), None),
            P(("row", "col"), None),
            P(("row", "col"), None),
            P(),
            P(),
            P(),
            P(),
        ),
        check_vma=False,
    )
```

```python
import functools
import math

import jax
import jax.numpy as jnp
from jax import lax
from jax.experimental import pallas as pl
from jax.experimental.pallas import tpu as pltpu
from jax.sharding import PartitionSpec as P

GRID = 8


EPSILON = 1e-05
GELU_SCALE = math.sqrt(2.0 / math.pi)
HIGHEST = lax.Precision.HIGHEST
MESH = pl.DeviceIdType.MESH
CONTRACT = (((0,), (0,)), ((), ()))
BACKWARD = (((1,), (1,)), ((), ()))


def gelu_slope(values):
    cubic = values * values * values
    bent = jnp.tanh(GELU_SCALE * (values + 0.044715 * cubic))
    result = 0.5 * values * (1.0 + bent)
    slope = 0.5 * (1.0 + bent) + 0.5 * values * (1.0 - bent * bent) * GELU_SCALE * (
        1.0 + 3.0 * 0.044715 * values * values
    )
    return (result, slope)


def layer_normalize(values):
    values = values.astype(jnp.float32)
    centred = values - jnp.mean(values, axis=-1, keepdims=True)
    inverse = lax.rsqrt(jnp.mean(centred * centred, axis=-1, keepdims=True) + EPSILON)
    return (centred * inverse, inverse)


def norm_backward_pass(normal_values, inverse, grads):
    grads = grads.astype(jnp.float32)
    return inverse * (
        grads
        - jnp.mean(grads, axis=-1, keepdims=True)
        - normal_values * jnp.mean(grads * normal_values, axis=-1, keepdims=True)
    )


def offset_table(side):
    places = jnp.arange(side * side, dtype=jnp.int32)
    place_row = places // side
    place_col = places % side
    offset_index = (
        (place_row[None, :] - place_row[:, None] + side - 1) * (2 * side - 1)
        + place_col[None, :]
        - place_col[:, None]
        + side
        - 1
    )
    table_slots = jnp.arange((2 * side - 1) ** 2, dtype=jnp.int32)
    return (table_slots[:, None] == offset_index.reshape(1, -1)).astype(jnp.float32)


AXES = ("row", "col")


def halo_sends(rows, cols, row, col, parts, o_ref, sems):
    top_ref, down_ref, left_ref, right_ref = parts
    width, height = top_ref.shape[0], left_ref.shape[0]
    up, down = lax.rem(row + rows - 1, rows), lax.rem(row + 1, rows)
    left, right = lax.rem(col + cols - 1, cols), lax.rem(col + 1, cols)
    last = width - 16
    sends = (
        (down_ref, 0, width, (down, col)),
        (top_ref, width, width, (up, col)),
        (right_ref, 2 * width, height, (row, right)),
        (left_ref, 2 * width + height, height, (row, left)),
        (down_ref.at[pl.ds(last, 16)], 2 * (width + height), 16, (down, right)),
        (down_ref.at[pl.ds(0, 16)], 2 * (width + height) + 16, 16, (down, left)),
        (top_ref.at[pl.ds(last, 16)], 2 * (width + height) + 32, 16, (up, right)),
        (top_ref.at[pl.ds(0, 16)], 2 * (width + height) + 48, 16, (up, left)),
    )
    copies = [
        pltpu.make_async_remote_copy(
            src_ref=source,
            dst_ref=o_ref.at[pl.ds(start, size)],
            send_sem=sems.at[0, number],
            recv_sem=sems.at[1, number],
            device_id=device,
            device_id_type=MESH,
        )
        for number, (source, start, size, device) in enumerate(sends)
    ]
    return copies, [device for _, _, _, device in sends]


def halo_kernel(rows, cols, top_ref, down_ref, left_ref, right_ref, o_ref, sems):
    row = lax.axis_index("row")
    col = lax.axis_index("col")
    barrier = pltpu.get_barrier_semaphore()
    copies, devices = halo_sends(
        rows, cols, row, col, (top_ref, down_ref, left_ref, right_ref), o_ref, sems
    )
    for device in devices:
        pl.semaphore_signal(barrier, inc=1, device_id=device, device_id_type=MESH)
    pl.semaphore_wait(barrier, len(devices))
    for copy in copies:
        copy.start()
    for copy in copies:
        copy.wait()


def halo(cells, number):
    height, width, features = cells.shape
    rows, cols = lax.axis_size("row"), lax.axis_size("col")
    total = 2 * (width + height) + 64

    def body(*refs):
        halo_kernel(rows, cols, *refs)

    return pl.pallas_call(
        body,
        out_shape=jax.ShapeDtypeStruct((total, features), cells.dtype),
        in_specs=[pl.BlockSpec(memory_space=pltpu.VMEM)] * 4,
        out_specs=pl.BlockSpec(memory_space=pltpu.VMEM),
        scratch_shapes=[pltpu.SemaphoreType.DMA((2, 8))],
        compiler_params=pltpu.CompilerParams(
            collective_id=number, has_side_effects=True, vmem_limit_bytes=60 * 1024 * 1024
        ),
    )(cells[0], cells[-1], cells[:, 0], cells[:, -1])


def reduce_kernel(
    rows, cols, factor, w0_ref, w1_ref, w2_ref, s_ref, project_ref, expand_ref, qkv_ref, out_ref,
    so_ref, mine, half, buf1, buf2, buf3, sum1, sum2, rs_buf, own_buf, col_buf, sems, pair_sems,
    axis_sems
):
    row = lax.axis_index("row")
    col = lax.axis_index("col")
    core = lax.rem(col, 2)
    me = (row // 4, lax.rem(row, 4), col // 2)
    w_refs = (w0_ref, w1_ref, w2_ref)
    pair = (row, col + 1 - 2 * core)
    barrier = pltpu.get_barrier_semaphore()

    def device(axis, place):
        if axis == 0:
            return (place * 4 + me[1], col)
        if axis == 1:
            return (me[0] * 4 + place, col)
        return (row, place * 2 + core)

    def signal(target):
        pl.semaphore_signal(barrier, inc=1, device_id=target, device_id_type=MESH)

    def wait_like(ref, sem):
        pltpu.make_async_copy(ref, ref, sem).wait()

    def send(source, target, send_sem, recv_sem, to):
        pltpu.make_async_remote_copy(
            src_ref=source,
            dst_ref=target,
            send_sem=send_sem,
            recv_sem=recv_sem,
            device_id=to,
            device_id_type=MESH,
        ).start()

    kept = [
        pltpu.make_async_copy(w_refs[p].at[:, :, :, core], mine.at[p], pair_sems.at[2, p])
        for p in range(3)
    ]
    for copy in kept:
        copy.start()
    signal(pair)
    for axis in range(3):
        for k in range(1, 4):
            signal(device(axis, lax.rem(me[axis] + k, 4)))

    @pl.loop(1, rows)
    def _(k):
        signal((lax.rem(row + k, rows), col))

    @pl.loop(1, cols)
    def _(k):
        signal((row, lax.rem(col + k, cols)))

    rs_buf[row] = s_ref[row]
    pl.semaphore_wait(barrier, 10 + rows - 1 + cols - 1)

    for p in range(3):
        send(
            w_refs[p].at[:, :, :, 1 - core], half.at[p], pair_sems.at[0, p], pair_sems.at[1, p], pair
        )

    @pl.loop(1, rows)
    def _(k):
        other = lax.rem(row + k, rows)
        send(s_ref.at[other], rs_buf.at[row], sems.at[0], sems.at[1], (other, col))

    def at_axis(ref, axis, place):
        if axis == 0:
            return ref.at[place]
        if axis == 1:
            return ref.at[:, place]
        return ref.at[:, :, place]

    orders = ((0, 1, 2), (1, 2, 0), (2, 0, 1))
    for p in range(3):
        first = orders[p][0]
        kept[p].wait()
        wait_like(half.at[p], pair_sems.at[1, p])

        @pl.loop(0, 16)
        def _(i):
            y, x = i // 4, lax.rem(i, 4)
            for z in range(4):
                both = mine[p, y, x, z].astype(jnp.float32) + half[p, y, x, z].astype(jnp.float32)
                half[p, y, x, z] = both.astype(jnp.bfloat16)

        for k in range(1, 4):
            place = lax.rem(me[first] + k, 4)
            send(
                at_axis(half.at[p], first, place),
                buf1.at[p, me[first]],
                axis_sems.at[0, 0, p],
                axis_sems.at[1, 0, p],
                device(first, place),
            )

    wait_like(rs_buf.at[pl.ds(0, rows - 1)], sems.at[1])
    total = rs_buf[0]
    for k in range(1, rows):
        total = total + rs_buf[k]
    own_buf[...] = total
    col_buf[col] = total

    @pl.loop(1, cols)
    def _(k):
        send(own_buf, col_buf.at[col], sems.at[2], sems.at[3], (row, lax.rem(col + k, cols)))

    for p in range(3):
        first, second, third = orders[p]
        wait_like(buf1.at[p, pl.ds(0, 3)], axis_sems.at[1, 0, p])
        own = at_axis(half.at[p], first, me[first])

        @pl.loop(0, 16)
        def _(i):
            u, v = i // 4, lax.rem(i, 4)
            total = own[u, v].astype(jnp.float32)
            for k in range(1, 4):
                total = total + buf1[p, lax.rem(me[first] + k, 4), u, v].astype(jnp.float32)
            sum1[p, u, v] = total.astype(jnp.bfloat16)

        for k in range(1, 4):
            place = lax.rem(me[second] + k, 4)
            send(
                at_axis(sum1.at[p], 0 if second < third else 1, place),
                buf2.at[p, me[second]],
                axis_sems.at[0, 1, p],
                axis_sems.at[1, 1, p],
                device(second, place),
            )

    wait_like(col_buf.at[pl.ds(0, cols - 1)], sems.at[3])
    total = col_buf[0]
    for k in range(1, cols):
        total = total + col_buf[k]
    so_ref[row] = total

    @pl.loop(1, rows)
    def _(k):
        send(so_ref.at[row], so_ref.at[row], sems.at[4], sems.at[5], (lax.rem(row + k, rows), col))

    for p in range(3):
        first, second, third = orders[p]
        wait_like(buf2.at[p, pl.ds(0, 3)], axis_sems.at[1, 1, p])
        own = at_axis(sum1.at[p], 0 if second < third else 1, me[second])

        @pl.loop(0, 4)
        def _(u):
            total = own[u].astype(jnp.float32)
            for k in range(1, 4):
                total = total + buf2[p, lax.rem(me[second] + k, 4), u].astype(jnp.float32)
            sum2[p, u] = total.astype(jnp.bfloat16)

        for k in range(1, 4):
            place = lax.rem(me[third] + k, 4)
            send(
                sum2.at[p, place],
                buf3.at[p, me[third]],
                axis_sems.at[0, 2, p],
                axis_sems.at[1, 2, p],
                device(third, place),
            )

    for p in range(3):
        third = orders[p][2]
        wait_like(buf3.at[p, pl.ds(0, 3)], axis_sems.at[1, 2, p])
        total = sum2[p, me[third]].astype(jnp.float32)
        for k in range(1, 4):
            total = total + buf3[p, lax.rem(me[third] + k, 4)].astype(jnp.float32)
        total = total * factor
        if p == 0:
            project_ref[...] = total
        elif p == 1:
            for q in range(4):
                expand_ref[:, q * 512 : (q + 1) * 512] = total[q * 4 : (q + 1) * 4]
        else:
            for q in range(3):
                qkv_ref[:, q * 512 : (q + 1) * 512] = total[q * 4 : (q + 1) * 4]
            out_ref[...] = total[12:16]

    wait_like(so_ref.at[pl.ds(0, rows - 1)], sems.at[5])
    wait_like(so_ref.at[pl.ds(0, rows - 1)], sems.at[4])
    wait_like(col_buf.at[pl.ds(0, cols - 1)], sems.at[2])
    wait_like(rs_buf.at[pl.ds(0, rows - 1)], sems.at[0])
    for p in range(3):
        wait_like(half.at[p], pair_sems.at[0, p])
        wait_like(buf1.at[p, pl.ds(0, 3)], axis_sems.at[0, 0, p])
        wait_like(buf2.at[p, pl.ds(0, 3)], axis_sems.at[0, 1, p])
        wait_like(buf3.at[p, pl.ds(0, 3)], axis_sems.at[0, 2, p])


def reduce_all(parts, small, factor, number):
    rows, cols = lax.axis_size("row"), lax.axis_size("col")
    block = small.shape[1:]
    chunk = parts[0].shape[1:]
    vmem = pl.BlockSpec(memory_space=pltpu.VMEM)

    def held(*lead):
        return pltpu.VMEM((3,) + lead + chunk, jnp.bfloat16)

    return pl.pallas_call(
        functools.partial(reduce_kernel, rows, cols, factor),
        out_shape=(
            jax.ShapeDtypeStruct((16, 512), jnp.float32),
            jax.ShapeDtypeStruct((4, 2048), jnp.float32),
            jax.ShapeDtypeStruct((4, 1536), jnp.float32),
            jax.ShapeDtypeStruct((4, 512), jnp.float32),
            jax.ShapeDtypeStruct(small.shape, jnp.float32),
        ),
        in_specs=[pl.BlockSpec(memory_space=pl.ANY)] * 3 + [vmem],
        out_specs=[vmem] * 5,
        scratch_shapes=[
            held(4, 4, 4),
            held(4, 4, 4),
            held(4, 4, 4),
            held(4, 4),
            held(4),
            held(4, 4),
            held(4),
            pltpu.VMEM(small.shape, jnp.float32),
            pltpu.VMEM(block, jnp.float32),
            pltpu.VMEM((cols,) + block, jnp.float32),
            pltpu.SemaphoreType.DMA((6,)),
            pltpu.SemaphoreType.DMA((3, 3)),
            pltpu.SemaphoreType.DMA((2, 3, 3)),
        ],
        compiler_params=pltpu.CompilerParams(
            collective_id=number, has_side_effects=True, vmem_limit_bytes=60 * 1024 * 1024
        ),
    )(*(part.reshape((4, 4, 4, 2) + chunk) for part in parts), small)


def sum_halo_kernel(
    rows, cols, x_ref, edge_ref, o_ref, got_ref, row_buf, sum_buf, col_buf, sems, halo_sems
):
    row = lax.axis_index("row")
    col = lax.axis_index("col")
    barrier = pltpu.get_barrier_semaphore()

    parts = [edge_ref.at[pl.ds(low, size)] for low, size in ((0, 32), (32, 32), (64, 16), (80, 16))]
    copies, devices = halo_sends(rows, cols, row, col, parts, got_ref, halo_sems)
    for device in devices:
        pl.semaphore_signal(barrier, inc=1, device_id=device, device_id_type=MESH)

    def row_peer(k):
        return lax.rem(row + k, rows)

    def col_peer(k):
        return lax.rem(col + k, cols)

    @pl.loop(1, rows)
    def _(k):
        pl.semaphore_signal(barrier, inc=1, device_id=(row_peer(k), col), device_id_type=MESH)

    @pl.loop(1, cols)
    def _(k):
        pl.semaphore_signal(barrier, inc=1, device_id=(row, col_peer(k)), device_id_type=MESH)

    row_buf[row] = x_ref[...]
    pl.semaphore_wait(barrier, rows + cols - 2 + len(devices))

    @pl.loop(1, rows)
    def _(k):
        pltpu.make_async_remote_copy(
            src_ref=x_ref,
            dst_ref=row_buf.at[row],
            send_sem=sems.at[0],
            recv_sem=sems.at[1],
            device_id=(row_peer(k), col),
            device_id_type=MESH,
        ).start()

    for copy in copies:
        copy.start()
    arrived = row_buf.at[pl.ds(0, rows - 1)]
    pltpu.make_async_copy(arrived, arrived, sems.at[1]).wait()
    total = row_buf[0]
    for k in range(1, rows):
        total = total + row_buf[k]
    sum_buf[...] = total
    col_buf[col] = total

    @pl.loop(1, cols)
    def _(k):
        pltpu.make_async_remote_copy(
            src_ref=sum_buf,
            dst_ref=col_buf.at[col],
            send_sem=sems.at[2],
            recv_sem=sems.at[3],
            device_id=(row, col_peer(k)),
            device_id_type=MESH,
        ).start()

    other = col_buf.at[pl.ds(0, cols - 1)]
    pltpu.make_async_copy(other, other, sems.at[3]).wait()
    total = col_buf[0]
    for k in range(1, cols):
        total = total + col_buf[k]
    o_ref[...] = total
    pltpu.make_async_copy(arrived, arrived, sems.at[0]).wait()
    pltpu.make_async_copy(other, other, sems.at[2]).wait()
    for copy in copies:
        copy.wait()


def sum_and_halo(values, edges, number):
    rows = lax.axis_size("row")
    cols = lax.axis_size("col")
    shape = values.shape
    vmem = pl.BlockSpec(memory_space=pltpu.VMEM)
    return pl.pallas_call(
        functools.partial(sum_halo_kernel, rows, cols),
        out_shape=(
            jax.ShapeDtypeStruct(shape, jnp.float32),
            jax.ShapeDtypeStruct((edges.shape[0] + 64, edges.shape[1]), edges.dtype),
        ),
        in_specs=[vmem, vmem],
        out_specs=[vmem, vmem],
        scratch_shapes=[
            pltpu.VMEM((rows,) + shape, jnp.float32),
            pltpu.VMEM(shape, jnp.float32),
            pltpu.VMEM((cols,) + shape, jnp.float32),
            pltpu.SemaphoreType.DMA((4,)),
            pltpu.SemaphoreType.DMA((2, 8)),
        ],
        compiler_params=pltpu.CompilerParams(
            collective_id=number, has_side_effects=True, vmem_limit_bytes=60 * 1024 * 1024
        ),
    )(values, edges)


def swap_kernel(parity, side, cols, x_ref, o_ref, sems):
    row = lax.axis_index("row")
    col = lax.axis_index("col")
    kind = lax.rem(row, parity)
    count = side * cols
    me = (row // parity) * cols + col
    barrier = pltpu.get_barrier_semaphore()

    def place(k):
        peer = lax.rem(me + k, count)
        return peer, ((peer // cols) * parity + kind, lax.rem(peer, cols))

    @pl.loop(1, count)
    def _(k):
        pl.semaphore_signal(barrier, inc=1, device_id=place(k)[1], device_id_type=MESH)

    own = pltpu.make_async_copy(x_ref.at[me], o_ref.at[me], sems.at[2])
    own.start()
    pl.semaphore_wait(barrier, count - 1)

    @pl.loop(1, count)
    def _(k):
        peer, device = place(k)
        pltpu.make_async_remote_copy(
            src_ref=x_ref.at[peer],
            dst_ref=o_ref.at[me],
            send_sem=sems.at[0],
            recv_sem=sems.at[1],
            device_id=device,
            device_id_type=MESH,
        ).start()

    own.wait()
    sent = x_ref.at[pl.ds(0, count - 1)]
    pltpu.make_async_copy(sent, sent, sems.at[0]).wait()
    arrived = o_ref.at[pl.ds(0, count - 1)]
    pltpu.make_async_copy(arrived, arrived, sems.at[1]).wait()


def swap(parts, number):
    parity = lax.axis_size("row") // GRID
    return pl.pallas_call(
        functools.partial(swap_kernel, parity, GRID, lax.axis_size("col")),
        out_shape=jax.ShapeDtypeStruct(parts.shape, parts.dtype),
        in_specs=[pl.BlockSpec(memory_space=pl.ANY)],
        out_specs=pl.BlockSpec(memory_space=pl.ANY),
        scratch_shapes=[pltpu.SemaphoreType.DMA((3,))],
        compiler_params=pltpu.CompilerParams(
            collective_id=number, has_side_effects=True, vmem_limit_bytes=60 * 1024 * 1024
        ),
    )(parts)


ROWS = 16
COLS = 32
MAIN = (ROWS + 2) * COLS
SIDE = (ROWS + 2) * 8
EDGE = 2 * (ROWS + COLS)


def edge_masks():
    row, col = lax.axis_index("row"), lax.axis_index("col")
    rows, cols = lax.axis_size("row"), lax.axis_size("col")
    return tuple(
        jnp.where(present, 1.0, 0.0).astype(jnp.float32)
        for present in (row > 0, row < rows - 1, col > 0, col < cols - 1)
    )


def fill_sides(got_ref, side_ref, masks, tiles):
    up, down, left, right = masks
    start = 2 * COLS
    corner = 2 * (COLS + ROWS)
    for tile in range(tiles):
        lanes = slice(tile * 128, (tile + 1) * 128)
        before = got_ref[start : start + ROWS, lanes].astype(jnp.float32)
        after = got_ref[start + ROWS : start + 2 * ROWS, lanes].astype(jnp.float32)
        side_ref[tile, pl.ds(8, ROWS, stride=8), :] = after * right
        side_ref[tile, pl.ds(15, ROWS, stride=8), :] = before * left
        corners = got_ref[corner : corner + 64, lanes].astype(jnp.float32)
        side_ref[tile, 7:8, :] = corners[15:16] * (up * left)
        side_ref[tile, 0:1, :] = corners[16:17] * (up * right)
        side_ref[tile, SIDE - 1 : SIDE, :] = corners[47:48] * (down * left)
        side_ref[tile, SIDE - 8 : SIDE - 7, :] = corners[48:49] * (down * right)


def expand_kernel(
    x_ref, got_ref, w_ref, taps_ref, mixed_ref, slope_mix_ref, slope_ref, main_ref,
    pooled_ref, edge_ref, normed, normed_side, side, pre, pre_side, padded, ends, slopes, mains, shifted
):
    step = pl.program_id(0)

    @pl.when(step == 0)
    def _():
        masks = edge_masks()
        side[...] = jnp.zeros_like(side)
        fill_sides(got_ref, side, masks, 4)
        values = jnp.concatenate([side[tile] for tile in range(4)], axis=-1)
        present = jnp.max(jnp.abs(values), axis=-1, keepdims=True) > 0.0
        standard = layer_normalize(values)[0]
        normed_side[...] = jnp.where(present, standard, 0.0).astype(jnp.bfloat16)
        normed[0:COLS, :] = (layer_normalize(got_ref[0:COLS, :])[0] * masks[0]).astype(jnp.bfloat16)
        normed[MAIN - COLS : MAIN, :] = (
            layer_normalize(got_ref[COLS : 2 * COLS, :])[0] * masks[1]
        ).astype(jnp.bfloat16)

        @pl.loop(0, ROWS, unroll=2)
        def _(y):
            rows = pl.ds(pl.multiple_of(y * COLS, COLS), COLS)
            after = pl.ds(pl.multiple_of((y + 1) * COLS, COLS), COLS)
            normed[after, :] = layer_normalize(x_ref[rows, :])[0].astype(jnp.bfloat16)

    width = w_ref.shape[1]
    pre[...] = jnp.dot(normed[...], w_ref[...], preferred_element_type=jnp.float32)
    pre_side[...] = jnp.dot(normed_side[...], w_ref[...], preferred_element_type=jnp.float32)

    @pl.loop(0, ROWS + 2, unroll=6)
    def _(y):
        rows = pl.ds(pl.multiple_of(y * COLS, COLS), COLS)
        result, slope = gelu_slope(pre[rows, :])
        rounded = result.astype(jnp.bfloat16)
        mains[rows, :] = rounded
        wide = rounded.astype(jnp.float32)
        padded[y, 8 : 8 + COLS, :] = wide
        shifted[1, y] = wide
        slopes[rows, :] = slope
        eight = pl.ds(pl.multiple_of(y * 8, 8), 8)
        edge = gelu_slope(pre_side[eight, :])[0].astype(jnp.bfloat16).astype(jnp.float32)
        padded[y, 0:8, :] = edge
        padded[y, 8 + COLS : 16 + COLS, :] = edge
        shifted[0, y] = padded[y, 7 : 7 + COLS, :]
        shifted[2, y] = padded[y, 9 : 9 + COLS, :]

    slope_ref[...] = slopes[COLS : MAIN - COLS, :]
    main_ref[...] = mains[COLS : MAIN - COLS, :]

    def mix(y, total):
        summed = jnp.zeros((COLS, width), jnp.float32)
        for r in range(3):
            for c in range(3):
                summed = summed + shifted[c, y + r] * taps_ref[r, c : c + 1, :]
        mixed, slope = gelu_slope(summed)
        rows = pl.ds(pl.multiple_of(y * COLS, COLS), COLS)
        mixed_ref[rows, :] = mixed
        slope_mix_ref[rows, :] = slope
        ends[0, pl.ds(y, 1), :] = slope[0:1]
        ends[1, pl.ds(y, 1), :] = slope[COLS - 1 : COLS]
        return total + jnp.sum(mixed.reshape(COLS // 8, 8, width), axis=0)

    total = lax.fori_loop(0, ROWS, mix, jnp.zeros((8, width), jnp.float32))
    tokens = ROWS * COLS
    edge_ref[0:COLS, :] = slope_mix_ref[0:COLS, :].astype(jnp.bfloat16)
    edge_ref[COLS : 2 * COLS, :] = slope_mix_ref[tokens - COLS : tokens, :].astype(jnp.bfloat16)
    edge_ref[2 * COLS : 2 * COLS + ROWS, :] = ends[0].astype(jnp.bfloat16)
    edge_ref[2 * COLS + ROWS : EDGE, :] = ends[1].astype(jnp.bfloat16)
    total = jnp.sum(total, axis=0, keepdims=True)
    for tile in range(width // 128):
        pooled_ref[0, tile : tile + 1, :] = total[:, tile * 128 : (tile + 1) * 128]


def expand_and_mix(tokens_in, got, w_expand, taps):
    tokens, channels = tokens_in.shape
    hidden = w_expand.shape[1]
    width = 512
    steps = hidden // width

    def fixed(shape):
        return pl.BlockSpec(shape, lambda e: (0, 0))

    def moving(height):
        return pl.BlockSpec((height, width), lambda e: (0, e))

    taps_spec = pl.BlockSpec((3, 3, width), lambda e: (0, 0, e))
    wide = jax.ShapeDtypeStruct((tokens, hidden), jnp.float32)
    return pl.pallas_call(
        expand_kernel,
        grid=(steps,),
        out_shape=(
            wide,
            wide,
            wide,
            jax.ShapeDtypeStruct((tokens, hidden), jnp.bfloat16),
            jax.ShapeDtypeStruct((steps, width // 128, 128), jnp.float32),
            jax.ShapeDtypeStruct((EDGE, hidden), jnp.bfloat16),
        ),
        in_specs=[fixed(tokens_in.shape), fixed(got.shape), moving(channels), taps_spec],
        out_specs=[
            moving(tokens),
            moving(tokens),
            moving(tokens),
            moving(tokens),
            pl.BlockSpec((1, width // 128, 128), lambda e: (e, 0, 0)),
            moving(EDGE),
        ],
        scratch_shapes=[
            pltpu.VMEM((MAIN, channels), jnp.bfloat16),
            pltpu.VMEM((SIDE, channels), jnp.bfloat16),
            pltpu.VMEM((4, SIDE, 128), jnp.float32),
            pltpu.VMEM((MAIN, width), jnp.float32),
            pltpu.VMEM((SIDE, width), jnp.float32),
            pltpu.VMEM((ROWS + 2, COLS + 16, width), jnp.float32),
            pltpu.VMEM((2, ROWS, width), jnp.float32),
            pltpu.VMEM((MAIN, width), jnp.float32),
            pltpu.VMEM((MAIN, width), jnp.bfloat16),
            pltpu.VMEM((3, ROWS + 2, COLS, width), jnp.float32),
        ],
        compiler_params=pltpu.CompilerParams(vmem_limit_bytes=60 * 1024 * 1024),
    )(tokens_in, got, w_expand, taps)


def project_kernel(
    mixed_ref, gate_ref, x_ref, cot_ref, w_ref, scaled_ref, middle_ref, out_ref, flat, packed
):
    scaled = (mixed_ref[...] * gate_ref[...]).astype(jnp.bfloat16)
    scaled_ref[...] = scaled
    middle = x_ref[...].astype(jnp.float32) + jnp.dot(
        scaled, w_ref[...], preferred_element_type=jnp.float32
    )
    middle_ref[...] = middle

    def pack(values, first_row):
        for piece in range(4):
            flat[piece] = values[:, piece * 128 : (piece + 1) * 128]
        for piece in range(4):
            half, tile = piece // 2, piece % 2
            for a in range(2):
                for place in range(8):
                    source = a * 64 + (place // 4) * 32 + place % 4
                    packed[tile, pl.ds(a * 128 + half * 8 + place, 8, stride=16), :] = flat[
                        piece, pl.ds(source, 8, stride=4), :
                    ]
        for tile in range(2):
            out_ref[:, first_row : first_row + 16, tile * 128 : (tile + 1) * 128] = (
                packed[tile].reshape(16, 16, 128).astype(jnp.bfloat16)
            )

    pack(layer_normalize(middle)[0], 0)
    pack(cot_ref[...].astype(jnp.float32), 16)


def project(mixed, gate, tokens_in, cotangent, w_project):
    tokens, hidden = mixed.shape
    channels = w_project.shape[1]
    height = 128

    def moving(width):
        return pl.BlockSpec((height, width), lambda t: (t, 0))

    def fixed(shape):
        return pl.BlockSpec(shape, lambda t: (0, 0))

    return pl.pallas_call(
        project_kernel,
        grid=(tokens // height,),
        out_shape=(
            jax.ShapeDtypeStruct((tokens, hidden), jnp.bfloat16),
            jax.ShapeDtypeStruct((tokens, channels), jnp.float32),
            jax.ShapeDtypeStruct((64, 32, channels // 2), jnp.bfloat16),
        ),
        in_specs=[
            moving(hidden),
            fixed((1, hidden)),
            moving(channels),
            moving(channels),
            fixed(w_project.shape),
        ],
        out_specs=[
            moving(hidden),
            moving(channels),
            pl.BlockSpec((16, 32, channels // 2), lambda t: (t, 0, 0)),
        ],
        scratch_shapes=[
            pltpu.VMEM((4, height, 128), jnp.float32),
            pltpu.VMEM((2, 256, 128), jnp.float32),
        ],
        compiler_params=pltpu.CompilerParams(vmem_limit_bytes=60 * 1024 * 1024),
    )(mixed, gate, tokens_in, cotangent, w_project)


def middle_kernel(
    ret_ref, middle_ref, cot_ref, mixed_ref, wout_ref, wproj_ref, out_ref, grad_ref, grad_b_ref,
    scaled_grad_ref, gate_ref, edge_ref, flat, packed, total, ends
):
    step = pl.program_id(0)

    def unpack(first_row):
        for tile in range(2):
            block = ret_ref[:, first_row : first_row + 16, tile * 128 : (tile + 1) * 128]
            packed[tile] = block.astype(jnp.float32).reshape(256, 128)
        for piece in range(4):
            half, tile = piece // 2, piece % 2
            for a in range(2):
                for place in range(8):
                    target = a * 64 + (place // 4) * 32 + place % 4
                    flat[piece, pl.ds(target, 8, stride=4), :] = packed[
                        tile, pl.ds(a * 128 + half * 8 + place, 8, stride=16), :
                    ]
        return jnp.concatenate([flat[piece] for piece in range(4)], axis=-1)

    middle = middle_ref[...]
    context = unpack(0).astype(jnp.bfloat16)
    out_ref[...] = (
        middle + jnp.dot(context, wout_ref[...], preferred_element_type=jnp.float32)
    ).astype(jnp.bfloat16)
    standard, inverse = layer_normalize(middle)
    grad = cot_ref[...].astype(jnp.float32) + norm_backward_pass(standard, inverse, unpack(16))
    grad_ref[...] = grad
    grad_b = grad.astype(jnp.bfloat16)
    grad_b_ref[...] = grad_b
    height = grad.shape[0]
    lines = height // COLS
    for k in range(lines):
        ends[0, pl.ds(step * lines + k, 1), :] = grad[k * COLS : k * COLS + 1]
        ends[1, pl.ds(step * lines + k, 1), :] = grad[(k + 1) * COLS - 1 : (k + 1) * COLS]

    @pl.when(step == 0)
    def _():
        total[...] = jnp.zeros_like(total)
        edge_ref[0:COLS, :] = grad_b[0:COLS]

    hidden = wproj_ref.shape[0]
    for low in range(0, hidden, 512):
        scaled_grad = lax.dot_general(
            grad_b, wproj_ref[low : low + 512, :], BACKWARD, preferred_element_type=jnp.float32
        )
        scaled_grad_ref[:, low : low + 512] = scaled_grad
        terms = scaled_grad * mixed_ref[:, low : low + 512]
        total[:, low : low + 512] += jnp.sum(terms.reshape(-1, 8, 512), axis=0)

    @pl.when(step == pl.num_programs(0) - 1)
    def _():
        edge_ref[COLS : 2 * COLS, :] = grad_b[height - COLS : height]
        edge_ref[2 * COLS : 2 * COLS + ROWS, :] = ends[0].astype(jnp.bfloat16)
        edge_ref[2 * COLS + ROWS : EDGE, :] = ends[1].astype(jnp.bfloat16)
        for tile in range(hidden // 128):
            gate_ref[tile : tile + 1, :] = jnp.sum(
                total[:, tile * 128 : (tile + 1) * 128], axis=0, keepdims=True
            )


def middle_backward(returned, middle, cotangent, mixed, w_out, w_project):
    tokens, hidden = mixed.shape
    channels = middle.shape[1]
    height = 128

    def moving(width):
        return pl.BlockSpec((height, width), lambda t: (t, 0))

    def fixed(shape):
        return pl.BlockSpec(shape, lambda t: (0, 0))

    return pl.pallas_call(
        middle_kernel,
        grid=(tokens // height,),
        out_shape=(
            jax.ShapeDtypeStruct((tokens, channels), jnp.bfloat16),
            jax.ShapeDtypeStruct((tokens, channels), jnp.float32),
            jax.ShapeDtypeStruct((tokens, channels), jnp.bfloat16),
            jax.ShapeDtypeStruct((tokens, hidden), jnp.float32),
            jax.ShapeDtypeStruct((hidden // 128, 128), jnp.float32),
            jax.ShapeDtypeStruct((EDGE, channels), jnp.bfloat16),
        ),
        in_specs=[
            pl.BlockSpec((16, 32, channels // 2), lambda t: (t, 0, 0)),
            moving(channels),
            moving(channels),
            moving(hidden),
            fixed(w_out.shape),
            fixed(w_project.shape),
        ],
        out_specs=[
            moving(channels),
            moving(channels),
            moving(channels),
            moving(hidden),
            fixed((hidden // 128, 128)),
            fixed((EDGE, channels)),
        ],
        scratch_shapes=[
            pltpu.VMEM((4, height, 128), jnp.float32),
            pltpu.VMEM((2, 256, 128), jnp.float32),
            pltpu.VMEM((8, hidden), jnp.float32),
            pltpu.VMEM((2, ROWS, channels), jnp.float32),
        ],
        compiler_params=pltpu.CompilerParams(vmem_limit_bytes=60 * 1024 * 1024),
    )(returned, middle, cotangent, mixed, w_out, w_project)


def regroup(values, flat, place, first):
    for tile in range(4):
        flat[tile] = values[:, tile * 128 : (tile + 1) * 128]
    for tile in range(4):
        for r in range(4):
            place[tile, pl.ds(first + r, 128, stride=16), :] = flat[
                tile, pl.ds(r, 128, stride=4), :
            ]


def back_kernel(
    scaled_grad_ref, slope_mix_ref, slope_got_ref, grad_got_ref, gate_ref, pooled_ref, project_ref,
    main_ref, slope_ref, w_ref, taps_ref, x_ref, grad_ref, scaled_ref, grad_b_ref,
    out_ref, parts_ref, terms_ref, project_parts_ref, got_ref, turned, side, padded, shifted, preexp, total, flat, place
):
    step = pl.program_id(0)
    last = pl.num_programs(0) - 1

    @pl.when(step == 0)
    def _():
        side[...] = jnp.zeros_like(side)
        total[...] = jnp.zeros_like(total)
        turned[...] = layer_normalize(x_ref[...])[0].T.astype(jnp.bfloat16)

    def premix(scaled_grad, slope):
        grads = (scaled_grad * gate_ref[...] + pooled_ref[...]) * slope
        return grads.astype(jnp.bfloat16).astype(jnp.float32)

    got_ref[...] = premix(
        lax.dot_general(
            grad_got_ref[...], project_ref[...], BACKWARD, preferred_element_type=jnp.float32
        ),
        slope_got_ref[...].astype(jnp.float32),
    )
    masks = edge_masks()
    fill_sides(got_ref, side, masks, 4)
    padded[0, 8 : 8 + COLS, :] = got_ref[0:COLS, :] * masks[0]
    padded[ROWS + 1, 8 : 8 + COLS, :] = got_ref[COLS : 2 * COLS, :] * masks[1]

    @pl.loop(0, ROWS, unroll=4)
    def _(y):
        rows = pl.ds(pl.multiple_of(y * COLS, COLS), COLS)
        padded[y + 1, 8 : 8 + COLS, :] = premix(scaled_grad_ref[rows, :], slope_mix_ref[rows, :])

    @pl.loop(0, ROWS + 2, unroll=6)
    def _(y):
        eight = pl.ds(pl.multiple_of(y * 8, 8), 8)
        edge = jnp.concatenate([side[tile, eight, :] for tile in range(4)], axis=-1)
        padded[y, 0:8, :] = edge
        padded[y, 8 + COLS : 16 + COLS, :] = edge
        shifted[0, y] = padded[y, 7 : 7 + COLS, :]
        shifted[1, y] = padded[y, 8 : 8 + COLS, :]
        shifted[2, y] = padded[y, 9 : 9 + COLS, :]

    for low in range(0, 512, 256):
        lanes = slice(low, low + 256)

        def unmix(y, sums):
            rows = pl.ds(pl.multiple_of(y * COLS, COLS), COLS)
            own = main_ref[rows, lanes].astype(jnp.float32)
            summed = jnp.zeros((COLS, 256), jnp.float32)
            new = []
            for r in range(3):
                for c in range(3):
                    window = shifted[2 - c, y + 2 - r, :, lanes]
                    summed = summed + window * taps_ref[r, c : c + 1, lanes]
                    term = own * window
                    new.append(sums[3 * r + c] + jnp.sum(term.reshape(-1, 8, 256), axis=0))
            preexp[rows, lanes] = (summed * slope_ref[rows, lanes]).astype(jnp.bfloat16)
            return tuple(new)

        sums = lax.fori_loop(0, ROWS, unmix, (jnp.zeros((8, 256), jnp.float32),) * 9, unroll=4)
        for k in range(9):
            terms_ref[k : k + 1, lanes] = jnp.sum(sums[k], axis=0, keepdims=True)

    project_parts_ref[...] = (
        lax.dot_general(
            scaled_ref[...], grad_b_ref[...], CONTRACT, preferred_element_type=jnp.float32
        )
        .astype(jnp.bfloat16)
        .reshape(project_parts_ref.shape)
    )
    regroup(
        jnp.dot(turned[...], preexp[...], preferred_element_type=jnp.float32), flat, place, step * 4
    )
    total[...] += lax.dot_general(
        preexp[...], w_ref[...], BACKWARD, preferred_element_type=jnp.float32
    )

    @pl.when(step == last)
    def _():
        for tile in range(4):
            parts_ref[:, :, tile * 128 : (tile + 1) * 128] = (
                place[tile].reshape(128, 16, 128).astype(jnp.bfloat16)
            )

        @pl.loop(0, ROWS, unroll=4)
        def _(y):
            rows = pl.ds(pl.multiple_of(y * COLS, COLS), COLS)
            standard, inverse = layer_normalize(x_ref[rows, :])
            out_ref[rows, :] = (
                grad_ref[rows, :] + norm_backward_pass(standard, inverse, total[rows, :])
            ).astype(jnp.bfloat16)


def mix_backward(
    scaled_grad, slope_mix, slope_got, grad_got, gate, pooled_grad, w_project, main, slope,
    w_expand, taps, tokens_in, grad, scaled, grad_b
):
    tokens, hidden = scaled_grad.shape
    channels = w_expand.shape[0]
    width = 512

    def fixed(shape):
        return pl.BlockSpec(shape, lambda e: (0,) * len(shape))

    def moving(height):
        return pl.BlockSpec((height, width), lambda e: (0, e))

    return pl.pallas_call(
        back_kernel,
        grid=(hidden // width,),
        out_shape=(
            jax.ShapeDtypeStruct((tokens, channels), jnp.bfloat16),
            jax.ShapeDtypeStruct((128, 16, width), jnp.bfloat16),
            jax.ShapeDtypeStruct((9, hidden), jnp.float32),
            jax.ShapeDtypeStruct((hidden // 16, 16, channels), jnp.bfloat16),
        ),
        in_specs=[
            moving(tokens),
            moving(tokens),
            moving(slope_got.shape[0]),
            fixed(grad_got.shape),
            moving(1),
            moving(1),
            pl.BlockSpec((width, channels), lambda e: (e, 0)),
            moving(tokens),
            moving(tokens),
            moving(channels),
            pl.BlockSpec((3, 3, width), lambda e: (0, 0, e)),
            fixed(tokens_in.shape),
            fixed(grad.shape),
            moving(tokens),
            fixed(grad_b.shape),
        ],
        out_specs=[
            fixed((tokens, channels)),
            fixed((128, 16, width)),
            moving(9),
            pl.BlockSpec((width // 16, 16, channels), lambda e: (e, 0, 0)),
        ],
        scratch_shapes=[
            pltpu.VMEM(slope_got.shape[:1] + (width,), jnp.float32),
            pltpu.VMEM((channels, tokens), jnp.bfloat16),
            pltpu.VMEM((4, SIDE, 128), jnp.float32),
            pltpu.VMEM((ROWS + 2, COLS + 16, width), jnp.float32),
            pltpu.VMEM((3, ROWS + 2, COLS, width), jnp.float32),
            pltpu.VMEM((tokens, width), jnp.bfloat16),
            pltpu.VMEM((tokens, channels), jnp.float32),
            pltpu.VMEM((4, tokens, 128), jnp.float32),
            pltpu.VMEM((4, 2048, 128), jnp.float32),
        ],
        compiler_params=pltpu.CompilerParams(vmem_limit_bytes=60 * 1024 * 1024),
    )(
        scaled_grad, slope_mix, slope_got, grad_got, gate, pooled_grad, w_project, main, slope,
        w_expand, taps, tokens_in, grad, scaled, grad_b
    )


HEAD_DIM = 32
QUAD = 4
PLACES = 64
GROUPS = 8
STAGE = 4


def attention_kernel(
    x_ref,
    wqkv_ref,
    wout_ref,
    bias_ref,
    ret_ref,
    parts_ref,
    table_ref,
    spread,
    qkv,
    cgrad,
    normed_ref,
    proj_ref,
    context_ref,
    cot_ref,
    flat,
    place,
    turned,
):
    channels = wout_ref.shape[0]
    factor = HEAD_DIM ** (-0.5)

    def gather(first_row, out_ref):
        for tile in range(2):
            block = x_ref[:, first_row : first_row + 16, tile * 128 : (tile + 1) * 128]
            spread[tile] = block.astype(jnp.float32).reshape(1024, 128)
        for group in range(GROUPS):
            for piece in range(4):
                half, tile = piece // 2, piece % 2
                rows = spread[tile, pl.ds(half * 8 + group, PLACES, stride=16), :]
                out_ref[group * PLACES : (group + 1) * PLACES, piece * 128 : (piece + 1) * 128] = (
                    rows.astype(jnp.bfloat16)
                )

    gather(0, normed_ref)
    gather(16, cot_ref)

    @pl.loop(0, 3 * channels // 256)
    def _(n):
        cols = pl.ds(pl.multiple_of(n * 256, 256), 256)
        qkv[:, cols] = jnp.dot(
            normed_ref[...], wqkv_ref[:, cols], preferred_element_type=jnp.float32
        ).astype(jnp.bfloat16)

    @pl.loop(0, channels // 256)
    def _(n):
        cols = pl.ds(pl.multiple_of(n * 256, 256), 256)
        cgrad[:, cols] = lax.dot_general(
            cot_ref[...], wout_ref[cols, :], BACKWARD, preferred_element_type=jnp.float32
        ).astype(jnp.bfloat16)

    table_ref[...] = jnp.zeros_like(table_ref)
    lane_head = lax.broadcasted_iota(jnp.int32, (PLACES, 128), 1) // HEAD_DIM
    masks = [(lane_head == h).astype(jnp.float32).astype(jnp.bfloat16) for h in range(QUAD)]
    masks_f = [(lane_head == h).astype(jnp.float32) for h in range(QUAD)]

    def widen(block):
        return jnp.concatenate([block * masks[h] for h in range(QUAD)], axis=0)

    def narrow(full):
        total = full[:PLACES] * masks_f[0]
        for h in range(1, QUAD):
            total = total + full[h * PLACES : (h + 1) * PLACES] * masks_f[h]
        return total

    @pl.loop(0, GROUPS)
    def _(group):
        rows = pl.ds(pl.multiple_of(group * PLACES, PLACES), PLACES)
        for first in range(0, 4, STAGE):
            quads = range(first, first + STAGE)
            lows = [quad * 128 for quad in quads]
            queries = [qkv[rows, low : low + 128] for low in lows]
            keys_in = [qkv[rows, channels + low : channels + low + 128] for low in lows]
            values_in = [qkv[rows, 2 * channels + low : 2 * channels + low + 128] for low in lows]
            grads = [cgrad[rows, low : low + 128] for low in lows]
            queries_wide = [widen(block) for block in queries]
            grads_wide = [widen(block) for block in grads]

            def product(left, right, dims):
                return [
                    lax.dot_general(x, y, dims, preferred_element_type=jnp.float32)
                    for x, y in zip(left, right)
                ]

            plain = (((1,), (0,)), ((), ()))
            scores = product(keys_in, queries_wide, BACKWARD)
            weights_grad = product(values_in, grads_wide, BACKWARD)
            scores = [x * factor + bias_ref[quad] for x, quad in zip(scores, quads)]
            scores = [jnp.exp(x - jnp.max(x, axis=0, keepdims=True)) for x in scores]
            weights = [x * (1.0 / jnp.sum(x, axis=0, keepdims=True)) for x in scores]
            weights_b = [x.astype(jnp.bfloat16) for x in weights]
            context = product(weights_b, values_in, CONTRACT)
            values_grad = product(weights_b, grads_wide, plain)
            scores_grad = [
                x * (y - jnp.sum(x * y, axis=0, keepdims=True))
                for x, y in zip(weights, weights_grad)
            ]
            scores_b = [(x * factor).astype(jnp.bfloat16) for x in scores_grad]
            queries_grad = product(scores_b, keys_in, CONTRACT)
            keys_grad = product(scores_b, queries_wide, plain)
            for k, (quad, low) in enumerate(zip(quads, lows)):
                table_ref[quad] += scores_grad[k]
                context_ref[rows, low : low + 128] = narrow(context[k]).astype(jnp.bfloat16)
                proj_ref[rows, low : low + 128] = narrow(queries_grad[k]).astype(jnp.bfloat16)
                proj_ref[rows, channels + low : channels + low + 128] = keys_grad[k].astype(
                    jnp.bfloat16
                )
                proj_ref[rows, 2 * channels + low : 2 * channels + low + 128] = values_grad[
                    k
                ].astype(jnp.bfloat16)

    def scatter(read, first_row):
        for group in range(GROUPS):
            for piece in range(4):
                half, tile = piece // 2, piece % 2
                spread[tile, pl.ds(half * 8 + group, PLACES, stride=16), :] = read(group, piece)
        for tile in range(2):
            ret_ref[:, first_row : first_row + 16, tile * 128 : (tile + 1) * 128] = (
                spread[tile].reshape(64, 16, 128).astype(jnp.bfloat16)
            )

    def read_context(group, piece):
        return context_ref[
            group * PLACES : (group + 1) * PLACES, piece * 128 : (piece + 1) * 128
        ].astype(jnp.float32)

    scatter(read_context, 0)

    for n in range(channels // 256):
        grads = lax.dot_general(
            proj_ref[...],
            wqkv_ref[n * 256 : (n + 1) * 256, :],
            BACKWARD,
            preferred_element_type=jnp.float32,
        )
        for group in range(GROUPS):
            for tile in range(2):
                spread[tile, pl.ds(n * 8 + group, PLACES, stride=16), :] = grads[
                    group * PLACES : (group + 1) * PLACES, tile * 128 : (tile + 1) * 128
                ]
    for tile in range(2):
        ret_ref[:, 16:32, tile * 128 : (tile + 1) * 128] = (
            spread[tile].reshape(64, 16, 128).astype(jnp.bfloat16)
        )

    turned[...] = normed_ref[...].T
    for q in range(3):
        regroup(
            jnp.dot(
                turned[...],
                proj_ref[:, q * channels : (q + 1) * channels],
                preferred_element_type=jnp.float32,
            ),
            flat,
            place,
            q * 4,
        )
    regroup(
        lax.dot_general(
            context_ref[...], cot_ref[...], CONTRACT, preferred_element_type=jnp.float32
        ),
        flat,
        place,
        12,
    )
    for tile in range(4):
        parts_ref[:, :, tile * 128 : (tile + 1) * 128] = (
            place[tile].reshape(128, 16, 128).astype(jnp.bfloat16)
        )


def attention(blocks, w_qkv, w_out, bias):
    channels = w_out.shape[0]
    tokens = GROUPS * PLACES
    shapes = (
        jax.ShapeDtypeStruct(blocks.shape, jnp.bfloat16),
        jax.ShapeDtypeStruct((128, 16, channels), jnp.bfloat16),
        jax.ShapeDtypeStruct(bias.shape, jnp.float32),
    )
    return pl.pallas_call(
        attention_kernel,
        out_shape=shapes,
        in_specs=[pl.BlockSpec(memory_space=pltpu.VMEM)] * 4,
        out_specs=[pl.BlockSpec(memory_space=pltpu.VMEM)] * 3,
        scratch_shapes=[
            pltpu.VMEM((2, 1024, 128), jnp.float32),
            pltpu.VMEM((tokens, 3 * channels), jnp.bfloat16),
            pltpu.VMEM((tokens, channels), jnp.bfloat16),
            pltpu.VMEM((tokens, channels), jnp.bfloat16),
            pltpu.VMEM((tokens, 3 * channels), jnp.bfloat16),
            pltpu.VMEM((tokens, channels), jnp.bfloat16),
            pltpu.VMEM((tokens, channels), jnp.bfloat16),
            pltpu.VMEM((4, tokens, 128), jnp.float32),
            pltpu.VMEM((4, 2048, 128), jnp.float32),
            pltpu.VMEM((channels, tokens), jnp.bfloat16),
        ],
        compiler_params=pltpu.CompilerParams(vmem_limit_bytes=60 * 1024 * 1024),
    )(blocks, w_qkv, w_out, bias)


def on_device(
    inputs, out_grad, w_expand, dw_kernel, se_reduce, se_expand, w_project, w_qkv, w_out, pos_table
):
    images, tile_rows, tile_cols, channels = inputs.shape
    hidden_units = w_expand.shape[1]
    heads = pos_table.shape[0]
    places = GRID * GRID
    full_rows = tile_rows * lax.axis_size("row")
    full_cols = tile_cols * lax.axis_size("col")
    cells = full_rows * full_cols
    factor = (images * cells) ** (-0.5)
    tokens = images * tile_rows * tile_cols
    onehot = offset_table(GRID)
    bias = (
        jnp.dot(pos_table, onehot, precision=HIGHEST)
        .reshape(heads // QUAD, QUAD, places, places)
        .transpose(0, 2, 1, 3)
        .reshape(heads // QUAD, places, QUAD * places)
    )
    flat_inputs = inputs.reshape(tokens, channels)
    flattened_cotangent = out_grad.reshape(tokens, channels)
    mixed, slope_mix, slope_expand, main, pooled, slope_edges = expand_and_mix(
        flat_inputs, halo(inputs[0], 5), w_expand, dw_kernel
    )
    pooled, slope_got = sum_and_halo(pooled.reshape(-1, 128), slope_edges, 3)
    pooled = pooled.reshape(images, -1) / cells
    squeeze_pre = jnp.dot(pooled, se_reduce, precision=HIGHEST)
    squeeze_sig = jax.nn.sigmoid(squeeze_pre)
    squeezed = squeeze_pre * squeeze_sig
    gate = jax.nn.sigmoid(jnp.dot(squeezed, se_expand, precision=HIGHEST))
    scaled, middle_activation, outgoing = project(
        mixed, gate, flat_inputs, flattened_cotangent, w_project
    )
    returned, attention_parts, scores_sum = attention(swap(outgoing, 1), w_qkv, w_out, bias)
    table_part = lax.dot_general(
        scores_sum.reshape(heads // QUAD, places, QUAD, places)
        .transpose(0, 2, 1, 3)
        .reshape(heads, places * places),
        onehot,
        BACKWARD,
        precision=HIGHEST,
    )
    block_out, middle_gradient, middle_b, scaled_grad, gate_grad, grad_edges = middle_backward(
        swap(returned, 2), middle_activation, flattened_cotangent, mixed, w_out, w_project
    )
    gate_grad, grad_got = sum_and_halo(gate_grad, grad_edges, 4)
    gate_grad = gate_grad.reshape(images, -1)
    excite_grad = gate_grad * gate * (1.0 - gate)
    squeezed_grad = lax.dot_general(excite_grad, se_expand, BACKWARD, precision=HIGHEST)
    squeeze_grad = squeezed_grad * squeeze_sig * (1.0 + squeeze_pre * (1.0 - squeeze_sig))
    pooled_grad = lax.dot_general(squeeze_grad, se_reduce, BACKWARD, precision=HIGHEST)
    se_reduce_grad = lax.dot_general(pooled, squeeze_grad, CONTRACT, precision=HIGHEST) * factor
    se_expand_grad = lax.dot_general(squeezed, excite_grad, CONTRACT, precision=HIGHEST) * factor
    input_gradient, expand_parts, kernel_part, project_parts = mix_backward(
        scaled_grad,
        slope_mix,
        slope_got,
        grad_got,
        gate,
        pooled_grad / cells,
        w_project,
        main,
        slope_expand,
        w_expand,
        dw_kernel,
        flat_inputs,
        middle_gradient,
        scaled,
        middle_b,
    )
    small = jnp.concatenate([kernel_part.reshape(-1), table_part.reshape(-1)])
    unit = lax.axis_size("row") * 1024
    room = -small.shape[0] % unit
    small = jnp.pad(small, (0, room)).reshape(lax.axis_size("row"), -1, 128)
    project_grad, expand_grad, qkv_grad, out_proj_grad, small = reduce_all(
        (project_parts, expand_parts, attention_parts), small, factor, 7
    )
    small = small.reshape(-1)
    kernel_size = kernel_part.size
    kernel_sum = small[:kernel_size].reshape(dw_kernel.shape)
    table_sum = small[kernel_size : kernel_size + table_part.size].reshape(table_part.shape)
    return (
        block_out.reshape(images, tile_rows, tile_cols, channels),
        input_gradient.reshape(images, tile_rows, tile_cols, channels),
        expand_grad,
        project_grad,
        qkv_grad,
        out_proj_grad,
        kernel_sum * factor,
        se_reduce_grad,
        se_expand_grad,
        table_sum * factor,
    )


def solution(mesh):
    placed = (
        P(None, "row", "col", None),
        P(None, "row", "col", None),
        P(),
        P(),
        P(),
        P(),
        P(),
        P(),
        P(),
        P(),
    )
    return jax.shard_map(
        on_device,
        mesh=mesh,
        in_specs=placed,
        out_specs=(
            P(None, "row", "col", None),
            P(None, "row", "col", None),
            P(("row", "col"), None),
            P(("row", "col"), None),
            P(("row", "col"), None),
            P(("row", "col"), None),
            P(),
            P(),
            P(),
            P(),
        ),
        check_vma=False,
    )
```
